512 devices in a mesh: view: 64 (over z_lo, x, core), row: 8 (over z_hi, y).
Axes of the slice: x: 4, y: 4, z: 16 (z_hi: 2, z_lo: 8; z = z_hi * 8 + z_lo), core: 2. Of those that a mesh axis runs over, the one named last changes fastest.
Arguments:
- layers: bfloat16 [3, 3, 384, 1024], P(None, None, 'row'), may hold values from 0.19921875 to 1
- target: bfloat16 [64, 384, 1024], P('view', 'row'), may hold values from 0.049804688 to 0.5
- shifts: int32 [64, 3, 2], P('view'), may hold values from -8 to 8, as said below
Outputs:
- updated: float32 [3, 3, 384, 1024], P(None, None, 'row')
The draws below stay inside these ranges and needn't reach their ends.
Inputs may be any that keep to these rules, and one draw needn't show every extreme that they name: `shifts`: for every layer and each of the two components, one view has shift 8 and another view has shift -8.
All inputs are finite; a program needn't handle non-finite values.
Results may differ from the reference program's by a relative error of at most 0.0003.
Values may be sent and summed in bfloat16 or wider, within the bound.
No kernel may reach another device: no remote copies, remote signals or barrier semaphores. Data moves between devices by JAX's collectives and lax.ppermute only.
A program may use at most 64 MiB of HBM per device.

```python
import jax
import jax.numpy as jnp
from jax import lax

COLS = 1024
LAYERS = 3
FRAMES = 3
HALO = 8
VIEWS = 64
ROWS = 384


def draw_shifts(key, part):
    key = jax.random.fold_in(key, 7)
    key_base, key_high, key_step = jax.random.split(key, 3)
    base = jax.random.randint(key_base, (VIEWS, LAYERS, 2), -HALO, HALO + 1)
    high = jax.random.randint(key_high, (LAYERS, 2), 0, VIEWS)
    step = jax.random.randint(key_step, (LAYERS, 2), 1, VIEWS)
    low = (high + step) % VIEWS
    view_ids = jnp.arange(VIEWS)[:, None, None]
    base = jnp.where(view_ids == high[None], HALO, base)
    base = jnp.where(view_ids == low[None], -HALO, base)
    return base.astype(jnp.int32)


def steps_of(key, extent, cuts, least, top_value):
    def one(axis_at, blocks):
        draws = jax.random.uniform(jax.random.fold_in(jax.random.fold_in(key, 6), axis_at), (blocks,), jnp.float32, least / len(cuts), top_value / len(cuts))
        return jnp.repeat(jnp.exp(draws), extent[axis_at] // blocks).reshape((-1,) + (1,) * (len(extent) - axis_at - 1))

    factor_of = one(*cuts[0])
    for cut in cuts[1:]:
        factor_of = factor_of * one(*cut)
    return factor_of


def setup_inputs(seed: int = 0) -> dict:
    key_list = jax.random.split(jax.random.key(seed), 4)
    layers = jnp.clip(0.19921875 + 0.80078125 * jax.random.uniform(key_list[0], (FRAMES, LAYERS, ROWS, COLS), jnp.float32) ** steps_of(key_list[0], (FRAMES, LAYERS, ROWS, COLS), ((2, 8),), -0.2, 0.2), 0.19921875, 1.0).astype(jnp.bfloat16)
    target = jnp.clip(0.049804688 + 0.4501953 * jax.random.uniform(key_list[1], (VIEWS, ROWS, COLS), jnp.float32) ** steps_of(key_list[1], (VIEWS, ROWS, COLS), ((0, 64), (1, 8)), -0.2, 0.2), 0.049804688, 0.5).astype(jnp.bfloat16)
    shifts = draw_shifts(jax.random.fold_in(key_list[3], 71), 0)
    return dict(layers=layers, target=target, shifts=shifts)


regular = 0.05


def project_view(padded, shift_pair, frame_count, row_count, col_count):
    pieces = []
    for layer in range(LAYERS):
        start_row = (HALO + shift_pair[layer, 0]).astype(jnp.int32)
        start_col = (HALO + shift_pair[layer, 1]).astype(jnp.int32)
        zero = jnp.zeros((), jnp.int32)
        piece = lax.dynamic_slice(padded[:, layer], (zero, start_row, start_col), (frame_count, row_count, col_count))
        pieces.append(piece.astype(jnp.float32))
    return pieces


def product_except(pieces, skip):
    result = None
    for layer in range(len(pieces)):
        if layer != skip:
            result = pieces[layer] if result is None else result * pieces[layer]
    return result


def reference(layers, target, shifts):
    frame_count, layer_count, row_count, col_count = layers.shape
    padded = jnp.pad(layers, ((0, 0), (0, 0), (HALO, HALO), (HALO, HALO)))

    def one_view(carry, inputs):
        upper, lower = carry
        image, shift_pair = inputs
        pieces = project_view(padded, shift_pair, frame_count, row_count, col_count)
        whole_product = pieces[0]
        for layer in range(1, layer_count):
            whole_product = whole_product * pieces[layer]
        shown = jnp.sum(whole_product, axis=0) / frame_count
        image_f = image.astype(jnp.float32)
        uppers = []
        lowers = []
        for layer in range(layer_count):
            others = product_except(pieces, layer)
            terms = jnp.stack([image_f[None] * others, shown[None] * others])
            terms = jnp.pad(terms, ((0, 0), (0, 0), (HALO, HALO), (HALO, HALO)))
            start_row = (HALO - shift_pair[layer, 0]).astype(jnp.int32)
            start_col = (HALO - shift_pair[layer, 1]).astype(jnp.int32)
            zero = jnp.zeros((), jnp.int32)
            back = lax.dynamic_slice(terms, (zero, zero, start_row, start_col), (2, frame_count, row_count, col_count))
            uppers.append(back[0])
            lowers.append(back[1])
        upper = upper + jnp.stack(uppers, axis=1)
        lower = lower + jnp.stack(lowers, axis=1)
        return (upper, lower), None

    start = jnp.zeros(layers.shape, jnp.float32)
    (upper, lower), _ = lax.scan(one_view, (start, start), (target, shifts))
    return layers.astype(jnp.float32) * (upper + regular) / (lower + regular)
```

```python
import jax
import jax.numpy as jnp
from jax import lax
from jax.experimental import pallas as pl
from jax.experimental.pallas import tpu as pltpu
from jax.sharding import Mesh, PartitionSpec as P

HALO = 8
SPAN = 2 * HALO + 1
TILE = 16
SEG = 32
REGULAR = 0.05
CODE_STEPS = 5041.0
CODE_BASE = 7.0
F32 = jnp.float32
BF16 = jnp.bfloat16
VIEW = ("zl", "x", "c")
ROW = ("zh", "y")
PARAMS = pltpu.CompilerParams(vmem_limit_bytes=48 * 1024 * 1024)


def lanes(rows):
    return lax.broadcasted_iota(jnp.int32, (rows, 128), 1)


def my_tile():
    high = lax.axis_index("zh")
    along = lax.rem(lax.axis_index("zl") + 4 * high, 8)
    return along, lax.axis_index("x") * 2 + lax.axis_index("c")


def pack_kernel(layers_ref, target_ref, shifts_ref, chunks_ref, own_ref, head_ref, tail_ref):
    high = lax.axis_index("zh")
    lane = lanes(16)
    extra = jnp.zeros((16, 128), F32)
    for layer in range(3):
        for part in range(2):
            extra = jnp.where(
                lane == 96 + 2 * layer + part, shifts_ref[0, layer, part].astype(F32), extra
            )
    zero = jnp.zeros((16, 128), F32)
    for group in range(8):
        sources = []
        for b in range(3):
            rows = slice(16 * b, 16 * b + 16)
            mid = target_ref[0, rows, 128 * group : 128 * group + 128].astype(F32)
            left = zero
            right = zero
            if group > 0:
                left = target_ref[0, rows, 128 * group - 128 : 128 * group].astype(F32)
            if group < 7:
                right = target_ref[0, rows, 128 * group + 128 : 128 * group + 256].astype(F32)
            sources.append(
                (jnp.where(lane >= 128 - HALO, left, mid), mid, jnp.where(lane < HALO, right, mid))
            )
        for t8 in range(8):
            which = 0 if t8 == 0 else (2 if t8 == 7 else 1)
            chunk = extra
            for b in range(3):
                amount = (SEG * b - (TILE * t8 - HALO)) % 128
                moved = pltpu.roll(sources[b][which], amount, 1) if amount else sources[b][which]
                chunk = jnp.where((lane >= SEG * b) & (lane < SEG * b + SEG), moved, chunk)
            place = lax.rem(group + 4 * high, 8) * 8 + t8
            chunks_ref[place] = chunk.astype(BF16)

    along, t8 = my_tile()
    first = along * 128 + t8 * TILE - 2 * HALO
    window = jnp.clip(jnp.where(first < 0, 0, first // 128), 0, 6)
    start = pl.multiple_of(window * 128, 128)
    row = lax.broadcasted_iota(jnp.int32, (256, 256), 0)
    col = lax.broadcasted_iota(jnp.int32, (256, 256), 1)
    wanted = first - start + (col & (SEG - 1)) + TILE * (col // 128)
    segment = (col & 127) // SEG
    total = None
    for frame in range(3):
        pick = jnp.where((row == wanted) & (segment == frame), 1.0, 0.0).astype(BF16)
        part = layers_ref[frame, :, :, pl.ds(start, 256)].reshape(3 * 48, 256)
        moved = jnp.dot(part, pick, preferred_element_type=F32)
        total = moved if total is None else total + moved
    for layer in range(3):
        for side in range(2):
            cells = total[48 * layer : 48 * layer + 48, 128 * side : 128 * side + 128]
            own_ref[2 * layer + side] = cells
            head_ref[2 * layer + side] = cells[:HALO]
            tail_ref[2 * layer + side] = cells[48 - HALO :]


def view_kernel(
    recv_ref, own_ref, above_ref, below_ref, own_out, up_out, down_out,
    seen_ref, image_ref, shift_ref, shift_smem, sem, *sums,
):
    shift_ref[...] = recv_ref[:, 0, :].astype(F32).astype(jnp.int32)
    copy = pltpu.make_async_copy(shift_ref, shift_smem, sem)
    copy.start()

    lane = lanes(64)
    within = lane & (SEG - 1)
    for layer in range(3):
        low, high = (
            jnp.concatenate(
                [above_ref[2 * layer + s], own_ref[2 * layer + s], below_ref[2 * layer + s]], axis=0
            )
            for s in range(2)
        )
        for d in range(SPAN):
            a = pltpu.roll(low, (128 - d) % 128, 1) if d else low
            b = pltpu.roll(high, 16 - d, 1) if d < 16 else high
            seen_ref[layer, d] = jnp.where(within < SEG - d, a, b)

    row = lax.broadcasted_iota(jnp.int32, (128, 384), 0)
    col = lax.broadcasted_iota(jnp.int32, (128, 384), 1)
    pick = (row == (col // 128) * SEG + (col & (SEG - 1))) & ((col & 127) < 3 * SEG)
    pick = jnp.where(pick, 1.0, 0.0).astype(BF16)
    for part in range(8):
        block = recv_ref[8 * part : 8 * part + 8].reshape(128, 128)
        spread = jnp.dot(block, pick, preferred_element_type=F32)
        for b in range(3):
            image_ref[8 * part : 8 * part + 8, 16 * b : 16 * b + 16, :] = spread[
                :, 128 * b : 128 * b + 128
            ].reshape(8, 16, 128)

    for ref in sums:
        ref[...] = jnp.zeros_like(ref)

    along, t8 = my_tile()
    column = along * 128 + t8 * TILE - HALO + (lanes(8) & (SEG - 1))
    third = jnp.where((column >= 0) & (column < 1024), 1.0 / 3.0, 0.0)[0:1]
    copy.wait()

    def one_view(view, carry):
        rows = [shift_smem[view, 96 + 2 * layer] + HALO for layer in range(3)]
        cols = [shift_smem[view, 97 + 2 * layer] + HALO for layer in range(3)]
        s0, s1, s2 = (
            seen_ref[layer, cols[layer], pl.ds(rows[layer], 48), :] for layer in range(3)
        )
        p01 = s0 * s1
        whole = p01 * s2
        pair = whole + pltpu.roll(whole, 64, 1)
        shown = (pair + pltpu.roll(pair, 32, 1)) * third
        image = image_ref[view]
        for layer, others in enumerate((s1 * s2, s0 * s2, p01)):
            for which, factor in enumerate((image, shown)):
                sums[2 * layer + which][cols[layer], pl.ds(rows[layer], 48), :] += factor * others
        return carry

    lax.fori_loop(0, 64, one_view, 0)

    for at in range(6):
        total = None
        for d in range(SPAN):
            cells = sums[at][d]
            moved = pltpu.roll(cells, (d - HALO) % 128, 1) if d != HALO else cells
            total = moved if total is None else total + moved
        up_out[at] = total[:HALO]
        own_out[at] = total[HALO : HALO + 48]
        down_out[at] = total[HALO + 48 :]


def update_kernel(own_ref, above_ref, below_ref, layer_ref, out_ref):
    lane = lanes(48)
    within = lane & (SEG - 1)
    codes = []
    for layer in range(3):
        low = pltpu.roll(layer_ref[2 * layer], 128 - HALO, 1)
        high = pltpu.roll(layer_ref[2 * layer + 1], HALO, 1)
        cells = jnp.where(within < SEG - HALO, low, high)
        sides = []
        for which in range(2):
            at = 2 * layer + which
            own = own_ref[at]
            sides.append(
                jnp.concatenate(
                    [own[:HALO] + above_ref[at], own[HALO:40], own[40:] + below_ref[at]], axis=0
                )
            )
        value = cells * (sides[0] + REGULAR) / (sides[1] + REGULAR)
        scaled = (jnp.log2(value) + CODE_BASE) * CODE_STEPS + 0.5
        codes.append(jnp.clip(scaled, 0.0, 65535.0).astype(jnp.int32))
    lane = lanes(8)
    blocks = [jnp.zeros((8, 128), jnp.int32) for _ in range(8)]
    for group in range(54):
        frame, layer, g = group // 18, (group // 6) % 3, group % 6
        cells = codes[layer][8 * g : 8 * g + 8]
        amount = (TILE * (group % 8) - (SEG * frame + HALO)) % 128
        moved = pltpu.roll(cells, amount, 1) if amount else cells
        blocks[group // 8] = jnp.where(lane // TILE == group % 8, moved, blocks[group // 8])
    _, t8 = my_tile()
    for j in range(4):
        word = blocks[j] + (blocks[j + 4] - 32768) * 65536
        word = pltpu.roll(word, TILE * t8, 1)
        for copy in range(8):
            out_ref[copy, 8 * j : 8 * j + 8] = word


def spread_kernel(words_ref, out_ref):
    high = lax.axis_index("zh")
    lane = lanes(8) // TILE

    def one(at, carry):
        place = pl.multiple_of(lax.rem(at + 4 * high, 8) * 128, 128)
        for j in range(4):
            words = [words_ref[t8, at, 8 * j : 8 * j + 8] for t8 in range(8)]
            for i in range(8):
                merged = words[0]
                for t8 in range(1, 8):
                    merged = jnp.where(lane == (i + t8) % 8, words[t8], merged)
                if i:
                    merged = pltpu.roll(merged, 128 - TILE * i, 1)
                for group, code in ((8 * j + i, merged & 65535), (8 * j + i + 32, (merged >> 16) + 32768)):
                    if group < 54:
                        value = jnp.exp2(code.astype(F32) * (1.0 / CODE_STEPS) - CODE_BASE)
                        frame, layer, g = group // 18, (group // 6) % 3, group % 6
                        out_ref[frame, layer, 8 * g : 8 * g + 8, pl.ds(place, 128)] = value
        return carry

    lax.fori_loop(0, 8, one, 0)


def row_pairs(step):
    pairs = []
    for zl in range(8):
        for zh in range(2):
            for y in range(4):
                at = zh * 4 + y + step
                if 0 <= at < 8:
                    other = (zl + 4 * (zh != at // 4)) % 8
                    pairs.append(((zl * 2 + zh) * 4 + y, (other * 2 + at // 4) * 4 + at % 4))
    return pairs


def body(layers, target, shifts):
    vmem = pl.BlockSpec(memory_space=pltpu.VMEM)
    smem = pl.BlockSpec(memory_space=pltpu.SMEM)
    shape = jax.ShapeDtypeStruct
    across = ("zl", "zh", "y")

    chunks, own, head, tail = pl.pallas_call(
        pack_kernel,
        out_shape=(
            shape((64, 16, 128), BF16),
            shape((6, 48, 128), F32),
            shape((6, HALO, 128), F32),
            shape((6, HALO, 128), F32),
        ),
        in_specs=[vmem, vmem, smem],
        out_specs=(vmem,) * 4,
        compiler_params=PARAMS,
    )(layers, target, shifts)
    above = lax.ppermute(tail, across, row_pairs(1))
    below = lax.ppermute(head, across, row_pairs(-1))
    received = lax.all_to_all(chunks, VIEW, 0, 0)

    sums, up, down = pl.pallas_call(
        view_kernel,
        out_shape=(
            shape((6, 48, 128), F32),
            shape((6, HALO, 128), F32),
            shape((6, HALO, 128), F32),
        ),
        in_specs=[vmem] * 4,
        out_specs=(vmem,) * 3,
        scratch_shapes=[
            pltpu.VMEM((3, SPAN, 64, 128), F32),
            pltpu.VMEM((64, 48, 128), F32),
            pltpu.VMEM((64, 128), jnp.int32),
            pltpu.SMEM((64, 128), jnp.int32),
            pltpu.SemaphoreType.DMA,
        ]
        + [pltpu.VMEM((SPAN, 64, 128), F32)] * 6,
        compiler_params=PARAMS,
    )(received, own, above, below)
    from_above = lax.ppermute(down, across, row_pairs(1))
    from_below = lax.ppermute(up, across, row_pairs(-1))

    words = pl.pallas_call(
        update_kernel,
        out_shape=shape((8, 32, 128), jnp.int32),
        in_specs=[vmem] * 4,
        out_specs=vmem,
        compiler_params=PARAMS,
    )(sums, from_above, from_below, own)
    words = lax.all_to_all(words, "zl", 0, 0)
    words = lax.all_gather(words, ("x", "c"))

    return pl.pallas_call(
        spread_kernel,
        out_shape=shape((3, 3, 48, 1024), F32),
        in_specs=[vmem],
        out_specs=vmem,
        compiler_params=PARAMS,
    )(words)


def solution(mesh):
    fine = Mesh(mesh.devices.reshape(8, 4, 2, 2, 4), ("zl", "x", "c", "zh", "y"))
    placed = (P(None, None, ROW, None), P(VIEW, ROW, None), P(VIEW, None, None))
    return jax.shard_map(
        body, mesh=fine, in_specs=placed, out_specs=P(None, None, ROW, None), check_vma=False
    )
```

```python
import jax
import jax.numpy as jnp
from jax import lax
from jax.experimental import pallas as pl
from jax.experimental.pallas import tpu as pltpu
from jax.sharding import Mesh, PartitionSpec as P

HALO = 8
SPAN = 2 * HALO + 1
TALL = 12
WIDE = 64
REGULAR = 0.05
CODE_STEPS = 5041.0
CODE_BASE = 7.0
WORDS = 30
F32 = jnp.float32
BF16 = jnp.bfloat16
I32 = jnp.int32
VIEW = ("zl", "x", "c")
ROW = ("zh", "y")
PARAMS = pltpu.CompilerParams(vmem_limit_bytes=48 * 1024 * 1024)


def lanes(rows):
    return lax.broadcasted_iota(I32, (rows, 128), 1)


def mirrored(q):
    return jnp.where(lax.rem(lax.axis_index("y"), 2) == 0, q, 3 - q)


def my_block():
    return lax.rem(lax.axis_index("zl") + 4 * lax.axis_index("zh"), 8)


def pack_kernel(target_ref, shifts_ref, chunks_ref, wide_ref):
    high = lax.axis_index("zh")
    lane = lanes(48)
    blocks = [target_ref[0, :, 128 * d : 128 * d + 128].astype(F32) for d in range(8)]
    zero = jnp.zeros((48, 128), F32)
    for d in range(8):
        left = blocks[d - 1] if d > 0 else zero
        right = blocks[d + 1] if d < 7 else zero
        mid = blocks[d]
        wide_ref[2 * d, :48] = pltpu.roll(jnp.where(lane >= 128 - HALO, left, mid), HALO, 1)
        wide_ref[2 * d + 1, :48] = pltpu.roll(jnp.where(lane < HALO, right, mid), 128 - 56, 1)
    lane = lanes(8)
    upper_half = lax.broadcasted_iota(I32, (8, 128), 0) < 4
    extra = jnp.zeros((8, 128), F32)
    for layer in range(3):
        for part in range(2):
            extra = jnp.where(
                lane == 120 + 2 * layer + part, shifts_ref[0, part, layer].astype(F32), extra
            )
    for q in range(4):
        x = mirrored(q)
        for d in range(8):
            zl = lax.rem(d + 4 * high, 8)
            for h in range(2):
                at = 2 * d + h
                main = wide_ref[at, TALL * q : TALL * q + 8]
                first = wide_ref[at, TALL * q + 8 : TALL * q + 16]
                second = wide_ref[at, TALL * q + 4 : TALL * q + 12]
                pieces = jnp.where(upper_half, pltpu.roll(first, 80, 1), pltpu.roll(second, 40, 1))
                chunk = jnp.where(lane < 80, main, jnp.where(lane < 120, pieces, extra))
                chunks_ref[(zl * 4 + x) * 2 + h] = chunk.astype(BF16)


def strip_kernel(layers_ref, own_ref, head_ref, tail_ref):
    half = lax.axis_index("c")
    block = my_block() - 1 + half
    amount = jnp.where(half == 0, 16, 80)
    left = pl.multiple_of(jnp.maximum(block, 0) * 128, 128)
    right = pl.multiple_of(jnp.minimum(block + 1, 7) * 128, 128)
    left_there = jnp.where(block >= 0, 1.0, 0.0)
    right_there = jnp.where(block + 1 <= 7, 1.0, 0.0)
    lane = lanes(48)
    for layer in range(3):
        for frame in range(3):
            a = layers_ref[frame, layer, :, pl.ds(left, 128)].astype(F32) * left_there
            b = layers_ref[frame, layer, :, pl.ds(right, 128)].astype(F32) * right_there
            cells = pltpu.roll(jnp.where(lane >= 128 - amount, a, b), amount, 1)
            own_ref[layer, frame] = cells
            head_ref[layer, frame] = cells[:HALO]
            tail_ref[layer, frame] = cells[48 - HALO :]


def seen_kernel(own_ref, above_ref, below_ref, seen_ref, tile_ref, tall_ref):
    q = mirrored(lax.axis_index("x"))
    start = q * TALL
    tall_ref[:, :, :HALO] = above_ref[...]
    tall_ref[:, :, HALO : HALO + 48] = own_ref[...]
    tall_ref[:, :, HALO + 48 : 64] = below_ref[...]
    tall_ref[:, :, 64:] = jnp.zeros((3, 3, 8, 128), F32)
    for layer in range(3):
        for frame in range(3):
            cells = tall_ref[layer, frame, pl.ds(start, 32), :]
            for d in range(SPAN):
                moved = pltpu.roll(cells, 128 - d, 1) if d else cells
                seen_ref[layer, d, frame] = moved
                if d == 16:
                    tile_ref[layer, frame] = moved[HALO : HALO + 16]


def view_kernel(
    recv_ref, seen_ref, own_out, up_out, down_out, image_ref, shift_ref, shift_smem, sem, *sums
):
    shift_ref[...] = recv_ref[:, 0, :].astype(F32).astype(I32)
    copy = pltpu.make_async_copy(shift_ref, shift_smem, sem)
    copy.start()

    lane = lanes(8)
    upper_half = lax.broadcasted_iota(I32, (8, 128), 0) < 4
    for view in range(64):
        cells = recv_ref[view].astype(F32)
        image_ref[view, :8] = cells
        low = pltpu.roll(cells, 128 - 80, 1)
        high = pltpu.roll(pltpu.roll(cells, 128 - 40, 1), 4, 0)
        rest = jnp.where(lane < 40, low, high)
        image_ref[view, 8:] = jnp.where(upper_half, rest, 0.0)

    for ref in sums:
        ref[...] = jnp.zeros_like(ref)

    column = my_block() * 128 + lax.axis_index("c") * WIDE - HALO + lanes(16)
    inside = (column >= 0) & (column < 1024)
    inside = inside & (lax.broadcasted_iota(I32, (16, 128), 0) < TALL)
    third = jnp.where(inside, 1.0 / 3.0, 0.0)
    copy.wait()

    def one_view(view, carry):
        rows = [shift_smem[view, 120 + 2 * layer] + HALO for layer in range(3)]
        cols = [shift_smem[view, 121 + 2 * layer] + HALO for layer in range(3)]
        s0, s1, s2 = (
            seen_ref[layer, cols[layer], :, pl.ds(rows[layer], 16), :] for layer in range(3)
        )
        p01 = s0 * s1
        whole = p01 * s2
        shown = (whole[0] + whole[1] + whole[2]) * third
        image = image_ref[view]
        for layer, others in enumerate((s1 * s2, s0 * s2, p01)):
            for which, factor in enumerate((image, shown)):
                sums[2 * layer + which][cols[layer], :, pl.ds(rows[layer], 16), :] += factor * others
        return carry

    lax.fori_loop(0, 64, one_view, 0)

    lane = lanes(32)
    for layer in range(3):
        for frame in range(3):
            sides = []
            for which, base in enumerate((-16, 48)):
                total = None
                for d in range(SPAN):
                    amount = (d + base) % 128
                    cells = sums[2 * layer + which][d, frame]
                    moved = pltpu.roll(cells, amount, 1) if amount else cells
                    total = moved if total is None else total + moved
                sides.append(total)
            both = jnp.where(lane < WIDE, sides[0], sides[1])
            up_out[layer, frame] = both[:HALO]
            own_out[layer, frame] = both[HALO : HALO + 16]
            down_out[layer, frame] = both[HALO + TALL : 2 * HALO + TALL]


def update_kernel(own_ref, above_ref, below_ref, tile_ref, out_ref, code_ref):
    lane = lanes(TALL)
    for layer in range(3):
        for frame in range(3):
            own = own_ref[layer, frame]
            above = above_ref[layer, frame]
            below = below_ref[layer, frame]
            none = jnp.zeros((4, 128), F32)
            both = own[:TALL] + jnp.concatenate([above, none], axis=0)
            both = both + jnp.concatenate([none, below], axis=0)
            lower = pltpu.roll(both, WIDE, 1)
            value = tile_ref[layer, frame, :TALL] * (both + REGULAR) / (lower + REGULAR)
            scaled = (jnp.log2(value) + CODE_BASE) * CODE_STEPS + 0.5
            code_ref[frame * 3 + layer, :TALL] = jnp.clip(scaled, 0.0, 65535.0).astype(I32)
    for pair in range(2):
        parts = []
        for p in (pair, pair + 2):
            even = code_ref[2 * p, :TALL]
            odd = pltpu.roll(code_ref[2 * p + 1, :TALL], WIDE, 1)
            parts.append(jnp.where(lane < WIDE, even, odd))
        word = parts[0] + (parts[1] - 32768) * 65536
        for copy in range(8):
            out_ref[copy, TALL * pair : TALL * pair + TALL] = word
    word = code_ref[8, :6] + (code_ref[8, 6:12] - 32768) * 65536
    for copy in range(8):
        out_ref[copy, 24:30] = word
        out_ref[copy, 30:] = jnp.zeros((2, 128), I32)


def dense_kernel(words_ref, out_ref):
    for zl in range(8):
        out_ref[WORDS * zl : WORDS * zl + WORDS] = words_ref[zl, :WORDS]


def decoded(code):
    return jnp.exp2(code.astype(F32) * (1.0 / CODE_STEPS) - CODE_BASE)


def spread_kernel(words_ref, out_ref):
    zl = lax.rem(pl.program_id(0) + 4 * lax.axis_index("zh"), 8)
    for q in range(4):
        x = mirrored(q)
        rows = slice(TALL * q, TALL * q + TALL)

        def words(c, first, count):
            return words_ref[x * 2 + c, pl.ds(zl * WORDS + first, count), :]

        lane = lanes(TALL)
        for pair in range(2):
            a, b = words(0, TALL * pair, TALL), words(1, TALL * pair, TALL)
            even = jnp.where(lane < WIDE, a, pltpu.roll(b, WIDE, 1))
            odd = jnp.where(lane < WIDE, pltpu.roll(a, WIDE, 1), b)
            for side, word in enumerate((even, odd)):
                for p, code in ((pair, word & 65535), (pair + 2, (word >> 16) + 32768)):
                    at = 2 * p + side
                    out_ref[at // 3, at % 3, rows] = decoded(code)
        a, b = words(0, 24, 6), words(1, 24, 6)
        word = jnp.where(lanes(6) < WIDE, a, pltpu.roll(b, WIDE, 1))
        out_ref[2, 2, TALL * q : TALL * q + 6] = decoded(word & 65535)
        out_ref[2, 2, TALL * q + 6 : TALL * q + TALL] = decoded((word >> 16) + 32768)


def row_pairs(step):
    pairs = []
    for zl in range(8):
        for at in range(8):
            to = at + step
            if 0 <= to < 8:
                other = (zl + 4 * (at // 4 != to // 4)) % 8
                pairs.append(((zl * 2 + at // 4) * 4 + at % 4, (other * 2 + to // 4) * 4 + to % 4))
    return pairs


def strip_pairs(step):
    def index(block, strip):
        at, q = strip // 4, strip % 4
        x = q if at % 2 == 0 else 3 - q
        zl = (block + 4 * (at // 4)) % 8
        return ((zl * 4 + x) * 2 + at // 4) * 4 + at % 4

    return [
        (index(block, strip), index(block, strip + step))
        for block in range(8)
        for strip in range(32)
        if 0 <= strip + step < 32
    ]


VMEM = pl.BlockSpec(memory_space=pltpu.VMEM)
SMEM = pl.BlockSpec(memory_space=pltpu.SMEM)


def call(kernel, outs, ins, scratch=(), **more):
    return pl.pallas_call(
        kernel,
        out_shape=tuple(jax.ShapeDtypeStruct(*out) for out in outs),
        in_specs=ins,
        out_specs=(VMEM,) * len(outs),
        scratch_shapes=scratch,
        compiler_params=PARAMS,
        **more,
    )


def body(layers, target, shifts):
    (chunks,) = call(
        pack_kernel,
        [((64, 8, 128), BF16)],
        [VMEM, SMEM],
        [pltpu.VMEM((16, 56, 128), F32)],
    )(target, shifts.transpose(0, 2, 1))
    received = lax.all_to_all(chunks, VIEW, 0, 0)

    own, head, tail = call(
        strip_kernel,
        [((3, 3, 48, 128), F32), ((3, 3, HALO, 128), F32), ((3, 3, HALO, 128), F32)],
        [VMEM],
    )(layers)
    across = ("zl", "zh", "y")
    above = lax.ppermute(tail, across, row_pairs(1))
    below = lax.ppermute(head, across, row_pairs(-1))
    seen, tile = call(
        seen_kernel,
        [((3, SPAN, 3, 32, 128), F32), ((3, 3, 16, 128), F32)],
        [VMEM] * 3,
        [pltpu.VMEM((3, 3, 72, 128), F32)],
    )(own, above, below)

    sums, up, down = call(
        view_kernel,
        [((3, 3, 16, 128), F32), ((3, 3, HALO, 128), F32), ((3, 3, HALO, 128), F32)],
        [VMEM] * 2,
        [
            pltpu.VMEM((64, 16, 128), F32),
            pltpu.VMEM((64, 128), I32),
            pltpu.SMEM((64, 128), I32),
            pltpu.SemaphoreType.DMA,
        ]
        + [pltpu.VMEM((SPAN, 3, 32, 128), F32)] * 6,
    )(received, seen)
    across = ("zl", "x", "zh", "y")
    from_above = lax.ppermute(down, across, strip_pairs(1))
    from_below = lax.ppermute(up, across, strip_pairs(-1))

    (words,) = call(
        update_kernel,
        [((8, 32, 128), I32)],
        [VMEM] * 4,
        [pltpu.VMEM((9, 16, 128), I32)],
    )(sums, from_above, from_below, tile)
    words = lax.all_to_all(words, "zl", 0, 0)
    (words,) = call(dense_kernel, [((8 * WORDS, 128), I32)], [VMEM])(words)
    words = lax.all_gather(words, ("x", "c"))

    return pl.pallas_call(
        spread_kernel,
        grid=(8,),
        out_shape=jax.ShapeDtypeStruct((3, 3, 48, 1024), F32),
        in_specs=[pl.BlockSpec((8, 8 * WORDS, 128), lambda d: (0, 0, 0))],
        out_specs=pl.BlockSpec((3, 3, 48, 128), lambda d: (0, 0, 0, d)),
        compiler_params=PARAMS,
    )(words)


def solution(mesh):
    fine = Mesh(mesh.devices.reshape(8, 4, 2, 2, 4), ("zl", "x", "c", "zh", "y"))
    placed = (P(None, None, ROW, None), P(VIEW, ROW, None), P(VIEW, None, None))
    return jax.shard_map(
        body, mesh=fine, in_specs=placed, out_specs=P(None, None, ROW, None), check_vma=False
    )
```

```python
import jax
import jax.numpy as jnp
from jax import lax
from jax.experimental import pallas as pl
from jax.experimental.pallas import tpu as pltpu
from jax.sharding import Mesh, PartitionSpec as P

HALO = 8
SPAN = 2 * HALO + 1
TALL = 12
WIDE = 64
REGULAR = 0.05
CODE_STEPS = 5041.0
CODE_BASE = 7.0
WORDS = 30
F32 = jnp.float32
BF16 = jnp.bfloat16
I32 = jnp.int32
VIEW = ("zl", "x", "c")
ROW = ("zh", "y")
PARAMS = pltpu.CompilerParams(vmem_limit_bytes=48 * 1024 * 1024)


def lanes(rows):
    return lax.broadcasted_iota(I32, (rows, 128), 1)


def mirrored(q):
    return jnp.where(lax.rem(lax.axis_index("y"), 2) == 0, q, 3 - q)


def my_block():
    return lax.rem(lax.axis_index("zl") + 4 * lax.axis_index("zh"), 8)


def pack_kernel(target_ref, shifts_ref, chunks_ref, wide_ref):
    high = lax.axis_index("zh")
    lane = lanes(48)
    blocks = [target_ref[0, :, 128 * d : 128 * d + 128].astype(F32) for d in range(8)]
    zero = jnp.zeros((48, 128), F32)
    for d in range(8):
        left = blocks[d - 1] if d > 0 else zero
        right = blocks[d + 1] if d < 7 else zero
        mid = blocks[d]
        wide_ref[2 * d, :48] = pltpu.roll(jnp.where(lane >= 128 - HALO, left, mid), HALO, 1)
        wide_ref[2 * d + 1, :48] = pltpu.roll(jnp.where(lane < HALO, right, mid), 128 - 56, 1)
    lane = lanes(8)
    upper_half = lax.broadcasted_iota(I32, (8, 128), 0) < 4
    extra = jnp.zeros((8, 128), F32)
    for layer in range(3):
        for part in range(2):
            extra = jnp.where(
                lane == 120 + 2 * layer + part, shifts_ref[0, part, layer].astype(F32), extra
            )
    for q in range(4):
        x = mirrored(q)
        for d in range(8):
            zl = lax.rem(d + 4 * high, 8)
            for h in range(2):
                at = 2 * d + h
                main = wide_ref[at, TALL * q : TALL * q + 8]
                first = wide_ref[at, TALL * q + 8 : TALL * q + 16]
                second = wide_ref[at, TALL * q + 4 : TALL * q + 12]
                pieces = jnp.where(upper_half, pltpu.roll(first, 80, 1), pltpu.roll(second, 40, 1))
                chunk = jnp.where(lane < 80, main, jnp.where(lane < 120, pieces, extra))
                chunks_ref[(zl * 4 + x) * 2 + h] = chunk.astype(BF16)


def strip_kernel(layers_ref, own_ref, edge_ref):
    last = mirrored(lax.axis_index("x")) == 3
    half = lax.axis_index("c")
    block = my_block() - 1 + half
    amount = jnp.where(half == 0, 16, 80)
    left = pl.multiple_of(jnp.maximum(block, 0) * 128, 128)
    right = pl.multiple_of(jnp.minimum(block + 1, 7) * 128, 128)
    left_there = jnp.where(block >= 0, 1.0, 0.0)
    right_there = jnp.where(block + 1 <= 7, 1.0, 0.0)
    lane = lanes(48)
    for layer in range(3):
        for frame in range(3):
            a = layers_ref[frame, layer, :, pl.ds(left, 128)].astype(F32) * left_there
            b = layers_ref[frame, layer, :, pl.ds(right, 128)].astype(F32) * right_there
            cells = pltpu.roll(jnp.where(lane >= 128 - amount, a, b), amount, 1)
            own_ref[layer, frame] = cells
            edge_ref[layer, frame] = jnp.where(last, cells[48 - HALO :], cells[:HALO])


def seen_kernel(own_ref, edge_ref, seen_ref, tile_ref, tall_ref):
    q = mirrored(lax.axis_index("x"))
    start = q * TALL
    tall_ref[:, :, :HALO] = edge_ref[...]
    tall_ref[:, :, HALO : HALO + 48] = own_ref[...]
    tall_ref[:, :, HALO + 48 : 64] = edge_ref[...]
    tall_ref[:, :, 64:] = jnp.zeros((3, 3, 8, 128), F32)
    for layer in range(3):
        for frame in range(3):
            cells = tall_ref[layer, frame, pl.ds(start, 32), :]
            for d in range(SPAN):
                moved = pltpu.roll(cells, 128 - d, 1) if d else cells
                seen_ref[layer, d, frame] = moved
                if d == 16:
                    tile_ref[layer, frame] = moved[HALO : HALO + 16]


def view_kernel(
    recv_ref, seen_ref, own_out, near_out, far_out, image_ref, shift_ref, shift_smem, sem, *sums
):
    shift_ref[...] = recv_ref[:, 0, :].astype(F32).astype(I32)
    copy = pltpu.make_async_copy(shift_ref, shift_smem, sem)
    copy.start()

    lane = lanes(8)
    upper_half = lax.broadcasted_iota(I32, (8, 128), 0) < 4
    for view in range(64):
        cells = recv_ref[view].astype(F32)
        image_ref[view, :8] = cells
        low = pltpu.roll(cells, 128 - 80, 1)
        high = pltpu.roll(pltpu.roll(cells, 128 - 40, 1), 4, 0)
        rest = jnp.where(lane < 40, low, high)
        image_ref[view, 8:] = jnp.where(upper_half, rest, 0.0)

    for ref in sums:
        ref[...] = jnp.zeros_like(ref)

    column = my_block() * 128 + lax.axis_index("c") * WIDE - HALO + lanes(16)
    inside = (column >= 0) & (column < 1024)
    inside = inside & (lax.broadcasted_iota(I32, (16, 128), 0) < TALL)
    third = jnp.where(inside, 1.0 / 3.0, 0.0)
    copy.wait()

    def one_view(view, carry):
        rows = [shift_smem[view, 120 + 2 * layer] + HALO for layer in range(3)]
        cols = [shift_smem[view, 121 + 2 * layer] + HALO for layer in range(3)]
        s0, s1, s2 = (
            seen_ref[layer, cols[layer], :, pl.ds(rows[layer], 16), :] for layer in range(3)
        )
        p01 = s0 * s1
        whole = p01 * s2
        shown = (whole[0] + whole[1] + whole[2]) * third
        image = image_ref[view]
        for layer, others in enumerate((s1 * s2, s0 * s2, p01)):
            for which, factor in enumerate((image, shown)):
                sums[2 * layer + which][cols[layer], :, pl.ds(rows[layer], 16), :] += factor * others
        return carry

    lax.fori_loop(0, 64, one_view, 0)

    even = lax.rem(mirrored(lax.axis_index("x")), 2) == 0
    lane = lanes(32)
    for layer in range(3):
        for frame in range(3):
            sides = []
            for which, base in enumerate((-16, 48)):
                total = None
                for d in range(SPAN):
                    amount = (d + base) % 128
                    cells = sums[2 * layer + which][d, frame]
                    moved = pltpu.roll(cells, amount, 1) if amount else cells
                    total = moved if total is None else total + moved
                sides.append(total)
            both = jnp.where(lane < WIDE, sides[0], sides[1])
            own_out[layer, frame] = both[HALO : HALO + 16]
            up = both[:HALO]
            down = both[HALO + TALL : 2 * HALO + TALL]
            near_out[layer, frame] = jnp.where(even, down, up)
            far_out[layer, frame] = jnp.where(even, up, down)


def update_kernel(own_ref, near_ref, far_ref, tile_ref, out_ref, code_ref):
    lane = lanes(TALL)
    even = lax.rem(mirrored(lax.axis_index("x")), 2) == 0
    for layer in range(3):
        for frame in range(3):
            own = own_ref[layer, frame]
            near = near_ref[layer, frame]
            far = far_ref[layer, frame]
            above = jnp.where(even, far, near)
            below = jnp.where(even, near, far)
            none = jnp.zeros((4, 128), F32)
            both = own[:TALL] + jnp.concatenate([above, none], axis=0)
            both = both + jnp.concatenate([none, below], axis=0)
            lower = pltpu.roll(both, WIDE, 1)
            value = tile_ref[layer, frame, :TALL] * (both + REGULAR) / (lower + REGULAR)
            scaled = (jnp.log2(value) + CODE_BASE) * CODE_STEPS + 0.5
            code_ref[frame * 3 + layer, :TALL] = jnp.clip(scaled, 0.0, 65535.0).astype(I32)
    for pair in range(2):
        parts = []
        for p in (pair, pair + 2):
            even = code_ref[2 * p, :TALL]
            odd = pltpu.roll(code_ref[2 * p + 1, :TALL], WIDE, 1)
            parts.append(jnp.where(lane < WIDE, even, odd))
        word = parts[0] + (parts[1] - 32768) * 65536
        for copy in range(8):
            out_ref[copy, TALL * pair : TALL * pair + TALL] = word
    word = code_ref[8, :6] + (code_ref[8, 6:12] - 32768) * 65536
    for copy in range(8):
        out_ref[copy, 24:30] = word
        out_ref[copy, 30:] = jnp.zeros((2, 128), I32)


def dense_kernel(words_ref, out_ref):
    for zl in range(8):
        out_ref[WORDS * zl : WORDS * zl + WORDS] = words_ref[zl, :WORDS]


def decoded(code):
    return jnp.exp2(code.astype(F32) * (1.0 / CODE_STEPS) - CODE_BASE)


def spread_kernel(words_ref, out_ref, block_ref, sems):
    high = lax.axis_index("zh")

    def sent(d):
        columns = pl.ds(pl.multiple_of(d * 128, 128), 128)
        return pltpu.make_async_copy(block_ref.at[d], out_ref.at[:, :, :, columns], sems.at[d])

    def one(d, carry):
        zl = lax.rem(d + 4 * high, 8)
        for q in range(4):
            x = mirrored(q)
            rows = slice(TALL * q, TALL * q + TALL)

            def words(c, first, count):
                return words_ref[x * 2 + c, pl.ds(zl * WORDS + first, count), :]

            lane = lanes(TALL)
            for pair in range(2):
                a, b = words(0, TALL * pair, TALL), words(1, TALL * pair, TALL)
                even = jnp.where(lane < WIDE, a, pltpu.roll(b, WIDE, 1))
                odd = jnp.where(lane < WIDE, pltpu.roll(a, WIDE, 1), b)
                for side, word in enumerate((even, odd)):
                    for p, code in ((pair, word & 65535), (pair + 2, (word >> 16) + 32768)):
                        at = 2 * p + side
                        block_ref[d, at // 3, at % 3, rows] = decoded(code)
            a, b = words(0, 24, 6), words(1, 24, 6)
            word = jnp.where(lanes(6) < WIDE, a, pltpu.roll(b, WIDE, 1))
            block_ref[d, 2, 2, TALL * q : TALL * q + 6] = decoded(word & 65535)
            block_ref[d, 2, 2, TALL * q + 6 : TALL * q + TALL] = decoded((word >> 16) + 32768)
        sent(d).start()
        return carry

    lax.fori_loop(0, 8, one, 0)
    for d in range(8):
        sent(d).wait()


def strip_pairs(first, step):
    def index(block, strip):
        at, q = strip // 4, strip % 4
        x = q if at % 2 == 0 else 3 - q
        zl = (block + 4 * (at // 4)) % 8
        return ((zl * 4 + x) * 2 + at // 4) * 4 + at % 4

    pairs = []
    for block in range(8):
        for strip in range(first, 31, step):
            a, b = index(block, strip), index(block, strip + 1)
            pairs += [(a, b), (b, a)]
    return pairs


VMEM = pl.BlockSpec(memory_space=pltpu.VMEM)
SMEM = pl.BlockSpec(memory_space=pltpu.SMEM)


def call(kernel, outs, ins, scratch=(), **more):
    return pl.pallas_call(
        kernel,
        out_shape=tuple(jax.ShapeDtypeStruct(*out) for out in outs),
        in_specs=ins,
        out_specs=(VMEM,) * len(outs),
        scratch_shapes=scratch,
        compiler_params=PARAMS,
        **more,
    )


def body(layers, target, shifts):
    (chunks,) = call(
        pack_kernel,
        [((64, 8, 128), BF16)],
        [VMEM, SMEM],
        [pltpu.VMEM((16, 56, 128), F32)],
    )(target, shifts.transpose(0, 2, 1))
    received = lax.all_to_all(chunks, VIEW, 0, 0)

    own, edge = call(
        strip_kernel,
        [((3, 3, 48, 128), F32), ((3, 3, HALO, 128), F32)],
        [VMEM],
    )(layers)
    across = ("zl", "x", "zh", "y")
    edge = lax.ppermute(edge, across, strip_pairs(3, 4))
    seen, tile = call(
        seen_kernel,
        [((3, SPAN, 3, 32, 128), F32), ((3, 3, 16, 128), F32)],
        [VMEM] * 2,
        [pltpu.VMEM((3, 3, 72, 128), F32)],
    )(own, edge)

    sums, near, far = call(
        view_kernel,
        [((3, 3, 16, 128), F32), ((3, 3, HALO, 128), F32), ((3, 3, HALO, 128), F32)],
        [VMEM] * 2,
        [
            pltpu.VMEM((64, 16, 128), F32),
            pltpu.VMEM((64, 128), I32),
            pltpu.SMEM((64, 128), I32),
            pltpu.SemaphoreType.DMA,
        ]
        + [pltpu.VMEM((SPAN, 3, 32, 128), F32)] * 6,
    )(received, seen)
    near = lax.ppermute(near, across, strip_pairs(0, 2))
    far = lax.ppermute(far, across, strip_pairs(1, 2))

    (words,) = call(
        update_kernel,
        [((8, 32, 128), I32)],
        [VMEM] * 4,
        [pltpu.VMEM((9, 16, 128), I32)],
    )(sums, near, far, tile)
    words = lax.all_to_all(words, "zl", 0, 0)
    (words,) = call(dense_kernel, [((8 * WORDS, 128), I32)], [VMEM])(words)
    words = lax.all_gather(words, ("x", "c"))

    return pl.pallas_call(
        spread_kernel,
        out_shape=jax.ShapeDtypeStruct((3, 3, 48, 1024), F32),
        in_specs=[VMEM],
        out_specs=pl.BlockSpec(memory_space=pl.ANY),
        scratch_shapes=[pltpu.VMEM((8, 3, 3, 48, 128), F32), pltpu.SemaphoreType.DMA((8,))],
        compiler_params=PARAMS,
    )(words)


def solution(mesh):
    fine = Mesh(mesh.devices.reshape(8, 4, 2, 2, 4), ("zl", "x", "c", "zh", "y"))
    placed = (P(None, None, ROW, None), P(VIEW, ROW, None), P(VIEW, None, None))
    return jax.shard_map(
        body, mesh=fine, in_specs=placed, out_specs=P(None, None, ROW, None), check_vma=False
    )
```

```python
import jax
import jax.numpy as jnp
from jax import lax
from jax.experimental import pallas as pl
from jax.experimental.pallas import tpu as pltpu
from jax.sharding import Mesh, PartitionSpec as P

HALO = 8
SPAN = 2 * HALO + 1
TALL = 12
WIDE = 64
REGULAR = 0.05
CODE_STEPS = 5041.0
CODE_BASE = 7.0
WORDS = 30
F32 = jnp.float32
BF16 = jnp.bfloat16
I32 = jnp.int32
VIEW = ("zl", "x", "c")
ROW = ("zh", "y")
PARAMS = pltpu.CompilerParams(vmem_limit_bytes=48 * 1024 * 1024)


def lanes(rows):
    return lax.broadcasted_iota(I32, (rows, 128), 1)


def home(block, q, high, odd):
    pair = block >> 1
    zl = pair + 4 * (pair >> 1) if q in (0, 3) else pair + 2
    x = block & 1 if q < 2 else 3 - (block & 1)
    return zl ^ (6 * high), x + odd * (3 - 2 * x)


def place():
    return lax.axis_index("zh"), lax.rem(lax.axis_index("y"), 2)


def my_tile():
    high, odd = place()
    zl = jnp.bitwise_xor(lax.axis_index("zl"), 6 * high)
    x = lax.axis_index("x")
    x = x + odd * (3 - 2 * x)
    outer = (zl < 2) | (zl > 5)
    pair = jnp.where(zl < 2, zl, jnp.where(zl > 5, zl - 4, zl - 2))
    block = 2 * pair + jnp.where(x < 2, x, 3 - x)
    return block, jnp.where(x < 2, jnp.where(outer, 0, 1), jnp.where(outer, 3, 2))


def pack_kernel(
    target_hbm, shifts_hbm, chunks_ref, target_ref, shifts_ref, wide_ref, target_sem, shifts_sem
):
    fetch_shifts = pltpu.make_async_copy(shifts_hbm, shifts_ref, shifts_sem)
    fetch_shifts.start()
    fetch = pltpu.make_async_copy(target_hbm, target_ref, target_sem)
    fetch.start()
    high, odd = place()
    fetch.wait()
    lane = lanes(48)
    blocks = [target_ref[0, :, 128 * d : 128 * d + 128].astype(F32) for d in range(8)]
    zero = jnp.zeros((48, 128), F32)
    for d in range(8):
        left = blocks[d - 1] if d > 0 else zero
        right = blocks[d + 1] if d < 7 else zero
        mid = blocks[d]
        wide_ref[2 * d, :48] = pltpu.roll(jnp.where(lane >= 128 - HALO, left, mid), HALO, 1)
        wide_ref[2 * d + 1, :48] = pltpu.roll(jnp.where(lane < HALO, right, mid), 128 - 56, 1)
    lane = lanes(8)
    upper_half = lax.broadcasted_iota(I32, (8, 128), 0) < 4
    fetch_shifts.wait()
    extra = jnp.zeros((8, 128), F32)
    for layer in range(3):
        for part in range(2):
            extra = jnp.where(
                lane == 120 + 2 * layer + part, shifts_ref[0, part, layer].astype(F32), extra
            )
    for q in range(4):
        for d in range(8):
            zl, x = home(d, q, high, odd)
            for h in range(2):
                at = 2 * d + h
                main = wide_ref[at, TALL * q : TALL * q + 8]
                first = wide_ref[at, TALL * q + 8 : TALL * q + 16]
                second = wide_ref[at, TALL * q + 4 : TALL * q + 12]
                pieces = jnp.where(upper_half, pltpu.roll(first, 80, 1), pltpu.roll(second, 40, 1))
                chunk = jnp.where(lane < 80, main, jnp.where(lane < 120, pieces, extra))
                chunks_ref[(zl * 4 + x) * 2 + h] = chunk.astype(BF16)


def strip_kernel(layers_ref, own_ref, edge_ref):
    block, q = my_tile()
    last = q == 3
    half = lax.axis_index("c")
    block = block - 1 + half
    amount = jnp.where(half == 0, 16, 80)
    left = pl.multiple_of(jnp.maximum(block, 0) * 128, 128)
    right = pl.multiple_of(jnp.minimum(block + 1, 7) * 128, 128)
    left_there = jnp.where(block >= 0, 1.0, 0.0)
    right_there = jnp.where(block + 1 <= 7, 1.0, 0.0)
    lane = lanes(48)
    for layer in range(3):
        for frame in range(3):
            a = layers_ref[frame, layer, :, pl.ds(left, 128)].astype(F32) * left_there
            b = layers_ref[frame, layer, :, pl.ds(right, 128)].astype(F32) * right_there
            cells = pltpu.roll(jnp.where(lane >= 128 - amount, a, b), amount, 1)
            own_ref[layer, frame] = cells
            edge_ref[layer, frame] = jnp.where(last, cells[48 - HALO :], cells[:HALO])


def seen_kernel(own_ref, edge_ref, seen_ref, tile_ref, tall_ref):
    _, q = my_tile()
    start = q * TALL
    tall_ref[:, :, :HALO] = edge_ref[...]
    tall_ref[:, :, HALO : HALO + 48] = own_ref[...]
    tall_ref[:, :, HALO + 48 : 64] = edge_ref[...]
    tall_ref[:, :, 64:] = jnp.zeros((3, 3, 8, 128), F32)
    for layer in range(3):
        for frame in range(3):
            cells = tall_ref[layer, frame, pl.ds(start, 32), :]
            for d in range(SPAN):
                moved = pltpu.roll(cells, 128 - d, 1) if d else cells
                seen_ref[layer, d, frame] = moved
                if d == 16:
                    tile_ref[layer, frame] = moved[HALO : HALO + 16]


def view_kernel(
    recv_ref, seen_ref, own_out, near_out, far_out, image_ref, shift_ref, shift_smem, sem, *sums
):
    shift_ref[...] = recv_ref[:, 0, :].astype(F32).astype(I32)
    copy = pltpu.make_async_copy(shift_ref, shift_smem, sem)
    copy.start()

    lane = lanes(8)
    upper_half = lax.broadcasted_iota(I32, (8, 128), 0) < 4
    for view in range(64):
        cells = recv_ref[view].astype(F32)
        image_ref[view, :8] = cells
        low = pltpu.roll(cells, 128 - 80, 1)
        high = pltpu.roll(pltpu.roll(cells, 128 - 40, 1), 4, 0)
        rest = jnp.where(lane < 40, low, high)
        image_ref[view, 8:] = jnp.where(upper_half, rest, 0.0)

    for ref in sums:
        ref[...] = jnp.zeros_like(ref)

    block, q = my_tile()
    column = block * 128 + lax.axis_index("c") * WIDE - HALO + lanes(16)
    inside = (column >= 0) & (column < 1024)
    inside = inside & (lax.broadcasted_iota(I32, (16, 128), 0) < TALL)
    third = jnp.where(inside, 1.0 / 3.0, 0.0)
    copy.wait()

    def one_view(view, carry):
        rows = [shift_smem[view, 120 + 2 * layer] + HALO for layer in range(3)]
        cols = [shift_smem[view, 121 + 2 * layer] + HALO for layer in range(3)]
        s0, s1, s2 = (
            seen_ref[layer, cols[layer], :, pl.ds(rows[layer], 16), :] for layer in range(3)
        )
        p01 = s0 * s1
        whole = p01 * s2
        shown = (whole[0] + whole[1] + whole[2]) * third
        image = image_ref[view]
        for layer, others in enumerate((s1 * s2, s0 * s2, p01)):
            for which, factor in enumerate((image, shown)):
                sums[2 * layer + which][cols[layer], :, pl.ds(rows[layer], 16), :] += factor * others
        return carry

    lax.fori_loop(0, 64, one_view, 0)

    even = lax.rem(q, 2) == 0
    lane = lanes(32)
    for layer in range(3):
        for frame in range(3):
            sides = []
            for which, base in enumerate((-16, 48)):
                total = None
                for d in range(SPAN):
                    amount = (d + base) % 128
                    cells = sums[2 * layer + which][d, frame]
                    moved = pltpu.roll(cells, amount, 1) if amount else cells
                    total = moved if total is None else total + moved
                sides.append(total)
            both = jnp.where(lane < WIDE, sides[0], sides[1])
            own_out[layer, frame] = both[HALO : HALO + 16]
            up = both[:HALO]
            down = both[HALO + TALL : 2 * HALO + TALL]
            near_out[layer, frame] = jnp.where(even, down, up)
            far_out[layer, frame] = jnp.where(even, up, down)


def update_kernel(own_ref, near_ref, far_ref, tile_ref, out_ref, code_ref):
    lane = lanes(TALL)
    _, q = my_tile()
    even = lax.rem(q, 2) == 0
    for layer in range(3):
        for frame in range(3):
            own = own_ref[layer, frame]
            near = near_ref[layer, frame]
            far = far_ref[layer, frame]
            above = jnp.where(even, far, near)
            below = jnp.where(even, near, far)
            none = jnp.zeros((4, 128), F32)
            both = own[:TALL] + jnp.concatenate([above, none], axis=0)
            both = both + jnp.concatenate([none, below], axis=0)
            lower = pltpu.roll(both, WIDE, 1)
            value = tile_ref[layer, frame, :TALL] * (both + REGULAR) / (lower + REGULAR)
            scaled = (jnp.log2(value) + CODE_BASE) * CODE_STEPS + 0.5
            code_ref[frame * 3 + layer, :TALL] = jnp.clip(scaled, 0.0, 65535.0).astype(I32)
    for pair in range(2):
        parts = []
        for p in (pair, pair + 2):
            even = code_ref[2 * p, :TALL]
            odd = pltpu.roll(code_ref[2 * p + 1, :TALL], WIDE, 1)
            parts.append(jnp.where(lane < WIDE, even, odd))
        word = parts[0] + (parts[1] - 32768) * 65536
        for copy in range(8):
            out_ref[copy, TALL * pair : TALL * pair + TALL] = word
    word = code_ref[8, :6] + (code_ref[8, 6:12] - 32768) * 65536
    for copy in range(8):
        out_ref[copy, 24:30] = word
        out_ref[copy, 30:] = jnp.zeros((2, 128), I32)


def dense_kernel(words_ref, out_ref):
    for zl in range(8):
        out_ref[WORDS * zl : WORDS * zl + WORDS] = words_ref[zl, :WORDS]


def decoded(code):
    return jnp.exp2(code.astype(F32) * (1.0 / CODE_STEPS) - CODE_BASE)


def spread_kernel(words_ref, out_ref, block_ref, sems):
    high, flip = place()

    def sent(d):
        columns = pl.ds(pl.multiple_of(d * 128, 128), 128)
        return pltpu.make_async_copy(block_ref.at[d], out_ref.at[:, :, :, columns], sems.at[d])

    def one(d, carry):
        for q in range(4):
            zl, x = home(d, q, high, flip)
            rows = slice(TALL * q, TALL * q + TALL)

            def words(c, first, count):
                return words_ref[x * 2 + c, pl.ds(zl * WORDS + first, count), :]

            lane = lanes(TALL)
            for pair in range(2):
                a, b = words(0, TALL * pair, TALL), words(1, TALL * pair, TALL)
                even = jnp.where(lane < WIDE, a, pltpu.roll(b, WIDE, 1))
                odd = jnp.where(lane < WIDE, pltpu.roll(a, WIDE, 1), b)
                for side, word in enumerate((even, odd)):
                    for p, code in ((pair, word & 65535), (pair + 2, (word >> 16) + 32768)):
                        at = 2 * p + side
                        block_ref[d, at // 3, at % 3, rows] = decoded(code)
            a, b = words(0, 24, 6), words(1, 24, 6)
            word = jnp.where(lanes(6) < WIDE, a, pltpu.roll(b, WIDE, 1))
            block_ref[d, 2, 2, TALL * q : TALL * q + 6] = decoded(word & 65535)
            block_ref[d, 2, 2, TALL * q + 6 : TALL * q + TALL] = decoded((word >> 16) + 32768)
        sent(d).start()
        return carry

    lax.fori_loop(0, 8, one, 0)
    for d in range(8):
        sent(d).wait()


def strip_pairs(first, step):
    def index(block, strip):
        at, q = strip // 4, strip % 4
        zl, x = home(block, q, at // 4, at % 2)
        return ((zl * 4 + x) * 2 + at // 4) * 4 + at % 4

    pairs = []
    for block in range(8):
        for strip in range(first, 31, step):
            a, b = index(block, strip), index(block, strip + 1)
            pairs += [(a, b), (b, a)]
    return pairs


VMEM = pl.BlockSpec(memory_space=pltpu.VMEM)


def call(kernel, outs, ins, scratch=(), **more):
    return pl.pallas_call(
        kernel,
        out_shape=tuple(jax.ShapeDtypeStruct(*out) for out in outs),
        in_specs=ins,
        out_specs=(VMEM,) * len(outs),
        scratch_shapes=scratch,
        compiler_params=PARAMS,
        **more,
    )


def body(layers, target, shifts):
    (chunks,) = call(
        pack_kernel,
        [((64, 8, 128), BF16)],
        [pl.BlockSpec(memory_space=pl.ANY)] * 2,
        [
            pltpu.VMEM((1, 48, 1024), BF16),
            pltpu.SMEM((1, 2, 3), I32),
            pltpu.VMEM((16, 56, 128), F32),
            pltpu.SemaphoreType.DMA,
            pltpu.SemaphoreType.DMA,
        ],
    )(target, shifts.transpose(0, 2, 1))
    received = lax.all_to_all(chunks, VIEW, 0, 0)

    own, edge = call(
        strip_kernel,
        [((3, 3, 48, 128), F32), ((3, 3, HALO, 128), F32)],
        [VMEM],
    )(layers)
    across = ("zl", "x", "zh", "y")
    edge = lax.ppermute(edge, across, strip_pairs(3, 4))
    seen, tile = call(
        seen_kernel,
        [((3, SPAN, 3, 32, 128), F32), ((3, 3, 16, 128), F32)],
        [VMEM] * 2,
        [pltpu.VMEM((3, 3, 72, 128), F32)],
    )(own, edge)

    sums, near, far = call(
        view_kernel,
        [((3, 3, 16, 128), F32), ((3, 3, HALO, 128), F32), ((3, 3, HALO, 128), F32)],
        [VMEM] * 2,
        [
            pltpu.VMEM((64, 16, 128), F32),
            pltpu.VMEM((64, 128), I32),
            pltpu.SMEM((64, 128), I32),
            pltpu.SemaphoreType.DMA,
        ]
        + [pltpu.VMEM((SPAN, 3, 32, 128), F32)] * 6,
    )(received, seen)
    near = lax.ppermute(near, across, strip_pairs(0, 2))
    far = lax.ppermute(far, across, strip_pairs(1, 2))

    (words,) = call(
        update_kernel,
        [((8, 32, 128), I32)],
        [VMEM] * 4,
        [pltpu.VMEM((9, 16, 128), I32)],
    )(sums, near, far, tile)
    words = lax.all_to_all(words, "zl", 0, 0)
    (words,) = call(dense_kernel, [((8 * WORDS, 128), I32)], [VMEM])(words)
    words = lax.all_gather(words, ("x", "c"))

    return pl.pallas_call(
        spread_kernel,
        out_shape=jax.ShapeDtypeStruct((3, 3, 48, 1024), F32),
        in_specs=[VMEM],
        out_specs=pl.BlockSpec(memory_space=pl.ANY),
        scratch_shapes=[pltpu.VMEM((8, 3, 3, 48, 128), F32), pltpu.SemaphoreType.DMA((8,))],
        compiler_params=PARAMS,
    )(words)


def solution(mesh):
    fine = Mesh(mesh.devices.reshape(8, 4, 2, 2, 4), ("zl", "x", "c", "zh", "y"))
    placed = (P(None, None, ROW, None), P(VIEW, ROW, None), P(VIEW, None, None))
    return jax.shard_map(
        body, mesh=fine, in_specs=placed, out_specs=P(None, None, ROW, None), check_vma=False
    )
```

```python
import jax
import jax.numpy as jnp
from jax import lax
from jax.experimental import pallas as pl
from jax.experimental.pallas import tpu as pltpu
from jax.sharding import Mesh, PartitionSpec as P

HALO = 8
SPAN = 2 * HALO + 1
TALL = 12
WIDE = 64
REGULAR = 0.05
CODE_STEPS = 5041.0
CODE_BASE = 7.0
WORDS = 30
F32 = jnp.float32
BF16 = jnp.bfloat16
I32 = jnp.int32
VIEW = ("zl", "x", "c")
ROW = ("zh", "y")
PARAMS = pltpu.CompilerParams(vmem_limit_bytes=48 * 1024 * 1024)


def lanes(rows):
    return lax.broadcasted_iota(I32, (rows, 128), 1)


def home(block, half, q, high, odd):
    column = 2 * block + half
    at = column >> 2
    outer, inner = at + 4 * (at >> 1), at + 2
    zl = outer + ((q >> 1) ^ odd) * (inner - outer)
    return zl ^ (6 * high), column & 3, q & 1


def place():
    return lax.axis_index("zh"), lax.rem(lax.axis_index("y"), 2)


def my_tile():
    high, odd = place()
    zl = jnp.bitwise_xor(lax.axis_index("zl"), 6 * high)
    outer = (zl < 2) | (zl > 5)
    at = jnp.where(zl < 2, zl, jnp.where(zl > 5, zl - 4, zl - 2))
    column = 4 * at + lax.axis_index("x")
    q = 2 * jnp.where(outer, odd, 1 - odd) + lax.axis_index("c")
    return column >> 1, column & 1, q


def pack_kernel(
    target_hbm, shifts_hbm, chunks_ref, target_ref, shifts_ref, wide_ref, target_sem, shifts_sem
):
    fetch_shifts = pltpu.make_async_copy(shifts_hbm, shifts_ref, shifts_sem)
    fetch_shifts.start()
    fetch = pltpu.make_async_copy(target_hbm, target_ref, target_sem)
    fetch.start()
    high, odd = place()
    fetch.wait()
    lane = lanes(48)
    blocks = [target_ref[0, :, 128 * d : 128 * d + 128].astype(F32) for d in range(8)]
    zero = jnp.zeros((48, 128), F32)
    for d in range(8):
        left = blocks[d - 1] if d > 0 else zero
        right = blocks[d + 1] if d < 7 else zero
        mid = blocks[d]
        wide_ref[2 * d, :48] = pltpu.roll(jnp.where(lane >= 128 - HALO, left, mid), HALO, 1)
        wide_ref[2 * d + 1, :48] = pltpu.roll(jnp.where(lane < HALO, right, mid), 128 - 56, 1)
    lane = lanes(8)
    upper_half = lax.broadcasted_iota(I32, (8, 128), 0) < 4
    fetch_shifts.wait()
    extra = jnp.zeros((8, 128), F32)
    for layer in range(3):
        for part in range(2):
            extra = jnp.where(
                lane == 120 + 2 * layer + part, shifts_ref[0, part, layer].astype(F32), extra
            )
    for q in range(4):
        for d in range(8):
            for h in range(2):
                zl, x, c = home(d, h, q, high, odd)
                at = 2 * d + h
                main = wide_ref[at, TALL * q : TALL * q + 8]
                first = wide_ref[at, TALL * q + 8 : TALL * q + 16]
                second = wide_ref[at, TALL * q + 4 : TALL * q + 12]
                pieces = jnp.where(upper_half, pltpu.roll(first, 80, 1), pltpu.roll(second, 40, 1))
                chunk = jnp.where(lane < 80, main, jnp.where(lane < 120, pieces, extra))
                chunks_ref[(zl * 4 + x) * 2 + c] = chunk.astype(BF16)


def strip_kernel(layers_ref, own_ref, edge_ref):
    block, half, q = my_tile()
    last = q == 3
    block = block - 1 + half
    amount = jnp.where(half == 0, 16, 80)
    left = pl.multiple_of(jnp.maximum(block, 0) * 128, 128)
    right = pl.multiple_of(jnp.minimum(block + 1, 7) * 128, 128)
    left_there = jnp.where(block >= 0, 1.0, 0.0)
    right_there = jnp.where(block + 1 <= 7, 1.0, 0.0)
    lane = lanes(48)
    for layer in range(3):
        for frame in range(3):
            a = layers_ref[frame, layer, :, pl.ds(left, 128)].astype(F32) * left_there
            b = layers_ref[frame, layer, :, pl.ds(right, 128)].astype(F32) * right_there
            cells = pltpu.roll(jnp.where(lane >= 128 - amount, a, b), amount, 1)
            own_ref[layer, frame] = cells
            edge_ref[layer, frame] = jnp.where(last, cells[48 - HALO :], cells[:HALO])


def seen_kernel(own_ref, edge_ref, seen_ref, tile_ref, tall_ref):
    _, _, q = my_tile()
    start = q * TALL
    tall_ref[:, :, :HALO] = edge_ref[...]
    tall_ref[:, :, HALO : HALO + 48] = own_ref[...]
    tall_ref[:, :, HALO + 48 : 64] = edge_ref[...]
    tall_ref[:, :, 64:] = jnp.zeros((3, 3, 8, 128), F32)
    for layer in range(3):
        for frame in range(3):
            cells = tall_ref[layer, frame, pl.ds(start, 32), :]
            for d in range(SPAN):
                moved = pltpu.roll(cells, 128 - d, 1) if d else cells
                seen_ref[layer, d, frame] = moved
                if d == 16:
                    tile_ref[layer, frame] = moved[HALO : HALO + 16]


def view_kernel(
    recv_ref, seen_ref, own_out, near_out, far_out, image_ref, shift_ref, shift_smem, sem, *sums
):
    shift_ref[...] = recv_ref[:, 0, :].astype(F32).astype(I32)
    copy = pltpu.make_async_copy(shift_ref, shift_smem, sem)
    copy.start()

    lane = lanes(8)
    upper_half = lax.broadcasted_iota(I32, (8, 128), 0) < 4
    for view in range(64):
        cells = recv_ref[view].astype(F32)
        image_ref[view, :8] = cells
        low = pltpu.roll(cells, 128 - 80, 1)
        high = pltpu.roll(pltpu.roll(cells, 128 - 40, 1), 4, 0)
        rest = jnp.where(lane < 40, low, high)
        image_ref[view, 8:] = jnp.where(upper_half, rest, 0.0)

    for ref in sums:
        ref[...] = jnp.zeros_like(ref)

    block, half, q = my_tile()
    column = block * 128 + half * WIDE - HALO + lanes(16)
    inside = (column >= 0) & (column < 1024)
    inside = inside & (lax.broadcasted_iota(I32, (16, 128), 0) < TALL)
    third = jnp.where(inside, 1.0 / 3.0, 0.0)
    copy.wait()

    def one_view(view, carry):
        rows = [shift_smem[view, 120 + 2 * layer] + HALO for layer in range(3)]
        cols = [shift_smem[view, 121 + 2 * layer] + HALO for layer in range(3)]
        s0, s1, s2 = (
            seen_ref[layer, cols[layer], :, pl.ds(rows[layer], 16), :] for layer in range(3)
        )
        p01 = s0 * s1
        whole = p01 * s2
        shown = (whole[0] + whole[1] + whole[2]) * third
        image = image_ref[view]
        for layer, others in enumerate((s1 * s2, s0 * s2, p01)):
            for which, factor in enumerate((image, shown)):
                sums[2 * layer + which][cols[layer], :, pl.ds(rows[layer], 16), :] += factor * others
        return carry

    lax.fori_loop(0, 64, one_view, 0)

    even = lax.rem(q, 2) == 0
    lane = lanes(32)
    for layer in range(3):
        for frame in range(3):
            sides = []
            for which, base in enumerate((-16, 48)):
                total = None
                for d in range(SPAN):
                    amount = (d + base) % 128
                    cells = sums[2 * layer + which][d, frame]
                    moved = pltpu.roll(cells, amount, 1) if amount else cells
                    total = moved if total is None else total + moved
                sides.append(total)
            both = jnp.where(lane < WIDE, sides[0], sides[1])
            own_out[layer, frame] = both[HALO : HALO + 16]
            up = both[:HALO]
            down = both[HALO + TALL : 2 * HALO + TALL]
            near_out[layer, frame] = jnp.where(even, down, up)
            far_out[layer, frame] = jnp.where(even, up, down)


def update_kernel(own_ref, near_ref, far_ref, tile_ref, out_ref, code_ref):
    lane = lanes(TALL)
    _, _, q = my_tile()
    even = lax.rem(q, 2) == 0
    for layer in range(3):
        for frame in range(3):
            own = own_ref[layer, frame]
            near = near_ref[layer, frame]
            far = far_ref[layer, frame]
            above = jnp.where(even, far, near)
            below = jnp.where(even, near, far)
            none = jnp.zeros((4, 128), F32)
            both = own[:TALL] + jnp.concatenate([above, none], axis=0)
            both = both + jnp.concatenate([none, below], axis=0)
            lower = pltpu.roll(both, WIDE, 1)
            value = tile_ref[layer, frame, :TALL] * (both + REGULAR) / (lower + REGULAR)
            scaled = (jnp.log2(value) + CODE_BASE) * CODE_STEPS + 0.5
            code_ref[frame * 3 + layer, :TALL] = jnp.clip(scaled, 0.0, 65535.0).astype(I32)
    for pair in range(2):
        parts = []
        for p in (pair, pair + 2):
            even = code_ref[2 * p, :TALL]
            odd = pltpu.roll(code_ref[2 * p + 1, :TALL], WIDE, 1)
            parts.append(jnp.where(lane < WIDE, even, odd))
        word = parts[0] + (parts[1] - 32768) * 65536
        for copy in range(8):
            out_ref[copy, TALL * pair : TALL * pair + TALL] = word
    word = code_ref[8, :6] + (code_ref[8, 6:12] - 32768) * 65536
    for copy in range(8):
        out_ref[copy, 24:30] = word
        out_ref[copy, 30:] = jnp.zeros((2, 128), I32)


def dense_kernel(words_ref, out_ref):
    for zl in range(8):
        out_ref[WORDS * zl : WORDS * zl + WORDS] = words_ref[zl, :WORDS]


def decoded(code):
    return jnp.exp2(code.astype(F32) * (1.0 / CODE_STEPS) - CODE_BASE)


def spread_kernel(words_ref, out_ref, block_ref, sems):
    high, flip = place()

    def sent(d):
        columns = pl.ds(pl.multiple_of(d * 128, 128), 128)
        return pltpu.make_async_copy(block_ref.at[d], out_ref.at[:, :, :, columns], sems.at[d])

    def one(d, carry):
        for q in range(4):
            rows = slice(TALL * q, TALL * q + TALL)

            def words(half, first, count):
                zl, x, c = home(d, half, q, high, flip)
                return words_ref[x * 2 + c, pl.ds(zl * WORDS + first, count), :]

            lane = lanes(TALL)
            for pair in range(2):
                a, b = words(0, TALL * pair, TALL), words(1, TALL * pair, TALL)
                even = jnp.where(lane < WIDE, a, pltpu.roll(b, WIDE, 1))
                odd = jnp.where(lane < WIDE, pltpu.roll(a, WIDE, 1), b)
                for side, word in enumerate((even, odd)):
                    for p, code in ((pair, word & 65535), (pair + 2, (word >> 16) + 32768)):
                        at = 2 * p + side
                        block_ref[d, at // 3, at % 3, rows] = decoded(code)
            a, b = words(0, 24, 6), words(1, 24, 6)
            word = jnp.where(lanes(6) < WIDE, a, pltpu.roll(b, WIDE, 1))
            block_ref[d, 2, 2, TALL * q : TALL * q + 6] = decoded(word & 65535)
            block_ref[d, 2, 2, TALL * q + 6 : TALL * q + TALL] = decoded((word >> 16) + 32768)
        sent(d).start()
        return carry

    lax.fori_loop(0, 8, one, 0)
    for d in range(8):
        sent(d).wait()


def strip_pairs(first, step):
    def index(column, strip):
        at = strip // 4
        zl, x, c = home(column // 2, column % 2, strip % 4, at // 4, at % 2)
        return (((zl * 4 + x) * 2 + c) * 2 + at // 4) * 4 + at % 4

    pairs = []
    for column in range(16):
        for strip in range(first, 31, step):
            a, b = index(column, strip), index(column, strip + 1)
            pairs += [(a, b), (b, a)]
    return pairs


VMEM = pl.BlockSpec(memory_space=pltpu.VMEM)


def call(kernel, outs, ins, scratch=(), **more):
    return pl.pallas_call(
        kernel,
        out_shape=tuple(jax.ShapeDtypeStruct(*out) for out in outs),
        in_specs=ins,
        out_specs=(VMEM,) * len(outs),
        scratch_shapes=scratch,
        compiler_params=PARAMS,
        **more,
    )


def body(layers, target, shifts):
    (chunks,) = call(
        pack_kernel,
        [((64, 8, 128), BF16)],
        [pl.BlockSpec(memory_space=pltpu.HBM)] * 2,
        [
            pltpu.VMEM((1, 48, 1024), BF16),
            pltpu.SMEM((1, 2, 3), I32),
            pltpu.VMEM((16, 56, 128), F32),
            pltpu.SemaphoreType.DMA,
            pltpu.SemaphoreType.DMA,
        ],
    )(target, shifts.transpose(0, 2, 1))
    received = lax.all_to_all(chunks, VIEW, 0, 0)

    own, edge = call(
        strip_kernel,
        [((3, 3, 48, 128), F32), ((3, 3, HALO, 128), F32)],
        [VMEM],
    )(layers)
    across = VIEW + ROW
    edge = lax.ppermute(edge, across, strip_pairs(3, 4))
    seen, tile = call(
        seen_kernel,
        [((3, SPAN, 3, 32, 128), F32), ((3, 3, 16, 128), F32)],
        [VMEM] * 2,
        [pltpu.VMEM((3, 3, 72, 128), F32)],
    )(own, edge)

    sums, near, far = call(
        view_kernel,
        [((3, 3, 16, 128), F32), ((3, 3, HALO, 128), F32), ((3, 3, HALO, 128), F32)],
        [VMEM] * 2,
        [
            pltpu.VMEM((64, 16, 128), F32),
            pltpu.VMEM((64, 128), I32),
            pltpu.SMEM((64, 128), I32),
            pltpu.SemaphoreType.DMA,
        ]
        + [pltpu.VMEM((SPAN, 3, 32, 128), F32)] * 6,
    )(received, seen)
    far = lax.ppermute(far, across, strip_pairs(1, 2))
    near = lax.ppermute(near, across, strip_pairs(0, 2))

    (words,) = call(
        update_kernel,
        [((8, 32, 128), I32)],
        [VMEM] * 4,
        [pltpu.VMEM((9, 16, 128), I32)],
    )(sums, near, far, tile)
    words = lax.all_to_all(words, "zl", 0, 0)
    (words,) = call(dense_kernel, [((8 * WORDS, 128), I32)], [VMEM])(words)
    words = lax.all_gather(words, ("x", "c"))

    return pl.pallas_call(
        spread_kernel,
        out_shape=jax.ShapeDtypeStruct((3, 3, 48, 1024), F32),
        in_specs=[VMEM],
        out_specs=pl.BlockSpec(memory_space=pl.ANY),
        scratch_shapes=[pltpu.VMEM((8, 3, 3, 48, 128), F32), pltpu.SemaphoreType.DMA((8,))],
        compiler_params=PARAMS,
    )(words)


def solution(mesh):
    fine = Mesh(mesh.devices.reshape(8, 4, 2, 2, 4), ("zl", "x", "c", "zh", "y"))
    placed = (P(None, None, ROW, None), P(VIEW, ROW, None), P(VIEW, None, None))
    return jax.shard_map(
        body, mesh=fine, in_specs=placed, out_specs=P(None, None, ROW, None), check_vma=False
    )
```

```python
import jax
import jax.numpy as jnp
from jax import lax
from jax.experimental import pallas as pl
from jax.experimental.pallas import tpu as pltpu
from jax.sharding import Mesh, PartitionSpec as P

HALO = 8
SPAN = 2 * HALO + 1
TALL = 12
WIDE = 64
REGULAR = 0.05
CODE_STEPS = 5041.0
CODE_BASE = 7.0
WORDS = 30
F32 = jnp.float32
BF16 = jnp.bfloat16
I32 = jnp.int32
VIEW = ("zl", "x", "c")
ROW = ("zh", "y")
PARAMS = pltpu.CompilerParams(vmem_limit_bytes=16 * 1024 * 1024)
WHOLE = pltpu.CompilerParams(vmem_limit_bytes=64 * 1024 * 1024)


def lanes(rows):
    return lax.broadcasted_iota(I32, (rows, 128), 1)


def home(block, half, q, high, odd):
    column = 2 * block + half
    at = column >> 2
    outer, inner = at + 4 * (at >> 1), at + 2
    zl = outer + ((q >> 1) ^ odd) * (inner - outer)
    return zl ^ (6 * high), column & 3, q & 1


def place():
    return lax.axis_index("zh"), lax.rem(lax.axis_index("y"), 2)


def my_tile():
    high, odd = place()
    zl = jnp.bitwise_xor(lax.axis_index("zl"), 6 * high)
    outer = (zl < 2) | (zl > 5)
    at = jnp.where(zl < 2, zl, jnp.where(zl > 5, zl - 4, zl - 2))
    column = 4 * at + lax.axis_index("x")
    q = 2 * jnp.where(outer, odd, 1 - odd) + lax.axis_index("c")
    return column >> 1, column & 1, q


def pack_kernel(
    target_hbm, shifts_hbm, chunks_ref, target_ref, shifts_ref, wide_ref, target_sem, shifts_sem
):
    fetch_shifts = pltpu.make_async_copy(shifts_hbm, shifts_ref, shifts_sem)
    fetch_shifts.start()
    fetch = pltpu.make_async_copy(target_hbm, target_ref, target_sem)
    fetch.start()
    high, odd = place()
    fetch.wait()
    lane = lanes(48)
    blocks = [target_ref[0, :, 128 * d : 128 * d + 128].astype(F32) for d in range(8)]
    zero = jnp.zeros((48, 128), F32)
    for d in range(8):
        left = blocks[d - 1] if d > 0 else zero
        right = blocks[d + 1] if d < 7 else zero
        mid = blocks[d]
        wide_ref[2 * d, :48] = pltpu.roll(jnp.where(lane >= 128 - HALO, left, mid), HALO, 1)
        wide_ref[2 * d + 1, :48] = pltpu.roll(jnp.where(lane < HALO, right, mid), 128 - 56, 1)
    lane = lanes(8)
    upper_half = lax.broadcasted_iota(I32, (8, 128), 0) < 4
    fetch_shifts.wait()
    extra = jnp.zeros((8, 128), F32)
    for layer in range(3):
        for part in range(2):
            extra = jnp.where(
                lane == 120 + 2 * layer + part, shifts_ref[0, part, layer].astype(F32), extra
            )
    for q in range(4):
        for d in range(8):
            for h in range(2):
                zl, x, c = home(d, h, q, high, odd)
                at = 2 * d + h
                main = wide_ref[at, TALL * q : TALL * q + 8]
                first = wide_ref[at, TALL * q + 8 : TALL * q + 16]
                second = wide_ref[at, TALL * q + 4 : TALL * q + 12]
                pieces = jnp.where(upper_half, pltpu.roll(first, 80, 1), pltpu.roll(second, 40, 1))
                chunk = jnp.where(lane < 80, main, jnp.where(lane < 120, pieces, extra))
                chunks_ref[(zl * 4 + x) * 2 + c] = chunk.astype(BF16)


def strip_kernel(layers_ref, own_ref, edge_ref):
    block, half, q = my_tile()
    last = q == 3
    block = block - 1 + half
    amount = jnp.where(half == 0, 16, 80)
    left = pl.multiple_of(jnp.maximum(block, 0) * 128, 128)
    right = pl.multiple_of(jnp.minimum(block + 1, 7) * 128, 128)
    left_there = jnp.where(block >= 0, 1.0, 0.0)
    right_there = jnp.where(block + 1 <= 7, 1.0, 0.0)
    lane = lanes(48)
    for layer in range(3):
        for frame in range(3):
            a = layers_ref[frame, layer, :, pl.ds(left, 128)].astype(F32) * left_there
            b = layers_ref[frame, layer, :, pl.ds(right, 128)].astype(F32) * right_there
            cells = pltpu.roll(jnp.where(lane >= 128 - amount, a, b), amount, 1)
            own_ref[layer, frame] = cells
            edge_ref[layer, frame] = jnp.where(last, cells[48 - HALO :], cells[:HALO])


def seen_kernel(own_ref, edge_ref, seen_ref, tile_ref, tall_ref):
    _, _, q = my_tile()
    start = q * TALL
    tall_ref[:, :, :HALO] = edge_ref[...]
    tall_ref[:, :, HALO : HALO + 48] = own_ref[...]
    tall_ref[:, :, HALO + 48 : 64] = edge_ref[...]
    tall_ref[:, :, 64:] = jnp.zeros((3, 3, 8, 128), F32)
    for layer in range(3):
        for frame in range(3):
            cells = tall_ref[layer, frame, pl.ds(start, 32), :]
            for d in range(SPAN):
                moved = pltpu.roll(cells, 128 - d, 1) if d else cells
                seen_ref[layer, d, frame] = moved
                if d == 16:
                    tile_ref[layer, frame] = moved[HALO : HALO + 16]


def view_kernel(
    recv_ref, seen_ref, far_out, near_out, s0_ref, s1_ref, s2_ref, s3_ref, s4_ref, s5_ref,
    image_ref, shift_ref, shift_smem, sem,
):
    sums = (s0_ref, s1_ref, s2_ref, s3_ref, s4_ref, s5_ref)
    shift_ref[...] = recv_ref[:, 0, :].astype(F32).astype(I32)
    copy = pltpu.make_async_copy(shift_ref, shift_smem, sem)
    copy.start()

    lane = lanes(8)
    upper_half = lax.broadcasted_iota(I32, (8, 128), 0) < 4
    for view in range(64):
        cells = recv_ref[view].astype(F32)
        image_ref[view, :8] = cells
        low = pltpu.roll(cells, 128 - 80, 1)
        high = pltpu.roll(pltpu.roll(cells, 128 - 40, 1), 4, 0)
        rest = jnp.where(lane < 40, low, high)
        image_ref[view, 8:] = jnp.where(upper_half, rest, 0.0)

    for ref in sums:
        ref[...] = jnp.zeros_like(ref)

    block, half, q = my_tile()
    column = block * 128 + half * WIDE - HALO + lanes(16)
    inside = (column >= 0) & (column < 1024)
    inside = inside & (lax.broadcasted_iota(I32, (16, 128), 0) < TALL)
    third = jnp.where(inside, 1.0 / 3.0, 0.0)
    copy.wait()

    def one_view(view, carry):
        rows = [shift_smem[view, 120 + 2 * layer] + HALO for layer in range(3)]
        cols = [shift_smem[view, 121 + 2 * layer] + HALO for layer in range(3)]
        s0, s1, s2 = (
            seen_ref[layer, cols[layer], :, pl.ds(rows[layer], 16), :] for layer in range(3)
        )
        p01 = s0 * s1
        whole = p01 * s2
        shown = (whole[0] + whole[1] + whole[2]) * third
        image = image_ref[view]
        for layer, others in enumerate((s1 * s2, s0 * s2, p01)):
            for which, factor in enumerate((image, shown)):
                sums[2 * layer + which][cols[layer], :, pl.ds(rows[layer], 16), :] += factor * others
        return carry

    lax.fori_loop(0, 64, one_view, 0, unroll=4)

    even = lax.rem(q, 2) == 0
    far_start = jnp.where(even, 0, HALO + TALL)
    near_start = jnp.where(even, HALO + TALL, 0)
    for layer in range(3):
        for frame in range(3):
            far_out[layer, frame] = folded(sums, layer, frame, far_start, HALO)
            near_out[layer, frame] = folded(sums, layer, frame, near_start, HALO)


def folded(sums, layer, frame, start, rows):
    sides = []
    for which, base in enumerate((-16, 48)):
        total = None
        for d in range(SPAN):
            amount = (d + base) % 128
            cells = sums[2 * layer + which][d, frame, pl.ds(start, rows), :]
            moved = pltpu.roll(cells, amount, 1) if amount else cells
            total = moved if total is None else total + moved
        sides.append(total)
    return jnp.where(lanes(rows) < WIDE, sides[0], sides[1])


def own_kernel(s0_ref, s1_ref, s2_ref, s3_ref, s4_ref, s5_ref, own_out):
    sums = (s0_ref, s1_ref, s2_ref, s3_ref, s4_ref, s5_ref)
    for layer in range(3):
        for frame in range(3):
            own_out[layer, frame] = folded(sums, layer, frame, HALO, 16)


def update_kernel(own_ref, far_ref, near_ref, tile_ref, out_ref, code_ref):
    lane = lanes(TALL)
    other = 1 - lax.axis_index("c")
    _, _, q = my_tile()
    even = lax.rem(q, 2) == 0
    for layer in range(3):
        for frame in range(3):
            own = own_ref[layer, frame]
            near = near_ref[other, layer, frame]
            far = far_ref[layer, frame]
            above = jnp.where(even, far, near)
            below = jnp.where(even, near, far)
            none = jnp.zeros((4, 128), F32)
            both = own[:TALL] + jnp.concatenate([above, none], axis=0)
            both = both + jnp.concatenate([none, below], axis=0)
            lower = pltpu.roll(both, WIDE, 1)
            value = tile_ref[layer, frame, :TALL] * (both + REGULAR) / (lower + REGULAR)
            scaled = (jnp.log2(value) + CODE_BASE) * CODE_STEPS + 0.5
            code_ref[frame * 3 + layer, :TALL] = jnp.clip(scaled, 0.0, 65535.0).astype(I32)
    for pair in range(2):
        parts = []
        for p in (pair, pair + 2):
            even = code_ref[2 * p, :TALL]
            odd = pltpu.roll(code_ref[2 * p + 1, :TALL], WIDE, 1)
            parts.append(jnp.where(lane < WIDE, even, odd))
        word = parts[0] + (parts[1] - 32768) * 65536
        for copy in range(8):
            out_ref[copy, TALL * pair : TALL * pair + TALL] = word
    word = code_ref[8, :6] + (code_ref[8, 6:12] - 32768) * 65536
    for copy in range(8):
        out_ref[copy, 24:30] = word
        out_ref[copy, 30:] = jnp.zeros((2, 128), I32)


def dense_kernel(words_ref, out_ref):
    for zl in range(8):
        out_ref[WORDS * zl : WORDS * zl + WORDS] = words_ref[zl, :WORDS]


def decoded(code):
    return jnp.exp2(code.astype(F32) * (1.0 / CODE_STEPS) - CODE_BASE)


def spread_kernel(words_ref, out_ref, block_ref, sems):
    high, flip = place()

    def sent(d):
        columns = pl.ds(pl.multiple_of(d * 128, 128), 128)
        return pltpu.make_async_copy(block_ref.at[d], out_ref.at[:, :, :, columns], sems.at[d])

    def one(d, carry):
        for q in range(4):
            rows = slice(TALL * q, TALL * q + TALL)

            def words(half, first, count):
                zl, x, c = home(d, half, q, high, flip)
                return words_ref[x * 2 + c, pl.ds(zl * WORDS + first, count), :]

            lane = lanes(TALL)
            for pair in range(2):
                a, b = words(0, TALL * pair, TALL), words(1, TALL * pair, TALL)
                even = jnp.where(lane < WIDE, a, pltpu.roll(b, WIDE, 1))
                odd = jnp.where(lane < WIDE, pltpu.roll(a, WIDE, 1), b)
                for side, word in enumerate((even, odd)):
                    for p, code in ((pair, word & 65535), (pair + 2, (word >> 16) + 32768)):
                        at = 2 * p + side
                        block_ref[d, at // 3, at % 3, rows] = decoded(code)
            a, b = words(0, 24, 6), words(1, 24, 6)
            word = jnp.where(lanes(6) < WIDE, a, pltpu.roll(b, WIDE, 1))
            block_ref[d, 2, 2, TALL * q : TALL * q + 6] = decoded(word & 65535)
            block_ref[d, 2, 2, TALL * q + 6 : TALL * q + TALL] = decoded((word >> 16) + 32768)
        sent(d).start()
        return carry

    lax.fori_loop(0, 8, one, 0)
    for d in range(8):
        sent(d).wait()


def strip_pairs(first, step):
    def index(column, strip):
        at = strip // 4
        zl, x, c = home(column // 2, column % 2, strip % 4, at // 4, at % 2)
        return (((zl * 4 + x) * 2 + c) * 2 + at // 4) * 4 + at % 4

    pairs = []
    for column in range(16):
        for strip in range(first, 31, step):
            a, b = index(column, strip), index(column, strip + 1)
            pairs += [(a, b), (b, a)]
    return pairs


VMEM = pl.BlockSpec(memory_space=pltpu.VMEM)


VIEW_SCRATCH = [
    pltpu.VMEM((64, 16, 128), F32),
    pltpu.VMEM((64, 128), I32),
    pltpu.SMEM((64, 128), I32),
    pltpu.SemaphoreType.DMA,
]


def call(kernel, outs, ins, scratch=(), params=PARAMS, cost=None):
    return pl.pallas_call(
        kernel,
        out_shape=tuple(jax.ShapeDtypeStruct(*out) for out in outs),
        in_specs=ins,
        out_specs=(VMEM,) * len(outs),
        scratch_shapes=scratch,
        compiler_params=params,
        cost_estimate=cost,
    )


def body(layers, target, shifts):
    (chunks,) = call(
        pack_kernel,
        [((64, 8, 128), BF16)],
        [pl.BlockSpec(memory_space=pltpu.HBM)] * 2,
        [
            pltpu.VMEM((1, 48, 1024), BF16),
            pltpu.SMEM((1, 2, 3), I32),
            pltpu.VMEM((16, 56, 128), F32),
            pltpu.SemaphoreType.DMA,
            pltpu.SemaphoreType.DMA,
        ],
        WHOLE,
    )(target, shifts.transpose(0, 2, 1))
    received = lax.all_to_all(chunks, VIEW, 0, 0)

    own, edge = call(
        strip_kernel,
        [((3, 3, 48, 128), F32), ((3, 3, HALO, 128), F32)],
        [VMEM],
    )(layers)
    across = VIEW + ROW
    edge = lax.ppermute(edge, across, strip_pairs(3, 4))
    seen, tile = call(
        seen_kernel,
        [((3, SPAN, 3, 32, 128), F32), ((3, 3, 16, 128), F32)],
        [VMEM] * 2,
        [pltpu.VMEM((3, 3, 72, 128), F32)],
    )(own, edge)

    far, near, *sums = call(
        view_kernel,
        [((3, 3, HALO, 128), F32)] * 2 + [((SPAN, 3, 32, 128), F32)] * 6,
        [VMEM] * 2,
        VIEW_SCRATCH,
    )(received, seen)
    far = lax.ppermute(far, across, strip_pairs(1, 2))
    (own,) = call(
        own_kernel,
        [((3, 3, 16, 128), F32)],
        [VMEM] * 6,
        cost=pl.CostEstimate(flops=4_000_000, bytes_accessed=5_100_000, transcendentals=0),
    )(*sums)
    near = lax.all_gather(near, "c")

    (words,) = call(
        update_kernel,
        [((8, 32, 128), I32)],
        [VMEM] * 4,
        [pltpu.VMEM((9, 16, 128), I32)],
    )(own, far, near, tile)
    words = lax.all_to_all(words, "zl", 0, 0)
    (words,) = call(dense_kernel, [((8 * WORDS, 128), I32)], [VMEM])(words)
    words = lax.all_gather(words, ("x", "c"))

    return pl.pallas_call(
        spread_kernel,
        out_shape=jax.ShapeDtypeStruct((3, 3, 48, 1024), F32),
        in_specs=[VMEM],
        out_specs=pl.BlockSpec(memory_space=pl.ANY),
        scratch_shapes=[pltpu.VMEM((8, 3, 3, 48, 128), F32), pltpu.SemaphoreType.DMA((8,))],
        compiler_params=PARAMS,
    )(words)


def solution(mesh):
    fine = Mesh(mesh.devices.reshape(8, 4, 2, 2, 4), ("zl", "x", "c", "zh", "y"))
    placed = (P(None, None, ROW, None), P(VIEW, ROW, None), P(VIEW, None, None))
    return jax.shard_map(
        body, mesh=fine, in_specs=placed, out_specs=P(None, None, ROW, None), check_vma=False
    )
```

```python
import jax
import jax.numpy as jnp
from jax import lax
from jax.experimental import pallas as pl
from jax.experimental.pallas import tpu as pltpu
from jax.sharding import Mesh, PartitionSpec as P

HALO = 8
SPAN = 2 * HALO + 1
TALL = 12
WIDE = 64
REGULAR = 0.05
CODE_STEPS = 5041.0
CODE_BASE = 7.0
MAIN = 24
REST = 3
F32 = jnp.float32
BF16 = jnp.bfloat16
I32 = jnp.int32
VIEW = ("zl", "x", "c")
ROW = ("zh", "y")
PARAMS = pltpu.CompilerParams(vmem_limit_bytes=16 * 1024 * 1024)
WHOLE = pltpu.CompilerParams(vmem_limit_bytes=64 * 1024 * 1024)


def lanes(rows):
    return lax.broadcasted_iota(I32, (rows, 128), 1)


def home(block, half, q, high, odd):
    column = 2 * block + half
    at = column >> 2
    outer, inner = at + 4 * (at >> 1), at + 2
    zl = outer + ((q >> 1) ^ odd) * (inner - outer)
    return zl ^ (6 * high), column & 3, q & 1


def place():
    return lax.axis_index("zh"), lax.rem(lax.axis_index("y"), 2)


def my_tile():
    high, odd = place()
    zl = jnp.bitwise_xor(lax.axis_index("zl"), 6 * high)
    outer = (zl < 2) | (zl > 5)
    at = jnp.where(zl < 2, zl, jnp.where(zl > 5, zl - 4, zl - 2))
    column = 4 * at + lax.axis_index("x")
    q = 2 * jnp.where(outer, odd, 1 - odd) + lax.axis_index("c")
    return column >> 1, column & 1, q


def window(block, half):
    first = block - 1 + half
    left = pl.multiple_of(jnp.maximum(first, 0) * 128, 128)
    right = pl.multiple_of(jnp.minimum(first + 1, 7) * 128, 128)
    there = jnp.where(first >= 0, 1.0, 0.0), jnp.where(first < 7, 1.0, 0.0)
    return left, right, there, jnp.where(half == 0, 16, 80)


def joined(a, b, there, amount):
    lane = lanes(a.shape[0])
    a = a.astype(F32) * there[0]
    b = b.astype(F32) * there[1]
    return pltpu.roll(jnp.where(lane >= 128 - amount, a, b), amount, 1)


def pack_kernel(
    target_hbm, shifts_hbm, layers_hbm, chunks_ref, edge_out,
    target_ref, shifts_ref, near_edge, wide_ref, target_sem, shifts_sem, edge_sems,
):
    fetch_shifts = pltpu.make_async_copy(shifts_hbm, shifts_ref, shifts_sem)
    fetch_shifts.start()
    fetch = pltpu.make_async_copy(target_hbm, target_ref, target_sem)
    fetch.start()
    block, half, q = my_tile()
    last = q == 3
    left, right, there, amount = window(block, half)
    start = pl.multiple_of(jnp.where(last, 32, 0), 16)
    fetch_edges = [
        pltpu.make_async_copy(
            layers_hbm.at[:, :, pl.ds(start, 16), pl.ds(side, 128)], near_edge.at[i], edge_sems.at[i]
        )
        for i, side in enumerate((left, right))
    ]
    for one in fetch_edges:
        one.start()
    high, odd = place()
    fetch.wait()
    lane = lanes(48)
    blocks = [target_ref[0, :, 128 * d : 128 * d + 128].astype(F32) for d in range(8)]
    zero = jnp.zeros((48, 128), F32)
    for d in range(8):
        left = blocks[d - 1] if d > 0 else zero
        right = blocks[d + 1] if d < 7 else zero
        mid = blocks[d]
        wide_ref[2 * d, :48] = pltpu.roll(jnp.where(lane >= 128 - HALO, left, mid), HALO, 1)
        wide_ref[2 * d + 1, :48] = pltpu.roll(jnp.where(lane < HALO, right, mid), 128 - 56, 1)
    lane = lanes(8)
    upper_half = lax.broadcasted_iota(I32, (8, 128), 0) < 4
    fetch_shifts.wait()
    extra = jnp.zeros((8, 128), F32)
    for layer in range(3):
        for part in range(2):
            extra = jnp.where(
                lane == 120 + 2 * layer + part, shifts_ref[0, part, layer].astype(F32), extra
            )
    for q in range(4):
        for d in range(8):
            for h in range(2):
                zl, x, c = home(d, h, q, high, odd)
                at = 2 * d + h
                main = wide_ref[at, TALL * q : TALL * q + 8]
                first = wide_ref[at, TALL * q + 8 : TALL * q + 16]
                second = wide_ref[at, TALL * q + 4 : TALL * q + 12]
                pieces = jnp.where(upper_half, pltpu.roll(first, 80, 1), pltpu.roll(second, 40, 1))
                chunk = jnp.where(lane < 80, main, jnp.where(lane < 120, pieces, extra))
                chunks_ref[(zl * 4 + x) * 2 + c] = chunk.astype(BF16)
    for one in fetch_edges:
        one.wait()
    for layer in range(3):
        for frame in range(3):
            a, b = near_edge[0, frame, layer], near_edge[1, frame, layer]
            cells = joined(a, b, there, amount)
            edge_out[layer, frame] = jnp.where(last, cells[HALO:], cells[:HALO])


def seen_kernel(layers_ref, seen_ref, tile_ref, tall_ref):
    block, half, q = my_tile()
    left, right, there, amount = window(block, half)
    start = q * TALL
    for layer in range(3):
        for frame in range(3):
            a = layers_ref[frame, layer, :, pl.ds(left, 128)]
            b = layers_ref[frame, layer, :, pl.ds(right, 128)]
            tall_ref[layer, frame, :HALO] = jnp.zeros((HALO, 128), F32)
            tall_ref[layer, frame, HALO : HALO + 48] = joined(a, b, there, amount)
            tall_ref[layer, frame, HALO + 48 :] = jnp.zeros((16, 128), F32)
            cells = tall_ref[layer, frame, pl.ds(start, 32), :]
            for d in range(SPAN):
                moved = pltpu.roll(cells, 128 - d, 1) if d else cells
                seen_ref[layer, d, frame] = moved
                if d == 16:
                    tile_ref[layer, frame] = moved[HALO : HALO + 16]


def edge_kernel(seen_in, edge_ref, seen_ref):
    _, _, q = my_tile()
    seen_ref[...] = seen_in[...]

    @pl.when((q == 0) | (q == 3))
    def _():
        start = jnp.where(q == 0, 0, HALO + TALL)
        for layer in range(3):
            for frame in range(3):
                cells = edge_ref[layer, frame]
                for d in range(SPAN):
                    moved = pltpu.roll(cells, 128 - d, 1) if d else cells
                    seen_ref[layer, d, frame, pl.ds(start, HALO), :] = moved


def view_kernel(
    recv_ref, seen_ref, far_out, near_out, s0_ref, s1_ref, s2_ref, s3_ref, s4_ref, s5_ref,
    image_ref, shift_ref, shift_smem, sem,
):
    sums = (s0_ref, s1_ref, s2_ref, s3_ref, s4_ref, s5_ref)
    shift_ref[...] = recv_ref[:, 0, :].astype(F32).astype(I32)
    copy = pltpu.make_async_copy(shift_ref, shift_smem, sem)
    copy.start()

    lane = lanes(8)
    upper_half = lax.broadcasted_iota(I32, (8, 128), 0) < 4
    for view in range(64):
        cells = recv_ref[view].astype(F32)
        image_ref[view, :8] = cells
        low = pltpu.roll(cells, 128 - 80, 1)
        high = pltpu.roll(pltpu.roll(cells, 128 - 40, 1), 4, 0)
        rest = jnp.where(lane < 40, low, high)
        image_ref[view, 8:] = jnp.where(upper_half, rest, 0.0)

    for ref in sums:
        ref[...] = jnp.zeros_like(ref)

    block, half, q = my_tile()
    column = block * 128 + half * WIDE - HALO + lanes(16)
    inside = (column >= 0) & (column < 1024)
    inside = inside & (lax.broadcasted_iota(I32, (16, 128), 0) < TALL)
    third = jnp.where(inside, 1.0 / 3.0, 0.0)
    copy.wait()

    def one_view(view, carry):
        rows = [shift_smem[view, 120 + 2 * layer] + HALO for layer in range(3)]
        cols = [shift_smem[view, 121 + 2 * layer] + HALO for layer in range(3)]
        s0, s1, s2 = (
            seen_ref[layer, cols[layer], :, pl.ds(rows[layer], 16), :] for layer in range(3)
        )
        p01 = s0 * s1
        whole = p01 * s2
        shown = (whole[0] + whole[1] + whole[2]) * third
        image = image_ref[view]
        for layer, others in enumerate((s1 * s2, s0 * s2, p01)):
            for which, factor in enumerate((image, shown)):
                sums[2 * layer + which][cols[layer], :, pl.ds(rows[layer], 16), :] += factor * others
        return carry

    lax.fori_loop(0, 64, one_view, 0, unroll=4)

    even = lax.rem(q, 2) == 0
    far_start = jnp.where(even, 0, HALO + TALL)
    near_start = jnp.where(even, HALO + TALL, 0)
    for layer in range(3):
        for frame in range(3):
            far_out[layer, frame] = folded(sums, layer, frame, far_start, HALO)
            near_out[layer, frame] = folded(sums, layer, frame, near_start, HALO)


def folded(sums, layer, frame, start, rows):
    sides = []
    for which, base in enumerate((-16, 48)):
        total = None
        for d in range(SPAN):
            amount = (d + base) % 128
            cells = sums[2 * layer + which][d, frame, pl.ds(start, rows), :]
            moved = pltpu.roll(cells, amount, 1) if amount else cells
            total = moved if total is None else total + moved
        sides.append(total)
    return jnp.where(lanes(rows) < WIDE, sides[0], sides[1])


def own_kernel(s0_ref, s1_ref, s2_ref, s3_ref, s4_ref, s5_ref, own_out):
    sums = (s0_ref, s1_ref, s2_ref, s3_ref, s4_ref, s5_ref)
    for layer in range(3):
        for frame in range(3):
            own_out[layer, frame] = folded(sums, layer, frame, HALO, 16)


def update_kernel(own_ref, far_ref, near_ref, tile_ref, out_ref, code_ref):
    lane = lanes(TALL)
    other = 1 - lax.axis_index("c")
    _, _, q = my_tile()
    even = lax.rem(q, 2) == 0
    for layer in range(3):
        for frame in range(3):
            own = own_ref[layer, frame]
            near = near_ref[other, layer, frame]
            far = far_ref[layer, frame]
            above = jnp.where(even, far, near)
            below = jnp.where(even, near, far)
            none = jnp.zeros((4, 128), F32)
            both = own[:TALL] + jnp.concatenate([above, none], axis=0)
            both = both + jnp.concatenate([none, below], axis=0)
            lower = pltpu.roll(both, WIDE, 1)
            value = tile_ref[layer, frame, :TALL] * (both + REGULAR) / (lower + REGULAR)
            scaled = (jnp.log2(value) + CODE_BASE) * CODE_STEPS + 0.5
            code_ref[frame * 3 + layer, :TALL] = jnp.clip(scaled, 0.0, 65535.0).astype(I32)
    for pair in range(2):
        parts = []
        for p in (pair, pair + 2):
            even = code_ref[2 * p, :TALL]
            odd = pltpu.roll(code_ref[2 * p + 1, :TALL], WIDE, 1)
            parts.append(jnp.where(lane < WIDE, even, odd))
        word = parts[0] + (parts[1] - 32768) * 65536
        for copy in range(8):
            out_ref[copy, TALL * pair : TALL * pair + TALL] = word
    code_ref[8, :6] = jnp.where(
        lanes(6) < WIDE, code_ref[8, :6], pltpu.roll(code_ref[8, 6:TALL], WIDE, 1)
    )
    word = code_ref[8, :REST] + (code_ref[8, REST : 2 * REST] - 32768) * 65536
    for copy in range(8):
        out_ref[copy, MAIN : MAIN + REST] = word
        out_ref[copy, MAIN + REST :] = jnp.zeros((5, 128), I32)


def dense_kernel(words_ref, out_ref):
    for zl in range(8):
        out_ref[MAIN * zl : MAIN * zl + MAIN] = words_ref[zl, :MAIN]
        at = 8 * MAIN + REST * zl
        out_ref[at : at + REST] = words_ref[zl, MAIN : MAIN + REST]


def decoded(code):
    return jnp.exp2(code.astype(F32) * (1.0 / CODE_STEPS) - CODE_BASE)


def spread_kernel(words_ref, out_ref, block_ref, sems):
    high, flip = place()

    def sent(d):
        columns = pl.ds(pl.multiple_of(d * 128, 128), 128)
        return pltpu.make_async_copy(block_ref.at[d], out_ref.at[:, :, :, columns], sems.at[d])

    def one(d, carry):
        for q in range(4):
            rows = slice(TALL * q, TALL * q + TALL)

            places = [home(d, half, q, high, flip) for half in range(2)]

            def halves(first, count, step):
                a, b = (
                    words_ref[x * 2 + c, pl.ds(first + step * zl, count), :] for zl, x, c in places
                )
                lane = lanes(count)
                even = jnp.where(lane < WIDE, a, pltpu.roll(b, WIDE, 1))
                return even, jnp.where(lane < WIDE, pltpu.roll(a, WIDE, 1), b)

            for side, word in enumerate(halves(0, MAIN, MAIN)):
                for p, code in ((0, word & 65535), (2, (word >> 16) + 32768)):
                    value = decoded(code)
                    for pair in range(2):
                        at = 2 * (p + pair) + side
                        block_ref[d, at // 3, at % 3, rows] = value[TALL * pair : TALL * pair + TALL]
            for side, word in enumerate(halves(8 * MAIN, REST, REST)):
                for part, code in ((0, word & 65535), (1, (word >> 16) + 32768)):
                    at = TALL * q + 6 * side + REST * part
                    block_ref[d, 2, 2, at : at + REST] = decoded(code)
        sent(d).start()
        return carry

    lax.fori_loop(0, 8, one, 0)
    for d in range(8):
        sent(d).wait()


def strip_pairs(first, step):
    def index(column, strip):
        at = strip // 4
        zl, x, c = home(column // 2, column % 2, strip % 4, at // 4, at % 2)
        return (((zl * 4 + x) * 2 + c) * 2 + at // 4) * 4 + at % 4

    pairs = []
    for column in range(16):
        for strip in range(first, 31, step):
            a, b = index(column, strip), index(column, strip + 1)
            pairs += [(a, b), (b, a)]
    return pairs


VMEM = pl.BlockSpec(memory_space=pltpu.VMEM)


VIEW_SCRATCH = [
    pltpu.VMEM((64, 16, 128), F32),
    pltpu.VMEM((64, 128), I32),
    pltpu.SMEM((64, 128), I32),
    pltpu.SemaphoreType.DMA,
]


def call(kernel, outs, ins, scratch=(), params=PARAMS, cost=None):
    return pl.pallas_call(
        kernel,
        out_shape=tuple(jax.ShapeDtypeStruct(*out) for out in outs),
        in_specs=ins,
        out_specs=(VMEM,) * len(outs),
        scratch_shapes=scratch,
        compiler_params=params,
        cost_estimate=cost,
    )


def body(layers, target, shifts):
    across = VIEW + ROW
    chunks, edge = call(
        pack_kernel,
        [((64, 8, 128), BF16), ((3, 3, HALO, 128), F32)],
        [pl.BlockSpec(memory_space=pltpu.HBM)] * 3,
        [
            pltpu.VMEM((1, 48, 1024), BF16),
            pltpu.SMEM((1, 2, 3), I32),
            pltpu.VMEM((2, 3, 3, 16, 128), BF16),
            pltpu.VMEM((16, 56, 128), F32),
            pltpu.SemaphoreType.DMA,
            pltpu.SemaphoreType.DMA,
            pltpu.SemaphoreType.DMA((2,)),
        ],
        WHOLE,
    )(target, shifts.transpose(0, 2, 1), layers)
    received = lax.all_to_all(chunks, VIEW, 0, 0)

    edge = lax.ppermute(edge, across, strip_pairs(3, 4))
    seen, tile = call(
        seen_kernel,
        [((3, SPAN, 3, 32, 128), F32), ((3, 3, 16, 128), F32)],
        [VMEM],
        [pltpu.VMEM((3, 3, 72, 128), F32)],
        cost=pl.CostEstimate(flops=1_000_000, bytes_accessed=3_600_000, transcendentals=0),
    )(layers)
    (seen,) = call(edge_kernel, [((3, SPAN, 3, 32, 128), F32)], [VMEM] * 2)(seen, edge)

    far, near, *sums = call(
        view_kernel,
        [((3, 3, HALO, 128), F32)] * 2 + [((SPAN, 3, 32, 128), F32)] * 6,
        [VMEM] * 2,
        VIEW_SCRATCH,
    )(received, seen)
    far = lax.ppermute(far, across, strip_pairs(1, 2))
    (own,) = call(
        own_kernel,
        [((3, 3, 16, 128), F32)],
        [VMEM] * 6,
        cost=pl.CostEstimate(flops=4_000_000, bytes_accessed=5_100_000, transcendentals=0),
    )(*sums)
    near = lax.all_gather(near, "c")

    (words,) = call(
        update_kernel,
        [((8, 32, 128), I32)],
        [VMEM] * 4,
        [pltpu.VMEM((9, 16, 128), I32)],
    )(own, far, near, tile)
    words = lax.all_to_all(words, "zl", 0, 0)
    (words,) = call(dense_kernel, [((8 * (MAIN + REST), 128), I32)], [VMEM])(words)
    words = lax.all_gather(words, ("x", "c"))

    return pl.pallas_call(
        spread_kernel,
        out_shape=jax.ShapeDtypeStruct((3, 3, 48, 1024), F32),
        in_specs=[VMEM],
        out_specs=pl.BlockSpec(memory_space=pl.ANY),
        scratch_shapes=[pltpu.VMEM((8, 3, 3, 48, 128), F32), pltpu.SemaphoreType.DMA((8,))],
        compiler_params=PARAMS,
    )(words)


def solution(mesh):
    fine = Mesh(mesh.devices.reshape(8, 4, 2, 2, 4), ("zl", "x", "c", "zh", "y"))
    placed = (P(None, None, ROW, None), P(VIEW, ROW, None), P(VIEW, None, None))
    return jax.shard_map(
        body, mesh=fine, in_specs=placed, out_specs=P(None, None, ROW, None), check_vma=False
    )
```

```python
import jax
import jax.numpy as jnp
from jax import lax
from jax.experimental import pallas as pl
from jax.experimental.pallas import tpu as pltpu
from jax.sharding import Mesh, PartitionSpec as P

HALO = 8
SPAN = 2 * HALO + 1
TALL = 12
WIDE = 64
REGULAR = 0.05
CODE_STEPS = 5041.0
CODE_BASE = 7.0
MAIN = 24
REST = 3
F32 = jnp.float32
BF16 = jnp.bfloat16
I32 = jnp.int32
VIEW = ("zl", "x", "c")
ROW = ("zh", "y")
PARAMS = pltpu.CompilerParams(vmem_limit_bytes=16 * 1024 * 1024)
WHOLE = pltpu.CompilerParams(vmem_limit_bytes=64 * 1024 * 1024)


def lanes(rows):
    return lax.broadcasted_iota(I32, (rows, 128), 1)


def home(block, half, q, high, odd):
    column = 2 * block + half
    at = column >> 2
    outer, inner = at + 4 * (at >> 1), at + 2
    zl = outer + ((q >> 1) ^ odd) * (inner - outer)
    return zl ^ (6 * high), column & 3, q & 1


def place():
    return lax.axis_index("zh"), lax.rem(lax.axis_index("y"), 2)


def my_tile():
    high, odd = place()
    zl = jnp.bitwise_xor(lax.axis_index("zl"), 6 * high)
    outer = (zl < 2) | (zl > 5)
    at = jnp.where(zl < 2, zl, jnp.where(zl > 5, zl - 4, zl - 2))
    column = 4 * at + lax.axis_index("x")
    q = 2 * jnp.where(outer, odd, 1 - odd) + lax.axis_index("c")
    return column >> 1, column & 1, q


def window(block, half):
    first = block - 1 + half
    left = pl.multiple_of(jnp.maximum(first, 0) * 128, 128)
    right = pl.multiple_of(jnp.minimum(first + 1, 7) * 128, 128)
    there = jnp.where(first >= 0, 1.0, 0.0), jnp.where(first < 7, 1.0, 0.0)
    return left, right, there, jnp.where(half == 0, 16, 80)


def joined(a, b, there, amount):
    lane = lanes(a.shape[0])
    a = a.astype(F32) * there[0]
    b = b.astype(F32) * there[1]
    return pltpu.roll(jnp.where(lane >= 128 - amount, a, b), amount, 1)


def pack_kernel(
    target_hbm, shifts_hbm, layers_hbm, chunks_ref, edge_out,
    target_ref, shifts_ref, near_edge, wide_ref, target_sem, shifts_sem, edge_sems,
):
    fetch_shifts = pltpu.make_async_copy(shifts_hbm, shifts_ref, shifts_sem)
    fetch_shifts.start()
    fetch = pltpu.make_async_copy(target_hbm, target_ref, target_sem)
    fetch.start()
    block, half, q = my_tile()
    last = q == 3
    left, right, there, amount = window(block, half)
    start = pl.multiple_of(jnp.where(last, 32, 0), 16)
    fetch_edges = [
        pltpu.make_async_copy(
            layers_hbm.at[:, :, pl.ds(start, 16), pl.ds(side, 128)], near_edge.at[i], edge_sems.at[i]
        )
        for i, side in enumerate((left, right))
    ]
    for one in fetch_edges:
        one.start()
    high, odd = place()
    fetch.wait()
    lane = lanes(48)
    blocks = [target_ref[0, :, 128 * d : 128 * d + 128].astype(F32) for d in range(8)]
    zero = jnp.zeros((48, 128), F32)
    for d in range(8):
        left = blocks[d - 1] if d > 0 else zero
        right = blocks[d + 1] if d < 7 else zero
        mid = blocks[d]
        wide_ref[2 * d, :48] = pltpu.roll(jnp.where(lane >= 128 - HALO, left, mid), HALO, 1)
        wide_ref[2 * d + 1, :48] = pltpu.roll(jnp.where(lane < HALO, right, mid), 128 - 56, 1)
    lane = lanes(8)
    upper_half = lax.broadcasted_iota(I32, (8, 128), 0) < 4
    fetch_shifts.wait()
    extra = jnp.zeros((8, 128), F32)
    for layer in range(3):
        for part in range(2):
            extra = jnp.where(
                lane == 120 + 2 * layer + part, shifts_ref[0, part, layer].astype(F32), extra
            )
    for q in range(4):
        for d in range(8):
            for h in range(2):
                zl, x, c = home(d, h, q, high, odd)
                at = 2 * d + h
                main = wide_ref[at, TALL * q : TALL * q + 8]
                first = wide_ref[at, TALL * q + 8 : TALL * q + 16]
                second = wide_ref[at, TALL * q + 4 : TALL * q + 12]
                pieces = jnp.where(upper_half, pltpu.roll(first, 80, 1), pltpu.roll(second, 40, 1))
                chunk = jnp.where(lane < 80, main, jnp.where(lane < 120, pieces, extra))
                chunks_ref[(zl * 4 + x) * 2 + c] = chunk.astype(BF16)
    for one in fetch_edges:
        one.wait()
    for layer in range(3):
        for frame in range(3):
            a, b = near_edge[0, frame, layer], near_edge[1, frame, layer]
            cells = joined(a, b, there, amount)
            edge_out[layer, frame] = jnp.where(last, cells[HALO:], cells[:HALO])


def seen_kernel(layers_ref, seen_ref, tile_ref, tall_ref):
    block, half, q = my_tile()
    left, right, there, amount = window(block, half)
    start = q * TALL
    for layer in range(3):
        for frame in range(3):
            a = layers_ref[frame, layer, :, pl.ds(left, 128)]
            b = layers_ref[frame, layer, :, pl.ds(right, 128)]
            tall_ref[layer, frame, :HALO] = jnp.zeros((HALO, 128), F32)
            tall_ref[layer, frame, HALO : HALO + 48] = joined(a, b, there, amount)
            tall_ref[layer, frame, HALO + 48 :] = jnp.zeros((16, 128), F32)
            cells = tall_ref[layer, frame, pl.ds(start, 32), :]
            for d in range(SPAN):
                moved = pltpu.roll(cells, 128 - d, 1) if d else cells
                seen_ref[layer, d, frame] = moved
                if d == 16:
                    tile_ref[layer, frame] = moved[HALO : HALO + 16]


def edge_kernel(seen_in, edge_ref, seen_ref):
    _, _, q = my_tile()
    seen_ref[...] = seen_in[...]

    @pl.when((q == 0) | (q == 3))
    def _():
        start = jnp.where(q == 0, 0, HALO + TALL)
        for layer in range(3):
            for frame in range(3):
                cells = edge_ref[layer, frame]
                for d in range(SPAN):
                    moved = pltpu.roll(cells, 128 - d, 1) if d else cells
                    seen_ref[layer, d, frame, pl.ds(start, HALO), :] = moved


def view_kernel(
    recv_ref, seen_ref, far_out, near_out, s0_ref, s1_ref, s2_ref, s3_ref, s4_ref, s5_ref,
    image_ref, shift_ref, shift_smem, sem,
):
    sums = (s0_ref, s1_ref, s2_ref, s3_ref, s4_ref, s5_ref)
    shift_ref[...] = recv_ref[:, 0, :].astype(F32).astype(I32)
    copy = pltpu.make_async_copy(shift_ref, shift_smem, sem)
    copy.start()

    lane = lanes(8)
    upper_half = lax.broadcasted_iota(I32, (8, 128), 0) < 4
    for view in range(64):
        cells = recv_ref[view].astype(F32)
        image_ref[view, :8] = cells
        low = pltpu.roll(cells, 128 - 80, 1)
        high = pltpu.roll(pltpu.roll(cells, 128 - 40, 1), 4, 0)
        rest = jnp.where(lane < 40, low, high)
        image_ref[view, 8:] = jnp.where(upper_half, rest, 0.0)

    for ref in sums:
        ref[...] = jnp.zeros_like(ref)

    block, half, q = my_tile()
    column = block * 128 + half * WIDE - HALO + lanes(16)
    inside = (column >= 0) & (column < 1024)
    inside = inside & (lax.broadcasted_iota(I32, (16, 128), 0) < TALL)
    third = jnp.where(inside, 1.0 / 3.0, 0.0)
    copy.wait()

    def one_view(view, carry):
        rows = [shift_smem[view, 120 + 2 * layer] + HALO for layer in range(3)]
        cols = [shift_smem[view, 121 + 2 * layer] + HALO for layer in range(3)]
        s0, s1, s2 = (
            seen_ref[layer, cols[layer], :, pl.ds(rows[layer], 16), :] for layer in range(3)
        )
        p01 = s0 * s1
        whole = p01 * s2
        shown = (whole[0] + whole[1] + whole[2]) * third
        image = image_ref[view]
        for layer, others in enumerate((s1 * s2, s0 * s2, p01)):
            for which, factor in enumerate((image, shown)):
                sums[2 * layer + which][cols[layer], :, pl.ds(rows[layer], 16), :] += factor * others
        return carry

    lax.fori_loop(0, 64, one_view, 0, unroll=4)

    even = lax.rem(q, 2) == 0
    far_start = jnp.where(even, 0, HALO + TALL)
    near_start = jnp.where(even, HALO + TALL, 0)
    for layer in range(3):
        for frame in range(3):
            far_out[layer, frame] = folded(sums, layer, frame, far_start, HALO)
            near_out[layer, frame] = folded(sums, layer, frame, near_start, HALO)


def folded(sums, layer, frame, start, rows):
    sides = []
    for which, base in enumerate((-16, 48)):
        total = None
        for d in range(SPAN):
            amount = (d + base) % 128
            cells = sums[2 * layer + which][d, frame, pl.ds(start, rows), :]
            moved = pltpu.roll(cells, amount, 1) if amount else cells
            total = moved if total is None else total + moved
        sides.append(total)
    return jnp.where(lanes(rows) < WIDE, sides[0], sides[1])


def own_kernel(s0_ref, s1_ref, s2_ref, s3_ref, s4_ref, s5_ref, own_out):
    sums = (s0_ref, s1_ref, s2_ref, s3_ref, s4_ref, s5_ref)
    for layer in range(3):
        for frame in range(3):
            own_out[layer, frame] = folded(sums, layer, frame, HALO, 16)


def update_kernel(own_ref, far_ref, near_ref, tile_ref, out_ref, code_ref):
    lane = lanes(TALL)
    other = 1 - lax.axis_index("c")
    _, _, q = my_tile()
    even = lax.rem(q, 2) == 0
    for layer in range(3):
        for frame in range(3):
            own = own_ref[layer, frame]
            near = near_ref[other, layer, frame]
            far = far_ref[layer, frame]
            above = jnp.where(even, far, near)
            below = jnp.where(even, near, far)
            none = jnp.zeros((4, 128), F32)
            both = own[:TALL] + jnp.concatenate([above, none], axis=0)
            both = both + jnp.concatenate([none, below], axis=0)
            lower = pltpu.roll(both, WIDE, 1)
            value = tile_ref[layer, frame, :TALL] * (both + REGULAR) / (lower + REGULAR)
            scaled = (jnp.log2(value) + CODE_BASE) * CODE_STEPS + 0.5
            code_ref[frame * 3 + layer, :TALL] = jnp.clip(scaled, 0.0, 65535.0).astype(I32)
    for pair in range(2):
        parts = []
        for p in (pair, pair + 2):
            even = code_ref[2 * p, :TALL]
            odd = pltpu.roll(code_ref[2 * p + 1, :TALL], WIDE, 1)
            parts.append(jnp.where(lane < WIDE, even, odd))
        word = parts[0] + (parts[1] - 32768) * 65536
        for copy in range(8):
            out_ref[copy, TALL * pair : TALL * pair + TALL] = word
    code_ref[8, :6] = jnp.where(
        lanes(6) < WIDE, code_ref[8, :6], pltpu.roll(code_ref[8, 6:TALL], WIDE, 1)
    )
    word = code_ref[8, :REST] + (code_ref[8, REST : 2 * REST] - 32768) * 65536
    for copy in range(8):
        out_ref[copy, MAIN : MAIN + REST] = word
        out_ref[copy, MAIN + REST :] = jnp.zeros((5, 128), I32)


def dense_kernel(words_ref, out_ref):
    for zl in range(8):
        main = words_ref[zl, :MAIN]
        rest = words_ref[zl, MAIN : MAIN + REST]
        at = 8 * MAIN + REST * zl
        for copy in range(4):
            out_ref[copy, MAIN * zl : MAIN * zl + MAIN] = main
            out_ref[copy, at : at + REST] = rest


def decoded(code):
    return jnp.exp2(code.astype(F32) * (1.0 / CODE_STEPS) - CODE_BASE)


def spread_kernel(words_ref, out_ref, block_ref, sems):
    high, flip = place()

    def sent(d):
        columns = pl.ds(pl.multiple_of(d * 128, 128), 128)
        return pltpu.make_async_copy(block_ref.at[d], out_ref.at[:, :, :, columns], sems.at[d])

    def one(d, carry):
        for q in range(4):
            rows = slice(TALL * q, TALL * q + TALL)

            places = [home(d, half, q, high, flip) for half in range(2)]

            def halves(first, count, step):
                a, b = (
                    words_ref[c, x, pl.ds(first + step * zl, count), :] for zl, x, c in places
                )
                lane = lanes(count)
                even = jnp.where(lane < WIDE, a, pltpu.roll(b, WIDE, 1))
                return even, jnp.where(lane < WIDE, pltpu.roll(a, WIDE, 1), b)

            for side, word in enumerate(halves(0, MAIN, MAIN)):
                for p, code in ((0, word & 65535), (2, (word >> 16) + 32768)):
                    value = decoded(code)
                    for pair in range(2):
                        at = 2 * (p + pair) + side
                        block_ref[d, at // 3, at % 3, rows] = value[TALL * pair : TALL * pair + TALL]
            for side, word in enumerate(halves(8 * MAIN, REST, REST)):
                for part, code in ((0, word & 65535), (1, (word >> 16) + 32768)):
                    at = TALL * q + 6 * side + REST * part
                    block_ref[d, 2, 2, at : at + REST] = decoded(code)
        sent(d).start()
        return carry

    lax.fori_loop(0, 8, one, 0)
    for d in range(8):
        sent(d).wait()


def strip_pairs(first, step):
    def index(column, strip):
        at = strip // 4
        zl, x, c = home(column // 2, column % 2, strip % 4, at // 4, at % 2)
        return (((zl * 4 + x) * 2 + c) * 2 + at // 4) * 4 + at % 4

    pairs = []
    for column in range(16):
        for strip in range(first, 31, step):
            a, b = index(column, strip), index(column, strip + 1)
            pairs += [(a, b), (b, a)]
    return pairs


VMEM = pl.BlockSpec(memory_space=pltpu.VMEM)


VIEW_SCRATCH = [
    pltpu.VMEM((64, 16, 128), F32),
    pltpu.VMEM((64, 128), I32),
    pltpu.SMEM((64, 128), I32),
    pltpu.SemaphoreType.DMA,
]


def call(kernel, outs, ins, scratch=(), params=PARAMS, cost=None):
    return pl.pallas_call(
        kernel,
        out_shape=tuple(jax.ShapeDtypeStruct(*out) for out in outs),
        in_specs=ins,
        out_specs=(VMEM,) * len(outs),
        scratch_shapes=scratch,
        compiler_params=params,
        cost_estimate=cost,
    )


def body(layers, target, shifts):
    across = VIEW + ROW
    chunks, edge = call(
        pack_kernel,
        [((64, 8, 128), BF16), ((3, 3, HALO, 128), F32)],
        [pl.BlockSpec(memory_space=pltpu.HBM)] * 3,
        [
            pltpu.VMEM((1, 48, 1024), BF16),
            pltpu.SMEM((1, 2, 3), I32),
            pltpu.VMEM((2, 3, 3, 16, 128), BF16),
            pltpu.VMEM((16, 56, 128), F32),
            pltpu.SemaphoreType.DMA,
            pltpu.SemaphoreType.DMA,
            pltpu.SemaphoreType.DMA((2,)),
        ],
        WHOLE,
    )(target, shifts.transpose(0, 2, 1), layers)
    received = lax.all_to_all(chunks, VIEW, 0, 0)

    edge = lax.ppermute(edge, across, strip_pairs(3, 4))
    seen, tile = call(
        seen_kernel,
        [((3, SPAN, 3, 32, 128), F32), ((3, 3, 16, 128), F32)],
        [VMEM],
        [pltpu.VMEM((3, 3, 72, 128), F32)],
        cost=pl.CostEstimate(flops=1_000_000, bytes_accessed=3_600_000, transcendentals=0),
    )(layers)
    (seen,) = call(edge_kernel, [((3, SPAN, 3, 32, 128), F32)], [VMEM] * 2)(seen, edge)

    far, near, *sums = call(
        view_kernel,
        [((3, 3, HALO, 128), F32)] * 2 + [((SPAN, 3, 32, 128), F32)] * 6,
        [VMEM] * 2,
        VIEW_SCRATCH,
    )(received, seen)
    far = lax.ppermute(far, across, strip_pairs(1, 2))
    (own,) = call(
        own_kernel,
        [((3, 3, 16, 128), F32)],
        [VMEM] * 6,
        cost=pl.CostEstimate(flops=4_000_000, bytes_accessed=5_100_000, transcendentals=0),
    )(*sums)
    near = lax.all_gather(near, "c")

    (words,) = call(
        update_kernel,
        [((8, 32, 128), I32)],
        [VMEM] * 4,
        [pltpu.VMEM((9, 16, 128), I32)],
    )(own, far, near, tile)
    words = lax.all_to_all(words, "zl", 0, 0)
    (words,) = call(dense_kernel, [((4, 8 * (MAIN + REST), 128), I32)], [VMEM])(words)
    words = lax.all_to_all(words, "x", 0, 0)
    words = lax.all_gather(words, "c")

    return pl.pallas_call(
        spread_kernel,
        out_shape=jax.ShapeDtypeStruct((3, 3, 48, 1024), F32),
        in_specs=[VMEM],
        out_specs=pl.BlockSpec(memory_space=pl.ANY),
        scratch_shapes=[pltpu.VMEM((8, 3, 3, 48, 128), F32), pltpu.SemaphoreType.DMA((8,))],
        compiler_params=PARAMS,
    )(words)


def solution(mesh):
    fine = Mesh(mesh.devices.reshape(8, 4, 2, 2, 4), ("zl", "x", "c", "zh", "y"))
    placed = (P(None, None, ROW, None), P(VIEW, ROW, None), P(VIEW, None, None))
    return jax.shard_map(
        body, mesh=fine, in_specs=placed, out_specs=P(None, None, ROW, None), check_vma=False
    )
```

```python
import jax
import jax.numpy as jnp
from jax import lax
from jax.experimental import pallas as pl
from jax.experimental.pallas import tpu as pltpu
from jax.sharding import Mesh, PartitionSpec as P

HALO = 8
SPAN = 2 * HALO + 1
TALL = 12
WIDE = 64
REGULAR = 0.05
CODE_STEPS = 5041.0
CODE_BASE = 7.0
MAIN = 24
REST = 3
F32 = jnp.float32
BF16 = jnp.bfloat16
I32 = jnp.int32
VIEW = ("zl", "x", "c")
ROW = ("zh", "y")
PARAMS = pltpu.CompilerParams(vmem_limit_bytes=16 * 1024 * 1024)
WHOLE = pltpu.CompilerParams(vmem_limit_bytes=64 * 1024 * 1024)


def lanes(rows):
    return lax.broadcasted_iota(I32, (rows, 128), 1)


def home(block, half, q, high, odd):
    column = 2 * block + half
    at = column >> 2
    outer, inner = at + 4 * (at >> 1), at + 2
    zl = outer + ((q >> 1) ^ odd) * (inner - outer)
    return zl ^ (6 * high), column & 3, q & 1


def place():
    return lax.axis_index("zh"), lax.rem(lax.axis_index("y"), 2)


def my_tile():
    high, odd = place()
    zl = jnp.bitwise_xor(lax.axis_index("zl"), 6 * high)
    outer = (zl < 2) | (zl > 5)
    at = jnp.where(zl < 2, zl, jnp.where(zl > 5, zl - 4, zl - 2))
    column = 4 * at + lax.axis_index("x")
    q = 2 * jnp.where(outer, odd, 1 - odd) + lax.axis_index("c")
    return column >> 1, column & 1, q


def window(block, half):
    first = block - 1 + half
    left = pl.multiple_of(jnp.maximum(first, 0) * 128, 128)
    right = pl.multiple_of(jnp.minimum(first + 1, 7) * 128, 128)
    there = jnp.where(first >= 0, 1.0, 0.0), jnp.where(first < 7, 1.0, 0.0)
    return left, right, there, jnp.where(half == 0, 16, 80)


def joined(a, b, there, amount):
    lane = lanes(a.shape[0])
    a = a.astype(F32) * there[0]
    b = b.astype(F32) * there[1]
    return pltpu.roll(jnp.where(lane >= 128 - amount, a, b), amount, 1)


def pack_kernel(
    target_hbm, shifts_hbm, layers_hbm, chunks_ref, edge_out,
    target_ref, shifts_ref, near_edge, wide_ref, target_sem, shifts_sem, edge_sems,
):
    fetch_shifts = pltpu.make_async_copy(shifts_hbm, shifts_ref, shifts_sem)
    fetch_shifts.start()
    fetch = pltpu.make_async_copy(target_hbm, target_ref, target_sem)
    fetch.start()
    block, half, q = my_tile()
    last = q == 3
    left, right, there, amount = window(block, half)
    start = pl.multiple_of(jnp.where(last, 32, 0), 16)
    fetch_edges = [
        pltpu.make_async_copy(
            layers_hbm.at[:, :, pl.ds(start, 16), pl.ds(side, 128)], near_edge.at[i], edge_sems.at[i]
        )
        for i, side in enumerate((left, right))
    ]
    for one in fetch_edges:
        one.start()
    high, odd = place()
    fetch.wait()
    lane = lanes(48)
    blocks = [target_ref[0, :, 128 * d : 128 * d + 128].astype(F32) for d in range(8)]
    zero = jnp.zeros((48, 128), F32)
    for d in range(8):
        left = blocks[d - 1] if d > 0 else zero
        right = blocks[d + 1] if d < 7 else zero
        mid = blocks[d]
        wide_ref[2 * d, :48] = pltpu.roll(jnp.where(lane >= 128 - HALO, left, mid), HALO, 1)
        wide_ref[2 * d + 1, :48] = pltpu.roll(jnp.where(lane < HALO, right, mid), 128 - 56, 1)
    lane = lanes(8)
    upper_half = lax.broadcasted_iota(I32, (8, 128), 0) < 4
    fetch_shifts.wait()
    extra = jnp.zeros((8, 128), F32)
    for layer in range(3):
        for part in range(2):
            extra = jnp.where(
                lane == 120 + 2 * layer + part, shifts_ref[0, part, layer].astype(F32), extra
            )
    for q in range(4):
        for d in range(8):
            for h in range(2):
                zl, x, c = home(d, h, q, high, odd)
                at = 2 * d + h
                main = wide_ref[at, TALL * q : TALL * q + 8]
                first = wide_ref[at, TALL * q + 8 : TALL * q + 16]
                second = wide_ref[at, TALL * q + 4 : TALL * q + 12]
                pieces = jnp.where(upper_half, pltpu.roll(first, 80, 1), pltpu.roll(second, 40, 1))
                chunk = jnp.where(lane < 80, main, jnp.where(lane < 120, pieces, extra))
                chunks_ref[(zl * 4 + x) * 2 + c] = chunk.astype(BF16)
    for one in fetch_edges:
        one.wait()
    for layer in range(3):
        for frame in range(3):
            a, b = near_edge[0, frame, layer], near_edge[1, frame, layer]
            cells = joined(a, b, there, amount)
            edge_out[layer, frame] = jnp.where(last, cells[HALO:], cells[:HALO])


def seen_kernel(layers_ref, seen_ref, tile_ref, tall_ref):
    block, half, q = my_tile()
    left, right, there, amount = window(block, half)
    start = q * TALL
    for layer in range(3):
        for frame in range(3):
            a = layers_ref[frame, layer, :, pl.ds(left, 128)]
            b = layers_ref[frame, layer, :, pl.ds(right, 128)]
            tall_ref[layer, frame, :HALO] = jnp.zeros((HALO, 128), F32)
            tall_ref[layer, frame, HALO : HALO + 48] = joined(a, b, there, amount)
            tall_ref[layer, frame, HALO + 48 :] = jnp.zeros((16, 128), F32)
            cells = tall_ref[layer, frame, pl.ds(start, 32), :]
            for d in range(SPAN):
                moved = pltpu.roll(cells, 128 - d, 1) if d else cells
                seen_ref[layer, d, frame] = moved
                if d == 16:
                    tile_ref[layer, frame] = moved[HALO : HALO + 16]


def edge_kernel(seen_in, edge_ref, seen_ref):
    _, _, q = my_tile()
    seen_ref[...] = seen_in[...]

    @pl.when((q == 0) | (q == 3))
    def _():
        start = jnp.where(q == 0, 0, HALO + TALL)
        for layer in range(3):
            for frame in range(3):
                cells = edge_ref[layer, frame]
                for d in range(SPAN):
                    moved = pltpu.roll(cells, 128 - d, 1) if d else cells
                    seen_ref[layer, d, frame, pl.ds(start, HALO), :] = moved


def view_kernel(
    recv_ref, seen_ref, far_out, s0_ref, s1_ref, s2_ref, s3_ref, s4_ref, s5_ref,
    image_ref, shift_ref, shift_smem, sem,
):
    sums = (s0_ref, s1_ref, s2_ref, s3_ref, s4_ref, s5_ref)
    row = lax.broadcasted_iota(I32, (16, 128), 0)
    pick = jnp.where(lanes(16) == 120 + row, 1.0, 0.0).astype(BF16)
    moved = lax.dot_general(
        pick, recv_ref[:, 0, :], (((1,), (1,)), ((), ())), preferred_element_type=F32
    )
    shift_ref[...] = jnp.zeros((8, 128), I32)
    shift_ref[:, :64] = moved[:8].astype(I32)
    copy = pltpu.make_async_copy(shift_ref, shift_smem, sem)
    copy.start()

    lane = lanes(8)
    upper_half = lax.broadcasted_iota(I32, (8, 128), 0) < 4
    for view in range(64):
        cells = recv_ref[view].astype(F32)
        image_ref[view, :8] = cells
        low = pltpu.roll(cells, 128 - 80, 1)
        high = pltpu.roll(pltpu.roll(cells, 128 - 40, 1), 4, 0)
        rest = jnp.where(lane < 40, low, high)
        image_ref[view, 8:] = jnp.where(upper_half, rest, 0.0)

    for ref in sums:
        ref[...] = jnp.zeros_like(ref)

    block, half, q = my_tile()
    column = block * 128 + half * WIDE - HALO + lanes(16)
    inside = (column >= 0) & (column < 1024)
    inside = inside & (lax.broadcasted_iota(I32, (16, 128), 0) < TALL)
    third = jnp.where(inside, 1.0 / 3.0, 0.0)
    copy.wait()

    def one_view(view, carry):
        rows = [shift_smem[2 * layer, view] + HALO for layer in range(3)]
        cols = [shift_smem[2 * layer + 1, view] + HALO for layer in range(3)]
        s0, s1, s2 = (
            seen_ref[layer, cols[layer], :, pl.ds(rows[layer], 16), :] for layer in range(3)
        )
        p01 = s0 * s1
        whole = p01 * s2
        shown = (whole[0] + whole[1] + whole[2]) * third
        image = image_ref[view]
        for layer, others in enumerate((s1 * s2, s0 * s2, p01)):
            for which, factor in enumerate((image, shown)):
                sums[2 * layer + which][cols[layer], :, pl.ds(rows[layer], 16), :] += factor * others
        return carry

    lax.fori_loop(0, 64, one_view, 0, unroll=4)

    start = jnp.where(lax.rem(q, 2) == 0, 0, HALO + TALL)
    for layer in range(3):
        for frame in range(3):
            far_out[layer, frame] = folded(sums, layer, frame, start, HALO)


def folded(sums, layer, frame, start, rows):
    sides = []
    for which, base in enumerate((-16, 48)):
        total = None
        for d in range(SPAN):
            amount = (d + base) % 128
            cells = sums[2 * layer + which][d, frame, pl.ds(start, rows), :]
            moved = pltpu.roll(cells, amount, 1) if amount else cells
            total = moved if total is None else total + moved
        sides.append(total)
    return jnp.where(lanes(rows) < WIDE, sides[0], sides[1])


def fold_kernel(s0_ref, s1_ref, s2_ref, s3_ref, s4_ref, s5_ref, near_out, own_out):
    sums = (s0_ref, s1_ref, s2_ref, s3_ref, s4_ref, s5_ref)
    _, _, q = my_tile()
    start = jnp.where(lax.rem(q, 2) == 0, HALO + TALL, 0)
    for layer in range(3):
        for frame in range(3):
            near_out[layer, frame] = folded(sums, layer, frame, start, HALO)
            own_out[layer, frame] = folded(sums, layer, frame, HALO, 16)


def update_kernel(own_ref, far_ref, near_ref, tile_ref, out_ref, code_ref):
    lane = lanes(TALL)
    other = 1 - lax.axis_index("c")
    _, _, q = my_tile()
    even = lax.rem(q, 2) == 0
    for layer in range(3):
        for frame in range(3):
            own = own_ref[layer, frame]
            near = near_ref[other, layer, frame]
            far = far_ref[layer, frame]
            above = jnp.where(even, far, near)
            below = jnp.where(even, near, far)
            none = jnp.zeros((4, 128), F32)
            both = own[:TALL] + jnp.concatenate([above, none], axis=0)
            both = both + jnp.concatenate([none, below], axis=0)
            lower = pltpu.roll(both, WIDE, 1)
            value = tile_ref[layer, frame, :TALL] * (both + REGULAR) / (lower + REGULAR)
            scaled = (jnp.log2(value) + CODE_BASE) * CODE_STEPS + 0.5
            code_ref[frame * 3 + layer, :TALL] = jnp.clip(scaled, 0.0, 65535.0).astype(I32)
    for pair in range(2):
        parts = []
        for p in (pair, pair + 2):
            even = code_ref[2 * p, :TALL]
            odd = pltpu.roll(code_ref[2 * p + 1, :TALL], WIDE, 1)
            parts.append(jnp.where(lane < WIDE, even, odd))
        word = parts[0] + (parts[1] - 32768) * 65536
        for copy in range(8):
            out_ref[copy, TALL * pair : TALL * pair + TALL] = word
    code_ref[8, :6] = jnp.where(
        lanes(6) < WIDE, code_ref[8, :6], pltpu.roll(code_ref[8, 6:TALL], WIDE, 1)
    )
    word = code_ref[8, :REST] + (code_ref[8, REST : 2 * REST] - 32768) * 65536
    for copy in range(8):
        out_ref[copy, MAIN : MAIN + REST] = word
        out_ref[copy, MAIN + REST :] = jnp.zeros((5, 128), I32)


def dense_kernel(words_ref, out_ref):
    for zl in range(8):
        main = words_ref[zl, :MAIN]
        rest = words_ref[zl, MAIN : MAIN + REST]
        at = 8 * MAIN + REST * zl
        for copy in range(4):
            out_ref[copy, MAIN * zl : MAIN * zl + MAIN] = main
            out_ref[copy, at : at + REST] = rest


def decoded(code):
    return jnp.exp2(code.astype(F32) * (1.0 / CODE_STEPS) - CODE_BASE)


def spread_kernel(words_ref, out_ref, block_ref, sems):
    high, flip = place()

    def sent(d):
        columns = pl.ds(pl.multiple_of(d * 128, 128), 128)
        return pltpu.make_async_copy(block_ref.at[d], out_ref.at[:, :, :, columns], sems.at[d])

    def one(d, carry):
        for q in range(4):
            rows = slice(TALL * q, TALL * q + TALL)

            places = [home(d, half, q, high, flip) for half in range(2)]

            def halves(first, count, step):
                a, b = (
                    words_ref[c, x, pl.ds(first + step * zl, count), :] for zl, x, c in places
                )
                lane = lanes(count)
                even = jnp.where(lane < WIDE, a, pltpu.roll(b, WIDE, 1))
                return even, jnp.where(lane < WIDE, pltpu.roll(a, WIDE, 1), b)

            for side, word in enumerate(halves(0, MAIN, MAIN)):
                for p, code in ((0, word & 65535), (2, (word >> 16) + 32768)):
                    value = decoded(code)
                    for pair in range(2):
                        at = 2 * (p + pair) + side
                        block_ref[d, at // 3, at % 3, rows] = value[TALL * pair : TALL * pair + TALL]
            for side, word in enumerate(halves(8 * MAIN, REST, REST)):
                for part, code in ((0, word & 65535), (1, (word >> 16) + 32768)):
                    at = TALL * q + 6 * side + REST * part
                    block_ref[d, 2, 2, at : at + REST] = decoded(code)
        sent(d).start()
        return carry

    lax.fori_loop(0, 8, one, 0)
    for d in range(8):
        sent(d).wait()


def strip_pairs(first, step):
    def index(column, strip):
        at = strip // 4
        zl, x, c = home(column // 2, column % 2, strip % 4, at // 4, at % 2)
        return (((zl * 4 + x) * 2 + c) * 2 + at // 4) * 4 + at % 4

    pairs = []
    for column in range(16):
        for strip in range(first, 31, step):
            a, b = index(column, strip), index(column, strip + 1)
            pairs += [(a, b), (b, a)]
    return pairs


VMEM = pl.BlockSpec(memory_space=pltpu.VMEM)


VIEW_SCRATCH = [
    pltpu.VMEM((64, 16, 128), F32),
    pltpu.VMEM((8, 128), I32),
    pltpu.SMEM((8, 128), I32),
    pltpu.SemaphoreType.DMA,
]


def call(kernel, outs, ins, scratch=(), params=PARAMS, cost=None):
    return pl.pallas_call(
        kernel,
        out_shape=tuple(jax.ShapeDtypeStruct(*out) for out in outs),
        in_specs=ins,
        out_specs=(VMEM,) * len(outs),
        scratch_shapes=scratch,
        compiler_params=params,
        cost_estimate=cost,
    )


def body(layers, target, shifts):
    across = VIEW + ROW
    chunks, edge = call(
        pack_kernel,
        [((64, 8, 128), BF16), ((3, 3, HALO, 128), F32)],
        [pl.BlockSpec(memory_space=pltpu.HBM)] * 3,
        [
            pltpu.VMEM((1, 48, 1024), BF16),
            pltpu.SMEM((1, 2, 3), I32),
            pltpu.VMEM((2, 3, 3, 16, 128), BF16),
            pltpu.VMEM((16, 56, 128), F32),
            pltpu.SemaphoreType.DMA,
            pltpu.SemaphoreType.DMA,
            pltpu.SemaphoreType.DMA((2,)),
        ],
        WHOLE,
    )(target, shifts.transpose(0, 2, 1), layers)
    received = lax.all_to_all(chunks, VIEW, 0, 0)

    edge = lax.ppermute(edge, across, strip_pairs(3, 4))
    seen, tile = call(
        seen_kernel,
        [((3, SPAN, 3, 32, 128), F32), ((3, 3, 16, 128), F32)],
        [VMEM],
        [pltpu.VMEM((3, 3, 72, 128), F32)],
        cost=pl.CostEstimate(flops=1_000_000, bytes_accessed=3_600_000, transcendentals=0),
    )(layers)
    (seen,) = call(edge_kernel, [((3, SPAN, 3, 32, 128), F32)], [VMEM] * 2)(seen, edge)

    far, *sums = call(
        view_kernel,
        [((3, 3, HALO, 128), F32)] + [((SPAN, 3, 32, 128), F32)] * 6,
        [VMEM] * 2,
        VIEW_SCRATCH,
    )(received, seen)
    far = lax.ppermute(far, across, strip_pairs(1, 2))
    near, own = call(
        fold_kernel,
        [((3, 3, HALO, 128), F32), ((3, 3, 16, 128), F32)],
        [VMEM] * 6,
        cost=pl.CostEstimate(flops=4_000_000, bytes_accessed=5_100_000, transcendentals=0),
    )(*sums)
    near = lax.all_gather(near, "c")

    (words,) = call(
        update_kernel,
        [((8, 32, 128), I32)],
        [VMEM] * 4,
        [pltpu.VMEM((9, 16, 128), I32)],
    )(own, far, near, tile)
    words = lax.all_to_all(words, "zl", 0, 0)
    (words,) = call(dense_kernel, [((4, 8 * (MAIN + REST), 128), I32)], [VMEM])(words)
    words = lax.all_to_all(words, "x", 0, 0)
    words = lax.all_gather(words, "c")

    return pl.pallas_call(
        spread_kernel,
        out_shape=jax.ShapeDtypeStruct((3, 3, 48, 1024), F32),
        in_specs=[VMEM],
        out_specs=pl.BlockSpec(memory_space=pl.ANY),
        scratch_shapes=[pltpu.VMEM((8, 3, 3, 48, 128), F32), pltpu.SemaphoreType.DMA((8,))],
        compiler_params=PARAMS,
    )(words)


def solution(mesh):
    fine = Mesh(mesh.devices.reshape(8, 4, 2, 2, 4), ("zl", "x", "c", "zh", "y"))
    placed = (P(None, None, ROW, None), P(VIEW, ROW, None), P(VIEW, None, None))
    return jax.shard_map(
        body, mesh=fine, in_specs=placed, out_specs=P(None, None, ROW, None), check_vma=False
    )
```

```python
import jax
import jax.numpy as jnp
from jax import lax
from jax.experimental import pallas as pl
from jax.experimental.pallas import tpu as pltpu
from jax.sharding import Mesh, PartitionSpec as P

HALO = 8
SPAN = 2 * HALO + 1
TALL = 12
WIDE = 64
REGULAR = 0.05
CODE_STEPS = 5041.0
CODE_BASE = 7.0
MAIN = 24
REST = 3
F32 = jnp.float32
BF16 = jnp.bfloat16
I32 = jnp.int32
VIEW = ("zl", "x", "c")
ROW = ("zh", "y")
PARAMS = pltpu.CompilerParams(vmem_limit_bytes=16 * 1024 * 1024)
WHOLE = pltpu.CompilerParams(vmem_limit_bytes=64 * 1024 * 1024)


def lanes(rows):
    return lax.broadcasted_iota(I32, (rows, 128), 1)


def home(block, half, q, high, odd):
    column = 2 * block + half
    at = column >> 2
    outer, inner = at + 4 * (at >> 1), at + 2
    zl = outer + ((q >> 1) ^ odd) * (inner - outer)
    return zl ^ (6 * high), column & 3, q & 1


def place():
    return lax.axis_index("zh"), lax.rem(lax.axis_index("y"), 2)


def my_tile():
    high, odd = place()
    zl = jnp.bitwise_xor(lax.axis_index("zl"), 6 * high)
    outer = (zl < 2) | (zl > 5)
    at = jnp.where(zl < 2, zl, jnp.where(zl > 5, zl - 4, zl - 2))
    column = 4 * at + lax.axis_index("x")
    q = 2 * jnp.where(outer, odd, 1 - odd) + lax.axis_index("c")
    return column >> 1, column & 1, q


def window(block, half):
    first = block - 1 + half
    left = pl.multiple_of(jnp.maximum(first, 0) * 128, 128)
    right = pl.multiple_of(jnp.minimum(first + 1, 7) * 128, 128)
    there = jnp.where(first >= 0, 1.0, 0.0), jnp.where(first < 7, 1.0, 0.0)
    return left, right, there, jnp.where(half == 0, 16, 80)


def joined(a, b, there, amount):
    lane = lanes(a.shape[0])
    a = a.astype(F32) * there[0]
    b = b.astype(F32) * there[1]
    return pltpu.roll(jnp.where(lane >= 128 - amount, a, b), amount, 1)


def pack_kernel(
    target_hbm, shifts_hbm, layers_hbm, chunks_ref, edge_out,
    target_ref, shifts_ref, near_edge, wide_ref, target_sem, shifts_sem, edge_sems,
):
    fetch_shifts = pltpu.make_async_copy(shifts_hbm, shifts_ref, shifts_sem)
    fetch_shifts.start()
    fetch = pltpu.make_async_copy(target_hbm, target_ref, target_sem)
    fetch.start()
    block, half, q = my_tile()
    last = q == 3
    left, right, there, amount = window(block, half)
    start = pl.multiple_of(jnp.where(last, 32, 0), 16)
    fetch_edges = [
        pltpu.make_async_copy(
            layers_hbm.at[:, :, pl.ds(start, 16), pl.ds(side, 128)], near_edge.at[i], edge_sems.at[i]
        )
        for i, side in enumerate((left, right))
    ]
    for one in fetch_edges:
        one.start()
    high, odd = place()
    fetch.wait()
    lane = lanes(48)
    blocks = [target_ref[0, :, 128 * d : 128 * d + 128].astype(F32) for d in range(8)]
    zero = jnp.zeros((48, 128), F32)
    for d in range(8):
        left = blocks[d - 1] if d > 0 else zero
        right = blocks[d + 1] if d < 7 else zero
        mid = blocks[d]
        wide_ref[2 * d, :48] = pltpu.roll(jnp.where(lane >= 128 - HALO, left, mid), HALO, 1)
        wide_ref[2 * d + 1, :48] = pltpu.roll(jnp.where(lane < HALO, right, mid), 128 - 56, 1)
    lane = lanes(8)
    upper_half = lax.broadcasted_iota(I32, (8, 128), 0) < 4
    fetch_shifts.wait()
    extra = jnp.zeros((8, 128), F32)
    for layer in range(3):
        for part in range(2):
            extra = jnp.where(
                lane == 120 + 2 * layer + part, shifts_ref[0, part, layer].astype(F32), extra
            )
    for q in range(4):
        for d in range(8):
            for h in range(2):
                zl, x, c = home(d, h, q, high, odd)
                at = 2 * d + h
                main = wide_ref[at, TALL * q : TALL * q + 8]
                first = wide_ref[at, TALL * q + 8 : TALL * q + 16]
                second = wide_ref[at, TALL * q + 4 : TALL * q + 12]
                pieces = jnp.where(upper_half, pltpu.roll(first, 80, 1), pltpu.roll(second, 40, 1))
                chunk = jnp.where(lane < 80, main, jnp.where(lane < 120, pieces, extra))
                chunks_ref[(zl * 4 + x) * 2 + c] = chunk.astype(BF16)
    for one in fetch_edges:
        one.wait()
    for layer in range(3):
        for frame in range(3):
            a, b = near_edge[0, frame, layer], near_edge[1, frame, layer]
            cells = joined(a, b, there, amount)
            edge_out[layer, frame] = jnp.where(last, cells[HALO:], cells[:HALO])


def seen_kernel(layers_ref, seen_ref, tile_ref, tall_ref):
    block, half, q = my_tile()
    left, right, there, amount = window(block, half)
    start = q * TALL
    for layer in range(3):
        for frame in range(3):
            a = layers_ref[frame, layer, :, pl.ds(left, 128)]
            b = layers_ref[frame, layer, :, pl.ds(right, 128)]
            tall_ref[layer, frame, :HALO] = jnp.zeros((HALO, 128), F32)
            tall_ref[layer, frame, HALO : HALO + 48] = joined(a, b, there, amount)
            tall_ref[layer, frame, HALO + 48 :] = jnp.zeros((16, 128), F32)
            cells = tall_ref[layer, frame, pl.ds(start, 32), :]
            for d in range(SPAN):
                moved = pltpu.roll(cells, 128 - d, 1) if d else cells
                seen_ref[layer, d, frame] = moved
                if d == 16:
                    tile_ref[layer, frame] = moved[HALO : HALO + 16]


def edge_kernel(seen_in, edge_ref, seen_ref):
    _, _, q = my_tile()
    seen_ref[...] = seen_in[...]

    @pl.when((q == 0) | (q == 3))
    def _():
        start = jnp.where(q == 0, 0, HALO + TALL)
        for layer in range(3):
            for frame in range(3):
                cells = edge_ref[layer, frame]
                for d in range(SPAN):
                    moved = pltpu.roll(cells, 128 - d, 1) if d else cells
                    seen_ref[layer, d, frame, pl.ds(start, HALO), :] = moved


def view_kernel(
    recv_ref, seen_ref, far_out, s0_ref, s1_ref, s2_ref, s3_ref, s4_ref, s5_ref,
    image_ref, shift_ref, shift_smem, sem,
):
    sums = (s0_ref, s1_ref, s2_ref, s3_ref, s4_ref, s5_ref)
    row = lax.broadcasted_iota(I32, (16, 128), 0)
    pick = jnp.where(lanes(16) == 120 + row, 1.0, 0.0).astype(BF16)
    moved = lax.dot_general(
        pick, recv_ref[:, 0, :], (((1,), (1,)), ((), ())), preferred_element_type=F32
    )
    shift_ref[...] = jnp.zeros((8, 128), I32)
    shift_ref[:, :64] = moved[:8].astype(I32)
    copy = pltpu.make_async_copy(shift_ref, shift_smem, sem)
    copy.start()

    lane = lanes(8)
    upper_half = lax.broadcasted_iota(I32, (8, 128), 0) < 4
    for view in range(64):
        cells = recv_ref[view].astype(F32)
        image_ref[view, :8] = cells
        low = pltpu.roll(cells, 128 - 80, 1)
        high = pltpu.roll(pltpu.roll(cells, 128 - 40, 1), 4, 0)
        rest = jnp.where(lane < 40, low, high)
        image_ref[view, 8:] = jnp.where(upper_half, rest, 0.0)

    for ref in sums:
        ref[...] = jnp.zeros_like(ref)

    block, half, q = my_tile()
    column = block * 128 + half * WIDE - HALO + lanes(16)
    inside = (column >= 0) & (column < 1024)
    inside = inside & (lax.broadcasted_iota(I32, (16, 128), 0) < TALL)
    third = jnp.where(inside, 1.0 / 3.0, 0.0)
    copy.wait()

    def one_view(view, carry):
        rows = [shift_smem[2 * layer, view] + HALO for layer in range(3)]
        cols = [shift_smem[2 * layer + 1, view] + HALO for layer in range(3)]
        s0, s1, s2 = (
            seen_ref[layer, cols[layer], :, pl.ds(rows[layer], 16), :] for layer in range(3)
        )
        p01 = s0 * s1
        whole = p01 * s2
        shown = (whole[0] + whole[1] + whole[2]) * third
        image = image_ref[view]
        for layer, others in enumerate((s1 * s2, s0 * s2, p01)):
            for which, factor in enumerate((image, shown)):
                sums[2 * layer + which][cols[layer], :, pl.ds(rows[layer], 16), :] += factor * others
        return carry

    lax.fori_loop(0, 64, one_view, 0, unroll=4)

    start = jnp.where(lax.rem(q, 2) == 0, 0, HALO + TALL)
    for layer in range(3):
        for frame in range(3):
            far_out[layer, frame] = folded(sums, layer, frame, start, HALO)


def folded(sums, layer, frame, start, rows):
    sides = []
    for which, base in enumerate((-16, 48)):
        total = None
        for d in range(SPAN):
            amount = (d + base) % 128
            cells = sums[2 * layer + which][d, frame, pl.ds(start, rows), :]
            moved = pltpu.roll(cells, amount, 1) if amount else cells
            total = moved if total is None else total + moved
        sides.append(total)
    return jnp.where(lanes(rows) < WIDE, sides[0], sides[1])


def fold_kernel(s0_ref, s1_ref, s2_ref, s3_ref, s4_ref, s5_ref, near_out, own_out):
    sums = (s0_ref, s1_ref, s2_ref, s3_ref, s4_ref, s5_ref)
    _, _, q = my_tile()
    start = jnp.where(lax.rem(q, 2) == 0, HALO + TALL, 0)
    for layer in range(3):
        for frame in range(3):
            near_out[layer, frame] = folded(sums, layer, frame, start, HALO)
            own_out[layer, frame] = folded(sums, layer, frame, HALO, 16)


def update_kernel(own_ref, far_ref, near_ref, tile_ref, out_ref, code_ref):
    lane = lanes(TALL)
    other = 1 - lax.axis_index("c")
    _, _, q = my_tile()
    even = lax.rem(q, 2) == 0
    for layer in range(3):
        for frame in range(3):
            own = own_ref[layer, frame]
            near = near_ref[other, layer, frame]
            far = far_ref[layer, frame]
            above = jnp.where(even, far, near)
            below = jnp.where(even, near, far)
            none = jnp.zeros((4, 128), F32)
            both = own[:TALL] + jnp.concatenate([above, none], axis=0)
            both = both + jnp.concatenate([none, below], axis=0)
            lower = pltpu.roll(both, WIDE, 1)
            value = tile_ref[layer, frame, :TALL] * (both + REGULAR) / (lower + REGULAR)
            scaled = (jnp.log2(value) + CODE_BASE) * CODE_STEPS + 0.5
            code_ref[frame * 3 + layer, :TALL] = jnp.clip(scaled, 0.0, 65535.0).astype(I32)
    for pair in range(2):
        parts = []
        for p in (pair, pair + 2):
            even = code_ref[2 * p, :TALL]
            odd = pltpu.roll(code_ref[2 * p + 1, :TALL], WIDE, 1)
            parts.append(jnp.where(lane < WIDE, even, odd))
        word = parts[0] + (parts[1] - 32768) * 65536
        for copy in range(8):
            out_ref[copy, TALL * pair : TALL * pair + TALL] = word
    code_ref[8, :6] = jnp.where(
        lanes(6) < WIDE, code_ref[8, :6], pltpu.roll(code_ref[8, 6:TALL], WIDE, 1)
    )
    word = code_ref[8, :8] + (code_ref[8, REST : REST + 8] - 32768) * 65536
    for copy in range(8):
        out_ref[copy, MAIN : MAIN + 8] = word


def dense_kernel(words_ref, out_ref):
    for zl in range(8):
        main = words_ref[zl, :MAIN]
        rest = words_ref[zl, MAIN : MAIN + REST]
        for copy in range(4):
            out_ref[copy, REST * zl : REST * zl + REST] = rest
            out_ref[copy, 8 * REST + MAIN * zl : 8 * REST + MAIN * zl + MAIN] = main


def decoded(code):
    return jnp.exp2(code.astype(F32) * (1.0 / CODE_STEPS) - CODE_BASE)


def spread_kernel(words_ref, out_ref, block_ref, sems):
    high, flip = place()

    def sent(d):
        columns = pl.ds(pl.multiple_of(d * 128, 128), 128)
        return pltpu.make_async_copy(block_ref.at[d, :, :, :48], out_ref.at[:, :, :, columns], sems.at[d])

    def one(d, carry):
        for q in range(4):
            rows = slice(TALL * q, TALL * q + TALL)

            places = [home(d, half, q, high, flip) for half in range(2)]

            def halves(first, count, step):
                a, b = (
                    words_ref[c, x, pl.ds(first + step * zl, count), :] for zl, x, c in places
                )
                lane = lanes(count)
                even = jnp.where(lane < WIDE, a, pltpu.roll(b, WIDE, 1))
                return even, jnp.where(lane < WIDE, pltpu.roll(a, WIDE, 1), b)

            for side, word in enumerate(halves(8 * REST, MAIN, MAIN)):
                for p, code in ((0, word & 65535), (2, (word >> 16) + 32768)):
                    value = decoded(code)
                    for pair in range(2):
                        at = 2 * (p + pair) + side
                        block_ref[d, at // 3, at % 3, rows] = value[TALL * pair : TALL * pair + TALL]
            for side, word in enumerate(halves(0, REST, REST)):
                for part, code in ((0, word & 65535), (1, (word >> 16) + 32768)):
                    at = TALL * q + 6 * side + REST * part
                    block_ref[d, 2, 2, at : at + REST] = decoded(code)
        sent(d).start()
        return carry

    lax.fori_loop(0, 8, one, 0)
    for d in range(8):
        sent(d).wait()


def strip_pairs(first, step):
    def index(column, strip):
        at = strip // 4
        zl, x, c = home(column // 2, column % 2, strip % 4, at // 4, at % 2)
        return (((zl * 4 + x) * 2 + c) * 2 + at // 4) * 4 + at % 4

    pairs = []
    for column in range(16):
        for strip in range(first, 31, step):
            a, b = index(column, strip), index(column, strip + 1)
            pairs += [(a, b), (b, a)]
    return pairs


VMEM = pl.BlockSpec(memory_space=pltpu.VMEM)


VIEW_SCRATCH = [
    pltpu.VMEM((64, 16, 128), F32),
    pltpu.VMEM((8, 128), I32),
    pltpu.SMEM((8, 128), I32),
    pltpu.SemaphoreType.DMA,
]


def call(kernel, outs, ins, scratch=(), params=PARAMS, cost=None):
    return pl.pallas_call(
        kernel,
        out_shape=tuple(jax.ShapeDtypeStruct(*out) for out in outs),
        in_specs=ins,
        out_specs=(VMEM,) * len(outs),
        scratch_shapes=scratch,
        compiler_params=params,
        cost_estimate=cost,
    )


def body(layers, target, shifts):
    across = VIEW + ROW
    chunks, edge = call(
        pack_kernel,
        [((64, 8, 128), BF16), ((3, 3, HALO, 128), F32)],
        [pl.BlockSpec(memory_space=pltpu.HBM)] * 3,
        [
            pltpu.VMEM((1, 48, 1024), BF16),
            pltpu.SMEM((1, 2, 3), I32),
            pltpu.VMEM((2, 3, 3, 16, 128), BF16),
            pltpu.VMEM((16, 56, 128), F32),
            pltpu.SemaphoreType.DMA,
            pltpu.SemaphoreType.DMA,
            pltpu.SemaphoreType.DMA((2,)),
        ],
        WHOLE,
    )(target, shifts.transpose(0, 2, 1), layers)
    received = lax.all_to_all(chunks, VIEW, 0, 0)

    edge = lax.ppermute(edge, across, strip_pairs(3, 4))
    seen, tile = call(
        seen_kernel,
        [((3, SPAN, 3, 32, 128), F32), ((3, 3, 16, 128), F32)],
        [VMEM],
        [pltpu.VMEM((3, 3, 72, 128), F32)],
        cost=pl.CostEstimate(flops=1_000_000, bytes_accessed=3_600_000, transcendentals=0),
    )(layers)
    (seen,) = call(edge_kernel, [((3, SPAN, 3, 32, 128), F32)], [VMEM] * 2)(seen, edge)

    far, *sums = call(
        view_kernel,
        [((3, 3, HALO, 128), F32)] + [((SPAN, 3, 32, 128), F32)] * 6,
        [VMEM] * 2,
        VIEW_SCRATCH,
    )(received, seen)
    far = lax.ppermute(far, across, strip_pairs(1, 2))
    near, own = call(
        fold_kernel,
        [((3, 3, HALO, 128), F32), ((3, 3, 16, 128), F32)],
        [VMEM] * 6,
        cost=pl.CostEstimate(flops=4_000_000, bytes_accessed=5_100_000, transcendentals=0),
    )(*sums)
    near = lax.all_gather(near, "c")

    (words,) = call(
        update_kernel,
        [((8, 32, 128), I32)],
        [VMEM] * 4,
        [pltpu.VMEM((9, 16, 128), I32)],
    )(own, far, near, tile)
    words = lax.all_to_all(words, "zl", 0, 0)
    (words,) = call(dense_kernel, [((4, 8 * (MAIN + REST), 128), I32)], [VMEM])(words)
    words = lax.all_to_all(words, "x", 0, 0)
    words = lax.all_gather(words, "c")

    return pl.pallas_call(
        spread_kernel,
        out_shape=jax.ShapeDtypeStruct((3, 3, 48, 1024), F32),
        in_specs=[VMEM],
        out_specs=pl.BlockSpec(memory_space=pl.ANY),
        scratch_shapes=[pltpu.VMEM((8, 3, 3, 56, 128), F32), pltpu.SemaphoreType.DMA((8,))],
        compiler_params=PARAMS,
    )(words)


def solution(mesh):
    fine = Mesh(mesh.devices.reshape(8, 4, 2, 2, 4), ("zl", "x", "c", "zh", "y"))
    placed = (P(None, None, ROW, None), P(VIEW, ROW, None), P(VIEW, None, None))
    return jax.shard_map(
        body, mesh=fine, in_specs=placed, out_specs=P(None, None, ROW, None), check_vma=False
    )
```

```python
import jax
import jax.numpy as jnp
from jax import lax
from jax.experimental import pallas as pl
from jax.experimental.pallas import tpu as pltpu
from jax.sharding import Mesh, PartitionSpec as P

HALO = 8
SPAN = 2 * HALO + 1
TALL = 12
WIDE = 64
REGULAR = 0.05
CODE_STEPS = 5041.0
CODE_BASE = 7.0
MAIN = 24
REST = 3
F32 = jnp.float32
BF16 = jnp.bfloat16
I32 = jnp.int32
VIEW = ("zl", "x", "c")
ROW = ("zh", "y")
PARAMS = pltpu.CompilerParams(vmem_limit_bytes=16 * 1024 * 1024)
WHOLE = pltpu.CompilerParams(vmem_limit_bytes=64 * 1024 * 1024)


def lanes(rows):
    return lax.broadcasted_iota(I32, (rows, 128), 1)


def home(block, half, q, high, odd):
    column = 2 * block + half
    at = column >> 2
    outer, inner = at + 4 * (at >> 1), at + 2
    zl = outer + ((q >> 1) ^ odd) * (inner - outer)
    return zl ^ (6 * high), column & 3, q & 1


def place():
    return lax.axis_index("zh"), lax.rem(lax.axis_index("y"), 2)


def my_tile():
    high, odd = place()
    zl = jnp.bitwise_xor(lax.axis_index("zl"), 6 * high)
    outer = (zl < 2) | (zl > 5)
    at = jnp.where(zl < 2, zl, jnp.where(zl > 5, zl - 4, zl - 2))
    column = 4 * at + lax.axis_index("x")
    q = 2 * jnp.where(outer, odd, 1 - odd) + lax.axis_index("c")
    return column >> 1, column & 1, q


def window(block, half):
    first = block - 1 + half
    left = pl.multiple_of(jnp.maximum(first, 0) * 128, 128)
    right = pl.multiple_of(jnp.minimum(first + 1, 7) * 128, 128)
    there = jnp.where(first >= 0, 1.0, 0.0), jnp.where(first < 7, 1.0, 0.0)
    return left, right, there, jnp.where(half == 0, 16, 80)


def joined(a, b, there, amount):
    lane = lanes(a.shape[0])
    a = a.astype(F32) * there[0]
    b = b.astype(F32) * there[1]
    return pltpu.roll(jnp.where(lane >= 128 - amount, a, b), amount, 1)


def pack_kernel(
    target_hbm, shifts_hbm, layers_hbm, chunks_ref, edge_out,
    target_ref, shifts_ref, near_edge, wide_ref, target_sem, shifts_sem, edge_sems,
):
    fetch_shifts = pltpu.make_async_copy(shifts_hbm, shifts_ref, shifts_sem)
    fetch_shifts.start()
    fetch = pltpu.make_async_copy(target_hbm, target_ref, target_sem)
    fetch.start()
    block, half, q = my_tile()
    last = q == 3
    left, right, there, amount = window(block, half)
    start = pl.multiple_of(jnp.where(last, 32, 0), 16)
    fetch_edges = [
        pltpu.make_async_copy(
            layers_hbm.at[:, :, pl.ds(start, 16), pl.ds(side, 128)], near_edge.at[i], edge_sems.at[i]
        )
        for i, side in enumerate((left, right))
    ]
    for one in fetch_edges:
        one.start()
    high, odd = place()
    fetch.wait()
    lane = lanes(48)
    blocks = [target_ref[0, :, 128 * d : 128 * d + 128].astype(F32) for d in range(8)]
    zero = jnp.zeros((48, 128), F32)
    for d in range(8):
        left = blocks[d - 1] if d > 0 else zero
        right = blocks[d + 1] if d < 7 else zero
        mid = blocks[d]
        wide_ref[2 * d, :48] = pltpu.roll(jnp.where(lane >= 128 - HALO, left, mid), HALO, 1)
        wide_ref[2 * d + 1, :48] = pltpu.roll(jnp.where(lane < HALO, right, mid), 128 - 56, 1)
    lane = lanes(8)
    upper_half = lax.broadcasted_iota(I32, (8, 128), 0) < 4
    fetch_shifts.wait()
    extra = jnp.zeros((8, 128), F32)
    for layer in range(3):
        for part in range(2):
            extra = jnp.where(
                lane == 120 + 2 * layer + part, shifts_ref[0, part, layer].astype(F32), extra
            )
    def strip(at_q, carry):
        for d in range(8):
            for h in range(2):
                zl, x, c = home(d, h, at_q, high, odd)
                at = 2 * d + h
                main = wide_ref[at, pl.ds(TALL * at_q, 8), :]
                first = wide_ref[at, pl.ds(TALL * at_q + 8, 8), :]
                second = wide_ref[at, pl.ds(TALL * at_q + 4, 8), :]
                pieces = jnp.where(upper_half, pltpu.roll(first, 80, 1), pltpu.roll(second, 40, 1))
                chunk = jnp.where(lane < 80, main, jnp.where(lane < 120, pieces, extra))
                chunks_ref[(zl * 4 + x) * 2 + c] = chunk.astype(BF16)
        return carry

    lax.fori_loop(0, 4, strip, 0)
    for one in fetch_edges:
        one.wait()
    for layer in range(3):
        for frame in range(3):
            a, b = near_edge[0, frame, layer], near_edge[1, frame, layer]
            cells = joined(a, b, there, amount)
            edge_out[layer, frame] = jnp.where(last, cells[HALO:], cells[:HALO])


def seen_kernel(layers_ref, seen_ref, tile_ref, tall_ref):
    block, half, q = my_tile()
    left, right, there, amount = window(block, half)
    start = q * TALL
    for layer in range(3):
        for frame in range(3):
            a = layers_ref[frame, layer, :, pl.ds(left, 128)]
            b = layers_ref[frame, layer, :, pl.ds(right, 128)]
            tall_ref[layer, frame, :HALO] = jnp.zeros((HALO, 128), F32)
            tall_ref[layer, frame, HALO : HALO + 48] = joined(a, b, there, amount)
            tall_ref[layer, frame, HALO + 48 :] = jnp.zeros((16, 128), F32)
            cells = tall_ref[layer, frame, pl.ds(start, 32), :]
            for d in range(SPAN):
                moved = pltpu.roll(cells, 128 - d, 1) if d else cells
                seen_ref[layer, d, frame] = moved
                if d == 16:
                    tile_ref[layer, frame] = moved[HALO : HALO + 16]


def edge_kernel(seen_in, edge_ref, seen_ref):
    _, _, q = my_tile()
    seen_ref[...] = seen_in[...]

    @pl.when((q == 0) | (q == 3))
    def _():
        start = jnp.where(q == 0, 0, HALO + TALL)
        for layer in range(3):
            for frame in range(3):
                cells = edge_ref[layer, frame]
                for d in range(SPAN):
                    moved = pltpu.roll(cells, 128 - d, 1) if d else cells
                    seen_ref[layer, d, frame, pl.ds(start, HALO), :] = moved


def view_kernel(
    recv_ref, seen_ref, far_out, s0_ref, s1_ref, s2_ref, s3_ref, s4_ref, s5_ref,
    image_ref, shift_ref, shift_smem, sem,
):
    sums = (s0_ref, s1_ref, s2_ref, s3_ref, s4_ref, s5_ref)
    row = lax.broadcasted_iota(I32, (16, 128), 0)
    pick = jnp.where(lanes(16) == 120 + row, 1.0, 0.0).astype(BF16)
    moved = lax.dot_general(
        pick, recv_ref[:, 0, :], (((1,), (1,)), ((), ())), preferred_element_type=F32
    )
    shift_ref[...] = jnp.zeros((8, 128), I32)
    shift_ref[:, :64] = moved[:8].astype(I32)
    copy = pltpu.make_async_copy(shift_ref, shift_smem, sem)
    copy.start()

    lane = lanes(8)
    upper_half = lax.broadcasted_iota(I32, (8, 128), 0) < 4
    for view in range(64):
        cells = recv_ref[view].astype(F32)
        image_ref[view, :8] = cells
        low = pltpu.roll(cells, 128 - 80, 1)
        high = pltpu.roll(pltpu.roll(cells, 128 - 40, 1), 4, 0)
        rest = jnp.where(lane < 40, low, high)
        image_ref[view, 8:] = jnp.where(upper_half, rest, 0.0)

    for ref in sums:
        ref[...] = jnp.zeros_like(ref)

    block, half, q = my_tile()
    column = block * 128 + half * WIDE - HALO + lanes(16)
    inside = (column >= 0) & (column < 1024)
    inside = inside & (lax.broadcasted_iota(I32, (16, 128), 0) < TALL)
    third = jnp.where(inside, 1.0 / 3.0, 0.0)
    copy.wait()

    def one_view(view, carry):
        rows = [shift_smem[2 * layer, view] + HALO for layer in range(3)]
        cols = [shift_smem[2 * layer + 1, view] + HALO for layer in range(3)]
        s0, s1, s2 = (
            seen_ref[layer, cols[layer], :, pl.ds(rows[layer], 16), :] for layer in range(3)
        )
        p01 = s0 * s1
        whole = p01 * s2
        shown = (whole[0] + whole[1] + whole[2]) * third
        image = image_ref[view]
        for layer, others in enumerate((s1 * s2, s0 * s2, p01)):
            for which, factor in enumerate((image, shown)):
                sums[2 * layer + which][cols[layer], :, pl.ds(rows[layer], 16), :] += factor * others
        return carry

    lax.fori_loop(0, 64, one_view, 0, unroll=4)

    start = jnp.where(lax.rem(q, 2) == 0, 0, HALO + TALL)
    for layer in range(3):
        for frame in range(3):
            far_out[layer, frame] = folded(sums, layer, frame, start, HALO)


def folded(sums, layer, frame, start, rows):
    sides = []
    for which, base in enumerate((-16, 48)):
        total = None
        for d in range(SPAN):
            amount = (d + base) % 128
            cells = sums[2 * layer + which][d, frame, pl.ds(start, rows), :]
            moved = pltpu.roll(cells, amount, 1) if amount else cells
            total = moved if total is None else total + moved
        sides.append(total)
    return jnp.where(lanes(rows) < WIDE, sides[0], sides[1])


def fold_kernel(s0_ref, s1_ref, s2_ref, s3_ref, s4_ref, s5_ref, near_out, own_out):
    sums = (s0_ref, s1_ref, s2_ref, s3_ref, s4_ref, s5_ref)
    _, _, q = my_tile()
    start = jnp.where(lax.rem(q, 2) == 0, HALO + TALL, 0)
    for layer in range(3):
        for frame in range(3):
            near_out[layer, frame] = folded(sums, layer, frame, start, HALO)
            own_out[layer, frame] = folded(sums, layer, frame, HALO, 16)


def update_kernel(own_ref, far_ref, near_ref, tile_ref, out_ref, code_ref):
    lane = lanes(TALL)
    other = 1 - lax.axis_index("c")
    _, _, q = my_tile()
    even = lax.rem(q, 2) == 0
    for layer in range(3):
        for frame in range(3):
            own = own_ref[layer, frame]
            near = near_ref[other, layer, frame]
            far = far_ref[layer, frame]
            above = jnp.where(even, far, near)
            below = jnp.where(even, near, far)
            none = jnp.zeros((4, 128), F32)
            both = own[:TALL] + jnp.concatenate([above, none], axis=0)
            both = both + jnp.concatenate([none, below], axis=0)
            lower = pltpu.roll(both, WIDE, 1)
            value = tile_ref[layer, frame, :TALL] * (both + REGULAR) / (lower + REGULAR)
            scaled = (jnp.log2(value) + CODE_BASE) * CODE_STEPS + 0.5
            code_ref[frame * 3 + layer, :TALL] = jnp.clip(scaled, 0.0, 65535.0).astype(I32)
    for pair in range(2):
        parts = []
        for p in (pair, pair + 2):
            even = code_ref[2 * p, :TALL]
            odd = pltpu.roll(code_ref[2 * p + 1, :TALL], WIDE, 1)
            parts.append(jnp.where(lane < WIDE, even, odd))
        word = parts[0] + (parts[1] - 32768) * 65536
        for copy in range(8):
            out_ref[copy, TALL * pair : TALL * pair + TALL] = word
    code_ref[8, :6] = jnp.where(
        lanes(6) < WIDE, code_ref[8, :6], pltpu.roll(code_ref[8, 6:TALL], WIDE, 1)
    )
    word = code_ref[8, :8] + (code_ref[8, REST : REST + 8] - 32768) * 65536
    for copy in range(8):
        out_ref[copy, MAIN : MAIN + 8] = word


def dense_kernel(words_ref, out_ref):
    for zl in range(8):
        main = words_ref[zl, :MAIN]
        rest = words_ref[zl, MAIN : MAIN + REST]
        for copy in range(4):
            out_ref[copy, REST * zl : REST * zl + REST] = rest
            out_ref[copy, 8 * REST + MAIN * zl : 8 * REST + MAIN * zl + MAIN] = main


def decoded(code):
    return jnp.exp2(code.astype(F32) * (1.0 / CODE_STEPS) - CODE_BASE)


def spread_kernel(words_ref, out_ref, block_ref, sems):
    high, flip = place()

    def sent(d):
        columns = pl.ds(pl.multiple_of(d * 128, 128), 128)
        return pltpu.make_async_copy(block_ref.at[d, :, :, :48], out_ref.at[:, :, :, columns], sems.at[d])

    def one(d, carry):
        for q in range(4):
            rows = slice(TALL * q, TALL * q + TALL)

            places = [home(d, half, q, high, flip) for half in range(2)]

            def halves(first, count, step):
                a, b = (
                    words_ref[c, x, pl.ds(first + step * zl, count), :] for zl, x, c in places
                )
                lane = lanes(count)
                even = jnp.where(lane < WIDE, a, pltpu.roll(b, WIDE, 1))
                return even, jnp.where(lane < WIDE, pltpu.roll(a, WIDE, 1), b)

            for side, word in enumerate(halves(8 * REST, MAIN, MAIN)):
                for p, code in ((0, word & 65535), (2, (word >> 16) + 32768)):
                    value = decoded(code)
                    for pair in range(2):
                        at = 2 * (p + pair) + side
                        block_ref[d, at // 3, at % 3, rows] = value[TALL * pair : TALL * pair + TALL]
            for side, word in enumerate(halves(0, REST, REST)):
                for part, code in ((0, word & 65535), (1, (word >> 16) + 32768)):
                    at = TALL * q + 6 * side + REST * part
                    block_ref[d, 2, 2, at : at + REST] = decoded(code)
        sent(d).start()
        return carry

    lax.fori_loop(0, 8, one, 0)
    for d in range(8):
        sent(d).wait()


def strip_pairs(first, step):
    def index(column, strip):
        at = strip // 4
        zl, x, c = home(column // 2, column % 2, strip % 4, at // 4, at % 2)
        return (((zl * 4 + x) * 2 + c) * 2 + at // 4) * 4 + at % 4

    pairs = []
    for column in range(16):
        for strip in range(first, 31, step):
            a, b = index(column, strip), index(column, strip + 1)
            pairs += [(a, b), (b, a)]
    return pairs


VMEM = pl.BlockSpec(memory_space=pltpu.VMEM)


VIEW_SCRATCH = [
    pltpu.VMEM((64, 16, 128), F32),
    pltpu.VMEM((8, 128), I32),
    pltpu.SMEM((8, 128), I32),
    pltpu.SemaphoreType.DMA,
]


def call(kernel, outs, ins, scratch=(), params=PARAMS, cost=None):
    return pl.pallas_call(
        kernel,
        out_shape=tuple(jax.ShapeDtypeStruct(*out) for out in outs),
        in_specs=ins,
        out_specs=(VMEM,) * len(outs),
        scratch_shapes=scratch,
        compiler_params=params,
        cost_estimate=cost,
    )


def body(layers, target, shifts):
    across = VIEW + ROW
    chunks, edge = call(
        pack_kernel,
        [((64, 8, 128), BF16), ((3, 3, HALO, 128), F32)],
        [pl.BlockSpec(memory_space=pltpu.HBM)] * 3,
        [
            pltpu.VMEM((1, 48, 1024), BF16),
            pltpu.SMEM((1, 2, 3), I32),
            pltpu.VMEM((2, 3, 3, 16, 128), BF16),
            pltpu.VMEM((16, 56, 128), F32),
            pltpu.SemaphoreType.DMA,
            pltpu.SemaphoreType.DMA,
            pltpu.SemaphoreType.DMA((2,)),
        ],
        WHOLE,
    )(target, shifts.transpose(0, 2, 1), layers)
    received = lax.all_to_all(chunks, VIEW, 0, 0)

    edge = lax.ppermute(edge, across, strip_pairs(3, 4))
    seen, tile = call(
        seen_kernel,
        [((3, SPAN, 3, 32, 128), F32), ((3, 3, 16, 128), F32)],
        [VMEM],
        [pltpu.VMEM((3, 3, 72, 128), F32)],
        cost=pl.CostEstimate(flops=1_000_000, bytes_accessed=3_600_000, transcendentals=0),
    )(layers)
    (seen,) = call(edge_kernel, [((3, SPAN, 3, 32, 128), F32)], [VMEM] * 2)(seen, edge)

    far, *sums = call(
        view_kernel,
        [((3, 3, HALO, 128), F32)] + [((SPAN, 3, 32, 128), F32)] * 6,
        [VMEM] * 2,
        VIEW_SCRATCH,
    )(received, seen)
    far = lax.ppermute(far, across, strip_pairs(1, 2))
    near, own = call(
        fold_kernel,
        [((3, 3, HALO, 128), F32), ((3, 3, 16, 128), F32)],
        [VMEM] * 6,
        cost=pl.CostEstimate(flops=4_000_000, bytes_accessed=5_100_000, transcendentals=0),
    )(*sums)
    near = lax.all_gather(near, "c")

    (words,) = call(
        update_kernel,
        [((8, 32, 128), I32)],
        [VMEM] * 4,
        [pltpu.VMEM((9, 16, 128), I32)],
    )(own, far, near, tile)
    words = lax.all_to_all(words, "zl", 0, 0)
    (words,) = call(dense_kernel, [((4, 8 * (MAIN + REST), 128), I32)], [VMEM])(words)
    words = lax.all_to_all(words, "x", 0, 0)
    words = lax.all_gather(words, "c")

    return pl.pallas_call(
        spread_kernel,
        out_shape=jax.ShapeDtypeStruct((3, 3, 48, 1024), F32),
        in_specs=[VMEM],
        out_specs=pl.BlockSpec(memory_space=pl.ANY),
        scratch_shapes=[pltpu.VMEM((8, 3, 3, 56, 128), F32), pltpu.SemaphoreType.DMA((8,))],
        compiler_params=PARAMS,
    )(words)


def solution(mesh):
    fine = Mesh(mesh.devices.reshape(8, 4, 2, 2, 4), ("zl", "x", "c", "zh", "y"))
    placed = (P(None, None, ROW, None), P(VIEW, ROW, None), P(VIEW, None, None))
    return jax.shard_map(
        body, mesh=fine, in_specs=placed, out_specs=P(None, None, ROW, None), check_vma=False
    )
```

```python
import jax
import jax.numpy as jnp
from jax import lax
from jax.experimental import pallas as pl
from jax.experimental.pallas import tpu as pltpu
from jax.sharding import Mesh, PartitionSpec as P

HALO = 8
SPAN = 2 * HALO + 1
TALL = 12
WIDE = 64
REGULAR = 0.05
CODE_STEPS = 5041.0
CODE_BASE = 7.0
MAIN = 24
REST = 3
F32 = jnp.float32
BF16 = jnp.bfloat16
I32 = jnp.int32
VIEW = ("zl", "x", "c")
ROW = ("zh", "y")
PARAMS = pltpu.CompilerParams(vmem_limit_bytes=16 * 1024 * 1024)
WHOLE = pltpu.CompilerParams(vmem_limit_bytes=64 * 1024 * 1024)


def lanes(rows):
    return lax.broadcasted_iota(I32, (rows, 128), 1)


def home(block, half, q, high, odd):
    column = 2 * block + half
    at = column >> 2
    outer, inner = at + 4 * (at >> 1), at + 2
    zl = outer + ((q >> 1) ^ odd) * (inner - outer)
    return zl ^ (6 * high), column & 3, q & 1


def place():
    return lax.axis_index("zh"), lax.rem(lax.axis_index("y"), 2)


def my_tile():
    high, odd = place()
    zl = jnp.bitwise_xor(lax.axis_index("zl"), 6 * high)
    outer = (zl < 2) | (zl > 5)
    at = jnp.where(zl < 2, zl, jnp.where(zl > 5, zl - 4, zl - 2))
    column = 4 * at + lax.axis_index("x")
    q = 2 * jnp.where(outer, odd, 1 - odd) + lax.axis_index("c")
    return column >> 1, column & 1, q


def window(block, half):
    first = block - 1 + half
    left = pl.multiple_of(jnp.maximum(first, 0) * 128, 128)
    right = pl.multiple_of(jnp.minimum(first + 1, 7) * 128, 128)
    there = jnp.where(first >= 0, 1.0, 0.0), jnp.where(first < 7, 1.0, 0.0)
    return left, right, there, jnp.where(half == 0, 16, 80)


def joined(a, b, there, amount):
    lane = lanes(a.shape[0])
    a = a.astype(F32) * there[0]
    b = b.astype(F32) * there[1]
    return pltpu.roll(jnp.where(lane >= 128 - amount, a, b), amount, 1)


def pack_kernel(
    target_hbm, shifts_hbm, layers_hbm, chunks_ref, edge_out,
    target_ref, shifts_ref, near_edge, wide_ref, target_sem, shifts_sem, edge_sems,
):
    fetch_shifts = pltpu.make_async_copy(shifts_hbm, shifts_ref, shifts_sem)
    fetch_shifts.start()
    fetch = pltpu.make_async_copy(target_hbm, target_ref, target_sem)
    fetch.start()
    block, half, q = my_tile()
    last = q == 3
    left, right, there, amount = window(block, half)
    start = pl.multiple_of(jnp.where(last, 32, 0), 16)
    fetch_edges = [
        pltpu.make_async_copy(
            layers_hbm.at[:, :, pl.ds(start, 16), pl.ds(side, 128)], near_edge.at[i], edge_sems.at[i]
        )
        for i, side in enumerate((left, right))
    ]
    for one in fetch_edges:
        one.start()
    high, odd = place()
    fetch.wait()
    lane = lanes(48)
    blocks = [target_ref[0, :, 128 * d : 128 * d + 128].astype(F32) for d in range(8)]
    zero = jnp.zeros((48, 128), F32)
    for d in range(8):
        left = blocks[d - 1] if d > 0 else zero
        right = blocks[d + 1] if d < 7 else zero
        mid = blocks[d]
        wide_ref[2 * d, :48] = pltpu.roll(jnp.where(lane >= 128 - HALO, left, mid), HALO, 1)
        wide_ref[2 * d + 1, :48] = pltpu.roll(jnp.where(lane < HALO, right, mid), 128 - 56, 1)
    lane = lanes(8)
    upper_half = lax.broadcasted_iota(I32, (8, 128), 0) < 4
    fetch_shifts.wait()
    extra = jnp.zeros((8, 128), F32)
    for layer in range(3):
        for part in range(2):
            extra = jnp.where(
                lane == 120 + 2 * layer + part, shifts_ref[0, part, layer].astype(F32), extra
            )
    for q in range(4):
        for d in range(8):
            for h in range(2):
                zl, x, c = home(d, h, q, high, odd)
                at = 2 * d + h
                main = wide_ref[at, TALL * q : TALL * q + 8]
                first = wide_ref[at, TALL * q + 8 : TALL * q + 16]
                second = wide_ref[at, TALL * q + 4 : TALL * q + 12]
                pieces = jnp.where(upper_half, pltpu.roll(first, 80, 1), pltpu.roll(second, 40, 1))
                chunk = jnp.where(lane < 80, main, jnp.where(lane < 120, pieces, extra))
                chunks_ref[(zl * 4 + x) * 2 + c] = chunk.astype(BF16)
    for one in fetch_edges:
        one.wait()
    for layer in range(3):
        for frame in range(3):
            a, b = near_edge[0, frame, layer], near_edge[1, frame, layer]
            cells = joined(a, b, there, amount)
            edge_out[layer, frame] = jnp.where(last, cells[HALO:], cells[:HALO])


def seen_kernel(layers_ref, seen_ref, tile_ref, tall_ref):
    block, half, q = my_tile()
    left, right, there, amount = window(block, half)
    start = q * TALL
    for layer in range(3):
        for frame in range(3):
            a = layers_ref[frame, layer, :, pl.ds(left, 128)]
            b = layers_ref[frame, layer, :, pl.ds(right, 128)]
            tall_ref[layer, frame, :HALO] = jnp.zeros((HALO, 128), F32)
            tall_ref[layer, frame, HALO : HALO + 48] = joined(a, b, there, amount)
            tall_ref[layer, frame, HALO + 48 :] = jnp.zeros((16, 128), F32)
            cells = tall_ref[layer, frame, pl.ds(start, 32), :]
            for d in range(SPAN):
                moved = pltpu.roll(cells, 128 - d, 1) if d else cells
                seen_ref[layer, d, frame] = moved
                if d == 16:
                    tile_ref[layer, frame] = moved[HALO : HALO + 16]


def edge_kernel(seen_in, edge_ref, seen_ref):
    _, _, q = my_tile()
    seen_ref[...] = seen_in[...]

    @pl.when((q == 0) | (q == 3))
    def _():
        start = jnp.where(q == 0, 0, HALO + TALL)
        for layer in range(3):
            for frame in range(3):
                cells = edge_ref[layer, frame]
                for d in range(SPAN):
                    moved = pltpu.roll(cells, 128 - d, 1) if d else cells
                    seen_ref[layer, d, frame, pl.ds(start, HALO), :] = moved


def view_kernel(
    recv_ref, seen_ref, far_out, s0_ref, s1_ref, s2_ref, s3_ref, s4_ref, s5_ref,
    image_ref, shift_ref, shift_smem, sem,
):
    sums = (s0_ref, s1_ref, s2_ref, s3_ref, s4_ref, s5_ref)
    row = lax.broadcasted_iota(I32, (16, 128), 0)
    pick = jnp.where(lanes(16) == 120 + row, 1.0, 0.0).astype(BF16)
    moved = lax.dot_general(
        pick, recv_ref[:, 0, :], (((1,), (1,)), ((), ())), preferred_element_type=F32
    )
    shift_ref[...] = jnp.zeros((8, 128), I32)
    shift_ref[:, :64] = moved[:8].astype(I32)
    copy = pltpu.make_async_copy(shift_ref, shift_smem, sem)
    copy.start()

    lane = lanes(8)
    upper_half = lax.broadcasted_iota(I32, (8, 128), 0) < 4
    for view in range(64):
        cells = recv_ref[view].astype(F32)
        image_ref[view, :8] = cells
        low = pltpu.roll(cells, 128 - 80, 1)
        high = pltpu.roll(pltpu.roll(cells, 128 - 40, 1), 4, 0)
        rest = jnp.where(lane < 40, low, high)
        image_ref[view, 8:] = jnp.where(upper_half, rest, 0.0)

    for ref in sums:
        ref[...] = jnp.zeros_like(ref)

    block, half, q = my_tile()
    column = block * 128 + half * WIDE - HALO + lanes(16)
    inside = (column >= 0) & (column < 1024)
    inside = inside & (lax.broadcasted_iota(I32, (16, 128), 0) < TALL)
    third = jnp.where(inside, 1.0 / 3.0, 0.0)
    copy.wait()

    def one_view(view, carry):
        rows = [shift_smem[2 * layer, view] + HALO for layer in range(3)]
        cols = [shift_smem[2 * layer + 1, view] + HALO for layer in range(3)]
        s0, s1, s2 = (
            seen_ref[layer, cols[layer], :, pl.ds(rows[layer], 16), :] for layer in range(3)
        )
        p01 = s0 * s1
        whole = p01 * s2
        shown = (whole[0] + whole[1] + whole[2]) * third
        image = image_ref[view]
        for layer, others in enumerate((s1 * s2, s0 * s2, p01)):
            for which, factor in enumerate((image, shown)):
                sums[2 * layer + which][cols[layer], :, pl.ds(rows[layer], 16), :] += factor * others
        return carry

    lax.fori_loop(0, 64, one_view, 0, unroll=4)

    start = jnp.where(lax.rem(q, 2) == 0, 0, HALO + TALL)
    for layer in range(3):
        for frame in range(3):
            far_out[layer, frame] = folded(sums, layer, frame, start, HALO)


def folded(sums, layer, frame, start, rows):
    sides = []
    for which, base in enumerate((-16, 48)):
        total = None
        for d in range(SPAN):
            amount = (d + base) % 128
            cells = sums[2 * layer + which][d, frame, pl.ds(start, rows), :]
            moved = pltpu.roll(cells, amount, 1) if amount else cells
            total = moved if total is None else total + moved
        sides.append(total)
    return jnp.where(lanes(rows) < WIDE, sides[0], sides[1])


def fold_kernel(s0_ref, s1_ref, s2_ref, s3_ref, s4_ref, s5_ref, near_out, own_out):
    sums = (s0_ref, s1_ref, s2_ref, s3_ref, s4_ref, s5_ref)
    _, _, q = my_tile()
    start = jnp.where(lax.rem(q, 2) == 0, HALO + TALL, 0)
    for layer in range(3):
        for frame in range(3):
            near_out[layer, frame] = folded(sums, layer, frame, start, HALO)
            own_out[layer, frame] = folded(sums, layer, frame, HALO, 16)


def update_kernel(own_ref, far_ref, near_ref, tile_ref, out_ref, code_ref):
    lane = lanes(TALL)
    other = 1 - lax.axis_index("c")
    _, _, q = my_tile()
    even = lax.rem(q, 2) == 0
    for layer in range(3):
        for frame in range(3):
            own = own_ref[layer, frame]
            near = near_ref[other, layer, frame]
            far = far_ref[layer, frame]
            above = jnp.where(even, far, near)
            below = jnp.where(even, near, far)
            none = jnp.zeros((4, 128), F32)
            both = own[:TALL] + jnp.concatenate([above, none], axis=0)
            both = both + jnp.concatenate([none, below], axis=0)
            lower = pltpu.roll(both, WIDE, 1)
            value = tile_ref[layer, frame, :TALL] * (both + REGULAR) / (lower + REGULAR)
            scaled = (jnp.log2(value) + CODE_BASE) * CODE_STEPS + 0.5
            code_ref[frame * 3 + layer, :TALL] = jnp.clip(scaled, 0.0, 65535.0).astype(I32)
    for pair in range(2):
        parts = []
        for p in (pair, pair + 2):
            even = code_ref[2 * p, :TALL]
            odd = pltpu.roll(code_ref[2 * p + 1, :TALL], WIDE, 1)
            parts.append(jnp.where(lane < WIDE, even, odd))
        word = parts[0] + (parts[1] - 32768) * 65536
        for copy in range(8):
            out_ref[copy, TALL * pair : TALL * pair + TALL] = word
    code_ref[8, :6] = jnp.where(
        lanes(6) < WIDE, code_ref[8, :6], pltpu.roll(code_ref[8, 6:TALL], WIDE, 1)
    )
    word = code_ref[8, :8] + (code_ref[8, REST : REST + 8] - 32768) * 65536
    for copy in range(8):
        out_ref[copy, MAIN : MAIN + 8] = word


def dense_kernel(words_ref, out_ref):
    for zl in range(8):
        main = words_ref[zl, :MAIN]
        rest = words_ref[zl, MAIN : MAIN + REST]
        for copy in range(4):
            out_ref[copy, REST * zl : REST * zl + REST] = rest
            out_ref[copy, 8 * REST + MAIN * zl : 8 * REST + MAIN * zl + MAIN] = main


def decoded(code):
    return jnp.exp2(code.astype(F32) * (1.0 / CODE_STEPS) - CODE_BASE)


def spread_kernel(words_ref, out_ref, block_ref, sems):
    high, flip = place()

    def sent(d):
        columns = pl.ds(pl.multiple_of(d * 128, 128), 128)
        return pltpu.make_async_copy(block_ref.at[d, :, :, :48], out_ref.at[:, :, :, columns], sems.at[d])

    def one(d, carry):
        for q in range(4):
            rows = slice(TALL * q, TALL * q + TALL)

            places = [home(d, half, q, high, flip) for half in range(2)]

            def halves(first, count, step):
                a, b = (
                    words_ref[c, x, pl.ds(first + step * zl, count), :] for zl, x, c in places
                )
                lane = lanes(count)
                even = jnp.where(lane < WIDE, a, pltpu.roll(b, WIDE, 1))
                return even, jnp.where(lane < WIDE, pltpu.roll(a, WIDE, 1), b)

            for side, word in enumerate(halves(8 * REST, MAIN, MAIN)):
                for p, code in ((0, word & 65535), (2, (word >> 16) + 32768)):
                    value = decoded(code)
                    for pair in range(2):
                        at = 2 * (p + pair) + side
                        block_ref[d, at // 3, at % 3, rows] = value[TALL * pair : TALL * pair + TALL]
            for side, word in enumerate(halves(0, REST, REST)):
                for part, code in ((0, word & 65535), (1, (word >> 16) + 32768)):
                    at = TALL * q + 6 * side + REST * part
                    block_ref[d, 2, 2, at : at + REST] = decoded(code)
        sent(d).start()
        return carry

    lax.fori_loop(0, 8, one, 0, unroll=8)
    for d in range(8):
        sent(d).wait()


def strip_pairs(first, step):
    def index(column, strip):
        at = strip // 4
        zl, x, c = home(column // 2, column % 2, strip % 4, at // 4, at % 2)
        return (((zl * 4 + x) * 2 + c) * 2 + at // 4) * 4 + at % 4

    pairs = []
    for column in range(16):
        for strip in range(first, 31, step):
            a, b = index(column, strip), index(column, strip + 1)
            pairs += [(a, b), (b, a)]
    return pairs


VMEM = pl.BlockSpec(memory_space=pltpu.VMEM)


VIEW_SCRATCH = [
    pltpu.VMEM((64, 16, 128), F32),
    pltpu.VMEM((8, 128), I32),
    pltpu.SMEM((8, 128), I32),
    pltpu.SemaphoreType.DMA,
]


def call(kernel, outs, ins, scratch=(), params=PARAMS, cost=None):
    return pl.pallas_call(
        kernel,
        out_shape=tuple(jax.ShapeDtypeStruct(*out) for out in outs),
        in_specs=ins,
        out_specs=(VMEM,) * len(outs),
        scratch_shapes=scratch,
        compiler_params=params,
        cost_estimate=cost,
    )


def body(layers, target, shifts):
    across = VIEW + ROW
    chunks, edge = call(
        pack_kernel,
        [((64, 8, 128), BF16), ((3, 3, HALO, 128), F32)],
        [pl.BlockSpec(memory_space=pltpu.HBM)] * 3,
        [
            pltpu.VMEM((1, 48, 1024), BF16),
            pltpu.SMEM((1, 2, 3), I32),
            pltpu.VMEM((2, 3, 3, 16, 128), BF16),
            pltpu.VMEM((16, 56, 128), F32),
            pltpu.SemaphoreType.DMA,
            pltpu.SemaphoreType.DMA,
            pltpu.SemaphoreType.DMA((2,)),
        ],
        WHOLE,
    )(target, shifts.transpose(0, 2, 1), layers)
    received = lax.all_to_all(chunks, VIEW, 0, 0)

    edge = lax.ppermute(edge, across, strip_pairs(3, 4))
    seen, tile = call(
        seen_kernel,
        [((3, SPAN, 3, 32, 128), F32), ((3, 3, 16, 128), F32)],
        [VMEM],
        [pltpu.VMEM((3, 3, 72, 128), F32)],
        cost=pl.CostEstimate(flops=1_000_000, bytes_accessed=3_600_000, transcendentals=0),
    )(layers)
    (seen,) = call(edge_kernel, [((3, SPAN, 3, 32, 128), F32)], [VMEM] * 2)(seen, edge)

    far, *sums = call(
        view_kernel,
        [((3, 3, HALO, 128), F32)] + [((SPAN, 3, 32, 128), F32)] * 6,
        [VMEM] * 2,
        VIEW_SCRATCH,
    )(received, seen)
    far = lax.ppermute(far, across, strip_pairs(1, 2))
    near, own = call(
        fold_kernel,
        [((3, 3, HALO, 128), F32), ((3, 3, 16, 128), F32)],
        [VMEM] * 6,
        cost=pl.CostEstimate(flops=4_000_000, bytes_accessed=5_100_000, transcendentals=0),
    )(*sums)
    near = lax.all_gather(near, "c")

    (words,) = call(
        update_kernel,
        [((8, 32, 128), I32)],
        [VMEM] * 4,
        [pltpu.VMEM((9, 16, 128), I32)],
    )(own, far, near, tile)
    words = lax.all_to_all(words, "zl", 0, 0)
    (words,) = call(dense_kernel, [((4, 8 * (MAIN + REST), 128), I32)], [VMEM])(words)
    words = lax.all_to_all(words, "x", 0, 0)
    words = lax.all_gather(words, "c")

    return pl.pallas_call(
        spread_kernel,
        out_shape=jax.ShapeDtypeStruct((3, 3, 48, 1024), F32),
        in_specs=[VMEM],
        out_specs=pl.BlockSpec(memory_space=pl.ANY),
        scratch_shapes=[pltpu.VMEM((8, 3, 3, 56, 128), F32), pltpu.SemaphoreType.DMA((8,))],
        compiler_params=PARAMS,
    )(words)


def solution(mesh):
    fine = Mesh(mesh.devices.reshape(8, 4, 2, 2, 4), ("zl", "x", "c", "zh", "y"))
    placed = (P(None, None, ROW, None), P(VIEW, ROW, None), P(VIEW, None, None))
    return jax.shard_map(
        body, mesh=fine, in_specs=placed, out_specs=P(None, None, ROW, None), check_vma=False
    )
```
